32 devices in a mesh: mode: 8 (over y, x, core), wall: 2 (over z_hi), ckpt: 2 (over z_lo).
Axes of the slice: x: 2, y: 2, z: 4 (z_hi: 2, z_lo: 2; z = z_hi * 2 + z_lo), core: 2. Of those that a mesh axis runs over, the one named last changes fastest.
Arguments:
- adjoint: float32 [2, 5, 1024, 4096], P(None, None, ('wall', 'ckpt'), 'mode'), may hold values from -6 to 6
- forward: float32 [2, 2, 1024, 4096], P('ckpt', None, 'wall', 'mode'), may hold values from -0.09375 to 0.09375
- mode_map: int32 [4096], P('mode'), may hold values from 0 to 4095, as said below
Outputs:
- adjoint_prev: float32 [2, 5, 1024, 4096], P(None, None, ('wall', 'ckpt'), 'mode')
The draws below stay inside these ranges and needn't reach their ends.
Inputs may be any that keep to these rules, and one draw needn't show every extreme that they name: mode_map is a permutation of the 64 x 64 modes laid out by frequency: for every block b of 64 consecutive slots there is a frequency p(b) such that slot b * 64 + r holds mode p(b) * 64 + r, and p takes every frequency once.
All inputs are finite; a program needn't handle non-finite values.
Results may differ from the reference program's by a relative error of at most 0.0001.
Values sent between devices are 32-bit elements; how exact they have to be, the bound alone decides.
No kernel may reach another device: no remote copies, remote signals or barrier semaphores. Data moves between devices by JAX's collectives and lax.ppermute only.
A program may use at most 128 MiB of HBM per device.

```python
import math
import jax
import jax.numpy as jnp
from jax import lax

NF = 64
NK = 64
FIELDS = 5
MODES = 4096
NY = 1024
STATIONS = 2


def draw_mode_map(key, part):
    freq_order = jax.random.permutation(jax.random.fold_in(key, 11), NF).astype(jnp.int32)
    span_ids = jnp.arange(NK, dtype=jnp.int32)
    return (freq_order[:, None] * NK + span_ids[None, :]).reshape(MODES).astype(jnp.int32)


def block_levels(own_key, shape, shards, smallest, largest):
    def one(position, blocks):
        steps = jax.random.uniform(jax.random.fold_in(jax.random.fold_in(own_key, 6), position), (blocks,), jnp.float32, smallest / len(shards), largest / len(shards))
        return jnp.repeat(jnp.exp(steps), shape[position] // blocks).reshape((-1,) + (1,) * (len(shape) - position - 1))

    loudness = one(*shards[0])
    for cut in shards[1:]:
        loudness = loudness * one(*cut)
    return loudness


def centred(rng, dims, width, reach, cuts=(), held_as=jnp.bfloat16):
    level = block_levels(rng, dims, cuts, -0.22, 0.18) if cuts else 1.0
    values = jax.random.normal(rng, dims, jnp.float32) * width * level
    return jnp.minimum(jnp.maximum(values, -reach), reach).astype(held_as)


def setup_inputs(seed: int = 0) -> dict:
    splits = jax.random.split(jax.random.key(seed), 4)
    return {
        "adjoint": centred(splits[0], (2, FIELDS, NY, MODES), 1.0, 6.0, ((2, 4), (3, 8)), jnp.float32),
        "forward": centred(splits[1], (STATIONS, 2, NY, MODES), MODES ** -0.5, 0.09375, ((0, 2), (2, 2), (3, 8)), jnp.float32),
        "mode_map": draw_mode_map(jax.random.fold_in(splits[3], 71), 0),
    }


def rates(grid_index):
    freq_index = grid_index // NK
    span_index = grid_index % NK
    freq_signed = (freq_index + NF // 2) % NF - NF // 2
    span_signed = (span_index + NK // 2) % NK - NK // 2
    return (2.0 / NF * freq_signed.astype(jnp.float32), 2.0 / NK * span_signed.astype(jnp.float32))

def reference(adjoint, forward, mode_map):
    slot_index = mode_map.astype(jnp.int32)
    placed = jnp.zeros((MODES,), jnp.int32).at[slot_index].set(jnp.arange(MODES, dtype=jnp.int32))
    alpha_rate, beta_rate = rates(slot_index)

    def to_phys(real_part, imag_part):
        joined = lax.complex(real_part, imag_part)[..., placed]
        joined = joined.reshape(joined.shape[:-1] + (NF, NK))
        return jnp.fft.ifft2(joined) * (NF * NK)

    def to_modes(product):
        spectrum = jnp.fft.fft2(product) / (NF * NK)
        spectrum = spectrum.reshape(spectrum.shape[:-2] + (MODES,))[..., slot_index]
        return (jnp.real(spectrum), jnp.imag(spectrum))
    row_scale = 1.0 / math.sqrt(NY)
    current = adjoint
    for station in range(STATIONS - 1, -1, -1):
        forward_phys = to_phys(forward[station, 0], forward[station, 1])
        adjoint_phys = to_phys(current[0], current[1])
        product = jnp.conj(forward_phys)[None] * adjoint_phys
        coupled_real, coupled_imag = to_modes(product)
        coupled = jnp.stack([coupled_real, coupled_imag])
        zero_row = jnp.zeros_like(current[:, :, :1])
        above_rows = jnp.concatenate([current[:, :, 1:], zero_row], 2)
        below_rows = jnp.concatenate([zero_row, current[:, :, :-1]], 2)
        stepped = current + 0.2 * (above_rows - 2.0 * current + below_rows) - 0.5 * coupled
        running_real = jnp.cumsum(alpha_rate * stepped[0, 0] + beta_rate * stepped[0, 2], axis=0)
        running_imag = jnp.cumsum(alpha_rate * stepped[1, 0] + beta_rate * stepped[1, 2], axis=0)
        stepped = stepped.at[0, 1].add(running_imag * row_scale)
        stepped = stepped.at[1, 1].add(-running_real * row_scale)
        current = stepped
    return current
```

```python
import functools
import math

import jax
import jax.numpy as jnp
import numpy as np
from jax import lax
from jax.experimental import pallas as pl
from jax.experimental.pallas import tpu as pltpu
from jax.sharding import PartitionSpec as P

NF = 64
NK = 64
LANES = 2 * NK
KAPPA = 0.2
COUPLING = 0.5
HIGHEST = lax.Precision.HIGHEST
ROW_BLOCKS = ("wall", "ckpt")
ALL_AXES = ("mode", "wall", "ckpt")
VMEM = pltpu.CompilerParams(vmem_limit_bytes=56 * 1024 * 1024)
F32 = jnp.float32


def complex_lanes(matrix):
    twice = np.kron(np.eye(2), matrix)
    return np.block([[twice.real, twice.imag], [-twice.imag, twice.real]]).astype(np.float32)


def span_matrix(direction):
    ids = np.arange(NK)
    return np.exp(2j * math.pi * direction * (np.outer(ids, ids) % NK) / NK)


def beta_matrix():
    ids = np.arange(NK)
    signed = (ids + NK // 2) % NK - NK // 2
    return span_matrix(-1) @ np.diag(2.0 / NK * signed) @ span_matrix(1) / NK


def low_half(shape):
    return lax.broadcasted_iota(jnp.int32, shape, len(shape) - 1) < NK


def swap(value):
    return pltpu.roll(value, NK, value.ndim - 1)


def dft4(x, sign):
    (ar, ai), (br, bi), (cr, ci), (dr, di) = x
    pr, pi, mr, mi = ar + cr, ai + ci, ar - cr, ai - ci
    qr, qi, nr, ni = br + dr, bi + di, br - dr, bi - di
    if sign > 0:
        nr, ni = -ni, nr
    else:
        nr, ni = ni, -nr
    return [(pr + qr, pi + qi), (mr + nr, mi + ni), (pr - qr, pi - qi), (mr - nr, mi - ni)]


def dft8(x, sign):
    even = dft4(x[0::2], sign)
    odd = dft4(x[1::2], sign)
    half = math.sqrt(0.5)
    (r1, i1), (r2, i2), (r3, i3) = odd[1], odd[2], odd[3]
    if sign > 0:
        odd[1] = (half * (r1 - i1), half * (i1 + r1))
        odd[2] = (-i2, r2)
        odd[3] = (-half * (r3 + i3), half * (r3 - i3))
    else:
        odd[1] = (half * (r1 + i1), half * (i1 - r1))
        odd[2] = (i2, -r2)
        odd[3] = (half * (i3 - r3), -half * (i3 + r3))
    first = [(a + c, b + d) for (a, b), (c, d) in zip(even, odd)]
    second = [(a - c, b - d) for (a, b), (c, d) in zip(even, odd)]
    return first + second


def turned(pair, power, sign):
    power %= NF
    if power == 0:
        return pair
    angle = 2.0 * math.pi * power / NF
    c, s = math.cos(angle), sign * math.sin(angle)
    re, im = pair
    return (c * re - s * im, c * im + s * re)


class Sizes:
    def __init__(self, rows, slots):
        self.group = lax.axis_size("mode")
        self.block_rows = rows
        self.slots = slots
        self.lane_groups = slots // LANES
        self.blocks = slots // NK
        self.rows = rows // self.group
        self.half = self.rows // 2
        self.tile = min(8, self.half)
        self.tiles = self.half // self.tile
        self.padded = (self.half + 7) // 8 * 8 + 16
        self.body = 2 * self.blocks * self.half
        self.rims = 2 * self.blocks


def cut_pieces(sz, with_rims, me, planes, out_at, k):
    row = pl.multiple_of((me ^ k) * sz.rows, sz.rows)
    for g in range(sz.lane_groups):
        whole = planes[g, pl.ds(row, sz.rows), :]
        for c in range(2):
            part = whole[:, c * LANES : (c + 1) * LANES]
            top, bottom = part[: sz.half], part[sz.half :]
            low = low_half(top.shape)
            for odd, value in (
                (0, jnp.where(low, top, swap(bottom))),
                (1, jnp.where(low, swap(top), bottom)),
            ):
                place = (c * sz.blocks + 2 * g + odd) * sz.half
                out_at(place, sz.half, value)
    if not with_rims:
        return
    dest = me ^ k
    before = jnp.where(dest == 0, sz.block_rows, dest * sz.rows - 1)
    after = jnp.where(dest == sz.group - 1, sz.block_rows + 1, (dest + 1) * sz.rows)
    for g in range(sz.lane_groups):
        down = planes[g, pl.ds(before, 1), :]
        up = planes[g, pl.ds(after, 1), :]
        for c in range(2):
            top = down[:, c * LANES : (c + 1) * LANES]
            bottom = up[:, c * LANES : (c + 1) * LANES]
            low = low_half(top.shape)
            place = sz.body + c * sz.blocks + 2 * g
            out_at(place, 1, jnp.where(low, top, swap(bottom)))
            out_at(place + 1, 1, jnp.where(low, swap(top), bottom))


def adjoint_prep_kernel(sz, me_ref, x_ref, rim_ref, w_ref, *rest):
    outs, planes = rest[: sz.group], rest[sz.group]
    w = w_ref[...]
    for g in range(sz.lane_groups):
        at = pl.ds(g * LANES, LANES)
        x = jnp.concatenate([x_ref[0, 0, :, at], x_ref[1, 0, :, at]], axis=1)
        planes[g, : sz.block_rows, :] = jnp.dot(x, w, precision=HIGHEST, preferred_element_type=F32)
        rim = jnp.concatenate([rim_ref[0, 0, :, at], rim_ref[1, 0, :, at]], axis=1)
        planes[g, sz.block_rows :, :] = jnp.dot(rim, w, precision=HIGHEST, preferred_element_type=F32)
    me = me_ref[0]
    for k in range(sz.group):

        def out_at(place, count, value, out=outs[k]):
            out[0, place : place + count, :] = value

        cut_pieces(sz, True, me, planes, out_at, k)


def adjoint_prep(sz, me, adjoint, rims, fields):
    count = len(fields)
    stride = fields[1] - fields[0] if count > 1 else 1
    first = fields[0]
    length = sz.body + sz.rims
    return pl.pallas_call(
        functools.partial(adjoint_prep_kernel, sz),
        grid_spec=pltpu.PrefetchScalarGridSpec(
            num_scalar_prefetch=1,
            grid=(count,),
            in_specs=[
                pl.BlockSpec(
                    (2, 1, sz.block_rows, sz.slots), lambda i, me: (0, first + stride * i, 0, 0)
                ),
                pl.BlockSpec((2, 1, 8, sz.slots), lambda i, me: (0, first + stride * i, 0, 0)),
                pl.BlockSpec((2 * LANES, 2 * LANES), lambda i, me: (0, 0)),
            ],
            out_specs=[pl.BlockSpec((1, length, LANES), lambda i, me: (i, 0, 0))] * sz.group,
            scratch_shapes=[pltpu.VMEM((sz.lane_groups, sz.block_rows + 8, 2 * LANES), F32)],
        ),
        out_shape=[jax.ShapeDtypeStruct((count, length, LANES), F32)] * sz.group,
        compiler_params=VMEM,
        name="adjoint_prep",
    )(me, adjoint, rims, jnp.asarray(complex_lanes(span_matrix(1))))


def forward_prep_kernel(sz, me_ref, x_ref, w_ref, *rest):
    outs, planes = rest[: sz.group], rest[sz.group]
    w = w_ref[...]
    for g in range(sz.lane_groups):
        at = pl.ds(g * LANES, LANES)
        x = jnp.concatenate([x_ref[0, 0, :, at], x_ref[0, 1, :, at]], axis=1)
        planes[g, :, :] = jnp.dot(x, w, precision=HIGHEST, preferred_element_type=F32)
    me = me_ref[0]
    for k in range(sz.group):

        def out_at(place, count, value, out=outs[k]):
            out[0, place : place + count, :] = value

        cut_pieces(sz, False, me, planes, out_at, k)


def forward_prep(sz, me, both):
    stations = both.shape[0]
    return pl.pallas_call(
        functools.partial(forward_prep_kernel, sz),
        grid_spec=pltpu.PrefetchScalarGridSpec(
            num_scalar_prefetch=1,
            grid=(stations,),
            in_specs=[
                pl.BlockSpec((1, 2, sz.block_rows, sz.slots), lambda i, me: (i, 0, 0, 0)),
                pl.BlockSpec((2 * LANES, 2 * LANES), lambda i, me: (0, 0)),
            ],
            out_specs=[pl.BlockSpec((1, sz.body, LANES), lambda i, me: (i, 0, 0))] * sz.group,
            scratch_shapes=[pltpu.VMEM((sz.lane_groups, sz.block_rows, 2 * LANES), F32)],
        ),
        out_shape=[jax.ShapeDtypeStruct((stations, sz.body, LANES), F32)] * sz.group,
        compiler_params=VMEM,
        name="forward_prep",
    )(me, both, jnp.asarray(complex_lanes(span_matrix(1))))


def gather_pieces(sz, table_ref, pieces, state, lead, rims=None):
    for k, piece in enumerate(pieces):
        for j in range(sz.blocks):
            freq = table_ref[k * sz.blocks + j]
            for c in range(2):
                at = (c * sz.blocks + j) * sz.half
                state[c, freq, lead : lead + sz.half, :] = piece[0, at : at + sz.half, :]
                if rims is not None:
                    rim = sz.body + c * sz.blocks + j
                    rims[c, pl.ds(freq, 1), :] = piece[0, rim : rim + 1, :]


def lead_first(sz, state, lead, work, s):
    rows = pl.ds(lead + s * sz.tile, sz.tile)
    out_rows = pl.ds(s * sz.tile, sz.tile)
    for a in range(8):
        x = [(state[0, a + 8 * b, rows, :], state[1, a + 8 * b, rows, :]) for b in range(8)]
        for t, pair in enumerate(dft8(x, 1)):
            re, im = turned(pair, a * t, 1)
            work[0, 8 * t + a, out_rows, :] = re
            work[1, 8 * t + a, out_rows, :] = im


def lead_second(sz, work, t, s):
    rows = pl.ds(s * sz.tile, sz.tile)
    x = [(work[0, 8 * t + a, rows, :], work[1, 8 * t + a, rows, :]) for a in range(8)]
    return dft8(x, 1)


def forward_kernel(sz, table_ref, *rest):
    pieces, out, state, work = rest[: sz.group], rest[sz.group], rest[-2], rest[-1]
    gather_pieces(sz, table_ref, pieces, state, 0)

    @pl.loop(0, sz.tiles)
    def _(s):
        rows = pl.ds(s * sz.tile, sz.tile)
        lead_first(sz, state, 0, work, s)
        for t in range(8):
            for u, (re, im) in enumerate(lead_second(sz, work, t, s)):
                out[0, 0, 8 * t + u, rows, :] = re
                out[0, 1, 8 * t + u, rows, :] = im


def forward_physical(sz, table, pieces):
    stations = pieces[0].shape[0]
    full = (2, NF, sz.half, LANES)
    return pl.pallas_call(
        functools.partial(forward_kernel, sz),
        grid_spec=pltpu.PrefetchScalarGridSpec(
            num_scalar_prefetch=1,
            grid=(stations,),
            in_specs=[pl.BlockSpec((1, sz.body, LANES), lambda i, t: (i, 0, 0))] * sz.group,
            out_specs=pl.BlockSpec((1,) + full, lambda i, t: (i, 0, 0, 0, 0)),
            scratch_shapes=[pltpu.VMEM(full, F32), pltpu.VMEM(full, F32)],
        ),
        out_shape=jax.ShapeDtypeStruct((stations,) + full, F32),
        compiler_params=VMEM,
        name="forward_physical",
    )(table, *pieces)


def place_edges(sz, state, rims):
    padded = sz.padded
    rows = state.reshape(2 * NF * padded, LANES)
    first = rows[pl.ds(8, 2 * NF, stride=padded), :]
    last = rows[pl.ds(8 + sz.half - 1, 2 * NF, stride=padded), :]
    low = low_half(first.shape)
    rows[pl.ds(7, 2 * NF, stride=padded), :] = jnp.where(low, rims, swap(last))
    rows[pl.ds(8 + sz.half, 2 * NF, stride=padded), :] = jnp.where(low, swap(first), rims)


def advance(sz, state, work, phys, store, s):
    rows = pl.ds(s * sz.tile, sz.tile)
    lead_first(sz, state, 8, work, s)
    for t in range(8):
        here = lead_second(sz, work, t, s)
        product = []
        for u, (re, im) in enumerate(here):
            wr, wi = phys[0, 0, 8 * t + u, rows, :], phys[0, 1, 8 * t + u, rows, :]
            product.append((wr * re + wi * im, wr * im - wi * re))
        for a, pair in enumerate(dft8(product, -1)):
            re, im = turned(pair, a * t, -1)
            work[0, 8 * t + a, rows, :] = re
            work[1, 8 * t + a, rows, :] = im
    for a in range(8):
        x = [(work[0, 8 * t + a, rows, :], work[1, 8 * t + a, rows, :]) for t in range(8)]
        for b, pair in enumerate(dft8(x, -1)):
            f = a + 8 * b
            for c in range(2):
                mid = state[c, f, pl.ds(8 + s * sz.tile, sz.tile), :]
                up = state[c, f, pl.ds(9 + s * sz.tile, sz.tile), :]
                down = state[c, f, pl.ds(7 + s * sz.tile, sz.tile), :]
                stepped = (1.0 - 2.0 * KAPPA) * mid + KAPPA * (up + down)
                store(c, f, s, stepped - (COUPLING / NF) * pair[c])


def ends_of(sz, stepped, first_ref, last_ref):
    if sz.half % 8:
        first = stepped[:, :, 0, :].reshape(2 * NF, LANES)
        last = stepped[:, :, sz.half - 1, :].reshape(2 * NF, LANES)
    else:
        rows = stepped.reshape(2 * NF * sz.half, LANES)
        first = rows[pl.ds(0, 2 * NF, stride=sz.half), :]
        last = rows[pl.ds(sz.half - 1, 2 * NF, stride=sz.half), :]
    low = low_half((NF, LANES))
    first_ref[0] = jnp.where(low, first[:NF], swap(first[NF:]))
    last_ref[0] = jnp.where(low, swap(last[:NF]), last[NF:])


def station_one_kernel(sz, table_ref, *rest):
    pieces = rest[: sz.group]
    phys, out, first_ref, last_ref, total_ref, state, work, rims = rest[sz.group :]
    gather_pieces(sz, table_ref, pieces, state, 8, rims)
    place_edges(sz, state, rims.reshape(2 * NF, LANES)[...])

    @pl.loop(0, sz.tiles)
    def _(s):
        def store(c, f, s, value):
            out[0, c, f, pl.ds(s * sz.tile, sz.tile), :] = value

        advance(sz, state, work, phys, store, s)

    ends_of(sz, out.at[0], first_ref, last_ref)
    sums = jnp.sum(out[0], axis=2)
    sums = sums + swap(sums)
    total_ref[0] = jnp.where(low_half((NF, LANES)), sums[0], sums[1])


def station_one(sz, table, pieces, phys, station):
    count = pieces[0].shape[0]
    full = (2, NF, sz.half, LANES)
    flat = pl.BlockSpec((1, NF, LANES), lambda i, t: (i, 0, 0))
    flat_shape = jax.ShapeDtypeStruct((count, NF, LANES), F32)
    return pl.pallas_call(
        functools.partial(station_one_kernel, sz),
        grid_spec=pltpu.PrefetchScalarGridSpec(
            num_scalar_prefetch=1,
            grid=(count,),
            in_specs=[pl.BlockSpec((1, sz.body + sz.rims, LANES), lambda i, t: (i, 0, 0))] * sz.group
            + [pl.BlockSpec((1,) + full, lambda i, t: (station, 0, 0, 0, 0))],
            out_specs=[pl.BlockSpec((1,) + full, lambda i, t: (i, 0, 0, 0, 0)), flat, flat, flat],
            scratch_shapes=[
                pltpu.VMEM((2, NF, sz.padded, LANES), F32),
                pltpu.VMEM(full, F32),
                pltpu.VMEM((2, NF, LANES), F32),
            ],
        ),
        out_shape=[jax.ShapeDtypeStruct((count,) + full, F32), flat_shape, flat_shape, flat_shape],
        compiler_params=VMEM,
        name="station_one",
    )(table, *pieces, phys)


def running_rows(sz, value, start):
    row = lax.broadcasted_iota(jnp.int32, value.shape, 0)
    reach = 1
    while reach < sz.half:
        value = value + jnp.where(row >= reach, pltpu.roll(value, reach, 0), 0.0)
        reach *= 2
    bottom = jnp.where(low_half((1, LANES)), 0.0, swap(value[sz.half - 1 :]))
    return value + (bottom + start)


def add_running_kernel(sz, row_scale, stepped, zero, two, alpha_ref, start, w_ref, out, first, last):
    both = jnp.concatenate([two[0, 0], two[0, 1]], axis=2).reshape(NF * sz.half, 2 * LANES)
    turned_two = jnp.dot(both, w_ref[...], precision=HIGHEST, preferred_element_type=F32)
    for f in range(NF):
        at = f * sz.half
        alpha = 2.0 / NF * ((f + NF // 2) % NF - NF // 2)
        spread = start[pl.ds(f, 1), :]
        low = low_half((1, LANES))
        starts = (jnp.where(low, spread, swap(spread)), jnp.where(low, swap(spread), spread))
        run = []
        for c in range(2):
            source = turned_two[at : at + sz.half, c * LANES : (c + 1) * LANES]
            source = source + alpha * zero[0, c, f]
            run.append(running_rows(sz, source, starts[c]))
        out[0, 0, f] = stepped[0, 0, f] + row_scale * run[1]
        out[0, 1, f] = stepped[0, 1, f] - row_scale * run[0]
    ends_of(sz, out.at[0], first, last)


def add_running(sz, row_scale, stepped, pair, start):
    full = (1, 2, NF, sz.half, LANES)
    flat = pl.BlockSpec((1, NF, LANES), lambda i: (0, 0, 0))
    flat_shape = jax.ShapeDtypeStruct((1, NF, LANES), F32)
    return pl.pallas_call(
        functools.partial(add_running_kernel, sz, row_scale),
        grid=(1,),
        in_specs=[
            pl.BlockSpec(full, lambda i: (0, 0, 0, 0, 0)),
            pl.BlockSpec(full, lambda i: (0, 0, 0, 0, 0)),
            pl.BlockSpec(full, lambda i: (1, 0, 0, 0, 0)),
            pl.BlockSpec((8, LANES), lambda i: (0, 0)),
            pl.BlockSpec((NF, LANES), lambda i: (0, 0)),
            pl.BlockSpec((2 * LANES, 2 * LANES), lambda i: (0, 0)),
        ],
        out_specs=[pl.BlockSpec(full, lambda i: (0, 0, 0, 0, 0)), flat, flat],
        out_shape=[jax.ShapeDtypeStruct(full, F32), flat_shape, flat_shape],
        compiler_params=VMEM,
        name="add_running",
    )(
        stepped,
        pair,
        pair,
        jnp.zeros((8, LANES), F32),
        start,
        jnp.asarray(complex_lanes(beta_matrix())),
    )


def station_zero_kernel(sz, table_ref, current, before, after, phys, *rest):
    outs, (state, work, stepped) = rest[: sz.group], rest[sz.group :]
    state[:, :, 8 : 8 + sz.half, :] = current[0]
    low = low_half((NF, LANES))
    rims = jnp.concatenate(
        [jnp.where(low, before[0], swap(after[0])), jnp.where(low, swap(before[0]), after[0])], 0
    )
    place_edges(sz, state, rims)

    @pl.loop(0, sz.tiles)
    def _(s):
        def store(c, f, s, value):
            stepped[c, f, pl.ds(s * sz.tile, sz.tile), :] = value

        advance(sz, state, work, phys, store, s)

    for k in range(sz.group):
        for j in range(sz.blocks):
            freq = table_ref[k * sz.blocks + j]
            for c in range(2):
                at = (c * sz.blocks + j) * sz.half
                outs[k][0, at : at + sz.half, :] = stepped[c, freq]


def station_zero(sz, table, current, before, after, phys, station):
    count = current.shape[0]
    full = (2, NF, sz.half, LANES)
    flat = pl.BlockSpec((1, NF, LANES), lambda i, t: (i, 0, 0))
    return pl.pallas_call(
        functools.partial(station_zero_kernel, sz),
        grid_spec=pltpu.PrefetchScalarGridSpec(
            num_scalar_prefetch=1,
            grid=(count,),
            in_specs=[
                pl.BlockSpec((1,) + full, lambda i, t: (i, 0, 0, 0, 0)),
                flat,
                flat,
                pl.BlockSpec((1,) + full, lambda i, t: (station, 0, 0, 0, 0)),
            ],
            out_specs=[pl.BlockSpec((1, sz.body, LANES), lambda i, t: (i, 0, 0))] * sz.group,
            scratch_shapes=[
                pltpu.VMEM((2, NF, sz.padded, LANES), F32),
                pltpu.VMEM(full, F32),
                pltpu.VMEM(full, F32),
            ],
        ),
        out_shape=[jax.ShapeDtypeStruct((count, sz.body, LANES), F32)] * sz.group,
        compiler_params=VMEM,
        name="station_zero",
    )(table, current, before, after, phys)


def join_pieces(sz, me, pieces, planes):
    for k, piece in enumerate(pieces):
        row = pl.multiple_of((me ^ k) * sz.rows, sz.rows)
        for g in range(sz.lane_groups):
            halves = []
            for c in range(2):
                at = (c * sz.blocks + 2 * g) * sz.half
                even = piece[0, at : at + sz.half, :]
                odd = piece[0, at + sz.half : at + 2 * sz.half, :]
                low = low_half(even.shape)
                top = jnp.where(low, even, swap(odd))
                bottom = jnp.where(low, swap(even), odd)
                halves.append(jnp.concatenate([top, bottom], axis=0))
            planes[g, pl.ds(row, sz.rows), :] = jnp.concatenate(halves, axis=1)


def post_kernel(sz, running, row_scale, me_ref, *rest):
    pieces, rest = rest[: sz.group], rest[sz.group :]
    w_ref, rest = rest[0], rest[1:]
    if running == "add":
        sums_ref, start_ref, rest = rest[0], rest[1], rest[2:]
    elif running == "make":
        alpha_ref, beta_ref, tri_ref, rest = rest[0], rest[1], rest[2], rest[3:]
    planes = rest[-1]
    outs = rest[:-1]
    if running != "make":
        outs = outs[1:]
    out = outs[0]
    join_pieces(sz, me_ref[0], pieces, planes)
    w = w_ref[...]
    for g in range(sz.lane_groups):
        at = pl.ds(g * LANES, LANES)
        back = jnp.dot(planes[g], w, precision=HIGHEST, preferred_element_type=F32)
        halves = [back[:, :LANES], back[:, LANES:]]
        if running == "add":
            sums = [sums_ref[c, :, at] + start_ref[pl.ds(c, 1), at] for c in range(2)]
            halves = [halves[0] + row_scale * sums[1], halves[1] - row_scale * sums[0]]
        for c in range(2):
            out[c, 0, :, at] = halves[c]
        if running == "make":
            rate = jnp.where(pl.program_id(0) == 0, alpha_ref[:, at], beta_ref[:, at])
            part = jnp.concatenate([halves[0] * rate, halves[1] * rate], axis=1)
            total = jnp.dot(tri_ref[...], part, precision=HIGHEST, preferred_element_type=F32)

            @pl.when(pl.program_id(0) == 0)
            def _():
                for c in range(2):
                    outs[1][c, :, at] = total[:, c * LANES : (c + 1) * LANES]

            @pl.when(pl.program_id(0) != 0)
            def _():
                for c in range(2):
                    outs[1][c, :, at] += total[:, c * LANES : (c + 1) * LANES]


def post(sz, row_scale, me, pieces, fields, held, running=None, extra=()):
    count = len(fields)
    stride = fields[1] - fields[0] if count > 1 else 1
    first = fields[0]
    w = jnp.asarray(complex_lanes(span_matrix(-1) / NK))
    w_spec = pl.BlockSpec((2 * LANES, 2 * LANES), lambda i, me: (0, 0))
    in_specs = [pl.BlockSpec((1, sz.body, LANES), lambda i, me: (i, 0, 0))] * sz.group + [w_spec]
    row_spec = pl.BlockSpec((1, sz.slots), lambda i, me: (0, 0))
    sums_spec = pl.BlockSpec((2, sz.block_rows, sz.slots), lambda i, me: (0, 0, 0))
    if running == "add":
        in_specs += [sums_spec, pl.BlockSpec((2, sz.slots), lambda i, me: (0, 0))]
    elif running == "make":
        square = pl.BlockSpec((sz.block_rows, sz.block_rows), lambda i, me: (0, 0))
        in_specs += [row_spec, row_spec, square]
    out_specs = [
        pl.BlockSpec((2, 1, sz.block_rows, sz.slots), lambda i, me: (0, first + stride * i, 0, 0))
    ]
    out_shape = [jax.ShapeDtypeStruct((2, 5, sz.block_rows, sz.slots), F32)]
    aliases = {}
    operands = [me, *pieces, w, *extra]
    if running == "make":
        out_specs.append(sums_spec)
        out_shape.append(jax.ShapeDtypeStruct((2, sz.block_rows, sz.slots), F32))
    else:
        in_specs.append(pl.BlockSpec(memory_space=pl.ANY))
        operands.append(held)
        aliases = {len(operands) - 1: 0}
    return pl.pallas_call(
        functools.partial(post_kernel, sz, running, row_scale),
        grid_spec=pltpu.PrefetchScalarGridSpec(
            num_scalar_prefetch=1,
            grid=(count,),
            in_specs=in_specs,
            out_specs=out_specs,
            scratch_shapes=[pltpu.VMEM((sz.lane_groups, sz.block_rows, 2 * LANES), F32)],
        ),
        out_shape=out_shape,
        input_output_aliases=aliases,
        compiler_params=VMEM,
        name="post",
    )(*operands)


def exchange(pieces):
    group = lax.axis_size("mode")
    return [pieces[0]] + [
        lax.ppermute(pieces[k], "mode", [(i, i ^ k) for i in range(group)])
        for k in range(1, group)
    ]


def device_of(position):
    group, blocks = lax.axis_size("mode"), lax.axis_size(ROW_BLOCKS)
    return position % group * blocks + position // group


def chain(value, step):
    count = lax.axis_size(ALL_AXES)
    pairs = [
        (device_of(i), device_of(i + step)) for i in range(count) if 0 <= i + step < count
    ]
    return lax.ppermute(value, ALL_AXES, pairs)


def on_device(adjoint, forward, mode_map):
    sz = Sizes(adjoint.shape[2], adjoint.shape[3])
    stations = lax.axis_size("ckpt")
    row_scale = 1.0 / math.sqrt(sz.block_rows * lax.axis_size("wall") * stations)
    me = lax.axis_index("mode").astype(jnp.int32)
    me_arg = me.reshape(1)

    freq_index = lax.div(mode_map, jnp.int32(NK))
    span_index = lax.rem(mode_map, jnp.int32(NK))
    alpha = 2.0 / NF * ((freq_index + NF // 2) % NF - NF // 2).astype(F32)
    beta = 2.0 / NK * ((span_index + NK // 2) % NK - NK // 2).astype(F32)
    freqs = lax.all_gather(freq_index.reshape(sz.blocks, NK)[:, 0], "mode", axis=0)
    table = freqs[jnp.arange(sz.group, dtype=jnp.int32) ^ me].reshape(-1)

    blocks = lax.axis_size(ROW_BLOCKS)
    low = lax.ppermute(adjoint[:, :, -1:], ROW_BLOCKS, [(i, i + 1) for i in range(blocks - 1)])
    high = lax.ppermute(adjoint[:, :, :1], ROW_BLOCKS, [(i + 1, i) for i in range(blocks - 1)])
    rims = jnp.concatenate([low, high, jnp.zeros_like(adjoint[:, :, :6])], 2)

    here = lax.axis_index("ckpt")
    parts = forward.reshape(2, stations, sz.block_rows, sz.slots)
    both = lax.all_to_all(parts, "ckpt", split_axis=1, concat_axis=1, tiled=True)
    both = jnp.moveaxis(both, 1, 0)

    chunks = [(0, 2), (3, 4), (1,)]
    adjoint_pieces = [exchange(adjoint_prep(sz, me_arg, adjoint, rims, c)) for c in chunks]
    phys = forward_physical(sz, table, exchange(forward_prep(sz, me_arg, both)))

    current = []
    for index, fields in enumerate(chunks):
        stepped, first, last, total = station_one(sz, table, adjoint_pieces[index], phys, 1)
        if index == 0:
            pair = stepped
            freq_ids = np.arange(NF)
            rate = (2.0 / NF * ((freq_ids + NF // 2) % NF - NF // 2)).astype(np.float32)
            bmat = beta_matrix()
            mixed = np.block([[bmat.real, bmat.imag], [-bmat.imag, bmat.real]]).astype(np.float32)
            mine = jnp.asarray(rate)[:, None] * total[0] + jnp.dot(
                total[1], jnp.asarray(mixed), precision=HIGHEST
            )
            everyone = lax.all_gather(mine, ALL_AXES, axis=0)
            order = np.argsort([device_of(i) for i in range(lax.axis_size(ALL_AXES))])
            place = lax.axis_index(ROW_BLOCKS) * sz.group + me
            earlier = jnp.asarray(order, jnp.int32)[:, None, None] < place
            start = jnp.sum(jnp.where(earlier, everyone, 0.0), axis=0)
        if fields == (1,):
            stepped, first, last = add_running(sz, row_scale, stepped, pair, start)
        current.append((stepped, chain(last, 1), chain(first, -1)))

    back = [exchange(station_zero(sz, table, *c, phys, 0)) for c in current]

    tri = jnp.asarray(np.tril(np.ones((sz.block_rows, sz.block_rows), np.float32)))
    out, sums = post(
        sz, row_scale, me_arg, back[0], chunks[0], None, "make", (alpha[None], beta[None], tri)
    )
    totals = lax.all_gather(sums[:, -1], ROW_BLOCKS, axis=0)
    earlier = lax.broadcasted_iota(jnp.int32, totals.shape, 0) < lax.axis_index(ROW_BLOCKS)
    start = jnp.sum(jnp.where(earlier, totals, 0.0), axis=0)
    (out,) = post(sz, row_scale, me_arg, back[1], chunks[1], out)
    (out,) = post(sz, row_scale, me_arg, back[2], chunks[2], out, "add", (sums, start))
    return out


def solution(mesh):
    placed = (P(None, None, ROW_BLOCKS, "mode"), P("ckpt", None, "wall", "mode"), P("mode"))
    return jax.shard_map(
        on_device,
        mesh=mesh,
        in_specs=placed,
        out_specs=P(None, None, ROW_BLOCKS, "mode"),
        check_vma=False,
    )
```

```python
import functools
import math

import jax
import jax.numpy as jnp
import numpy as np
from jax import lax
from jax.experimental import pallas as pl
from jax.experimental.pallas import tpu as pltpu
from jax.sharding import PartitionSpec as P

NF = 64
NK = 64
LANES = 2 * NK
KAPPA = 0.2
COUPLING = 0.5
HIGHEST = lax.Precision.HIGHEST
ROW_BLOCKS = ("wall", "ckpt")
VMEM = pltpu.CompilerParams(vmem_limit_bytes=56 * 1024 * 1024)
F32 = jnp.float32
CHUNKS = ((0, 2), (3, 4, 1))
INWARD = (True, True)
STORED = True
OUTWARD = (True, True)


def complex_lanes(matrix):
    twice = np.kron(np.eye(2), matrix)
    return np.block([[twice.real, twice.imag], [-twice.imag, twice.real]]).astype(np.float32)


def span_matrix(direction):
    ids = np.arange(NK)
    return np.exp(2j * math.pi * direction * (np.outer(ids, ids) % NK) / NK)


def beta_matrix():
    ids = np.arange(NK)
    signed = (ids + NK // 2) % NK - NK // 2
    return span_matrix(-1) @ np.diag(2.0 / NK * signed) @ span_matrix(1) / NK


def split(value):
    high = value.astype(jnp.bfloat16)
    return high, (value - high.astype(F32)).astype(jnp.bfloat16)


def halves_of(matrix):
    high, low = split(jnp.asarray(matrix))
    return jnp.stack([high, low])


def dot3(x, w_ref):
    high, low = split(x)
    dot = functools.partial(jnp.dot, preferred_element_type=F32)
    return (dot(low, w_ref[0]) + dot(high, w_ref[1])) + dot(high, w_ref[0])


def low_half(shape):
    return lax.broadcasted_iota(jnp.int32, shape, len(shape) - 1) < NK


def swap(value):
    return pltpu.roll(value, NK, value.ndim - 1)


def dft4(x, sign):
    (ar, ai), (br, bi), (cr, ci), (dr, di) = x
    pr, pi, mr, mi = ar + cr, ai + ci, ar - cr, ai - ci
    qr, qi, nr, ni = br + dr, bi + di, br - dr, bi - di
    if sign > 0:
        nr, ni = -ni, nr
    else:
        nr, ni = ni, -nr
    return [(pr + qr, pi + qi), (mr + nr, mi + ni), (pr - qr, pi - qi), (mr - nr, mi - ni)]


def dft8(x, sign):
    even = dft4(x[0::2], sign)
    odd = dft4(x[1::2], sign)
    half = math.sqrt(0.5)
    (r1, i1), (r2, i2), (r3, i3) = odd[1], odd[2], odd[3]
    if sign > 0:
        odd[1] = (half * (r1 - i1), half * (i1 + r1))
        odd[2] = (-i2, r2)
        odd[3] = (-half * (r3 + i3), half * (r3 - i3))
    else:
        odd[1] = (half * (r1 + i1), half * (i1 - r1))
        odd[2] = (i2, -r2)
        odd[3] = (half * (i3 - r3), -half * (i3 + r3))
    first = [(a + c, b + d) for (a, b), (c, d) in zip(even, odd)]
    second = [(a - c, b - d) for (a, b), (c, d) in zip(even, odd)]
    return first + second


def turned(pair, power, sign):
    power %= NF
    if power == 0:
        return pair
    angle = 2.0 * math.pi * power / NF
    c, s = math.cos(angle), sign * math.sin(angle)
    re, im = pair
    return (c * re - s * im, c * im + s * re)


class Sizes:
    def __init__(self, rows, slots):
        self.group = lax.axis_size("mode")
        self.block_rows = rows
        self.slots = slots
        self.lane_groups = slots // LANES
        self.blocks = slots // NK
        self.rows = rows // self.group
        self.half = self.rows // 2
        self.tile = min(8, self.half)
        self.tiles = self.half // self.tile
        self.padded = (self.half + 7) // 8 * 8 + 16
        self.body = 2 * self.blocks * self.half
        self.rims = 2 * self.blocks


class Pieces:
    def __init__(self, whole, arrays):
        self.whole, self.arrays = whole, arrays

    def specs(self, group):
        if self.whole:
            length = self.arrays[0].shape[2]
            return [pl.BlockSpec((group, 1, length, LANES), lambda i, *_: (0, i, 0, 0))]
        length = self.arrays[0].shape[1]
        return [pl.BlockSpec((1, length, LANES), lambda i, *_: (i, 0, 0))] * group

    @staticmethod
    def shapes(whole, group, count, length):
        if whole:
            return [jax.ShapeDtypeStruct((group, count, length, LANES), F32)]
        return [jax.ShapeDtypeStruct((count, length, LANES), F32)] * group

    def exchange(self):
        if self.whole:
            return Pieces(True, [lax.all_to_all(self.arrays[0], "mode", 0, 0, tiled=True)])
        group = len(self.arrays)
        moved = [
            lax.ppermute(self.arrays[k], "mode", [(i, i ^ k) for i in range(group)])
            for k in range(1, group)
        ]
        return Pieces(False, [self.arrays[0]] + moved)


def field_at(fields):
    return lambda i: sum(jnp.where(i == n, f, 0) for n, f in enumerate(fields))


def piece_refs(refs, whole, group):
    if whole:
        return [refs[0].at[k, 0] for k in range(group)], refs[1:]
    return [ref.at[0] for ref in refs[:group]], refs[group:]


def partner(whole, me, k):
    return k if whole else me ^ k


def pair_rows(top, bottom):
    low = low_half(top.shape)
    return jnp.where(low, top, swap(bottom)), jnp.where(low, swap(top), bottom)


def cut_pieces(sz, dest, planes, out, base=0):
    row = pl.multiple_of(8 + dest * sz.rows, 8)
    for g in range(sz.lane_groups):
        whole = planes[g, pl.ds(row, sz.rows), :]
        for c in range(2):
            part = whole[:, c * LANES : (c + 1) * LANES]
            for odd, value in enumerate(pair_rows(part[: sz.half], part[sz.half :])):
                place = base + (c * sz.blocks + 2 * g + odd) * sz.half
                out[place : place + sz.half, :] = value


def join(x_ref, at):
    return jnp.concatenate([x_ref[c, ..., at].reshape(-1, LANES) for c in range(2)], axis=1)


def join_rows(x_ref, rows, step, at):
    parts = [
        jnp.concatenate([x_ref[pl.ds(r + c * step, 1), :] for r in rows], axis=0) for c in range(2)
    ]
    at = slice(at.start, at.start + at.size)
    return jnp.concatenate([part[:, at] for part in parts], axis=1)


def put_rows(sz, out, place, rows):
    for c in range(2):
        at = slice(c * LANES, (c + 1) * LANES)
        for g, (down, up) in enumerate(rows):
            for odd, value in enumerate(pair_rows(down[:, at], up[:, at])):
                row = place + c * sz.blocks + 2 * g + odd
                out[row : row + 1, :] = value


def cut_rims(sz, dest, planes, out, place, depths):
    for depth in range(depths):
        down = pl.ds(8 - 1 - depth + dest * sz.rows, 1)
        up = pl.ds(8 + depth + (dest + 1) * sz.rows, 1)
        rows = [(planes[g, down, :], planes[g, up, :]) for g in range(sz.lane_groups)]
        put_rows(sz, out, place + depth * sz.rims, rows)


def adjoint_prep_kernel(sz, whole, with_rims, field, me_ref, x_ref, w_ref, *rest):
    _, *rest = rest
    if with_rims:
        low, high, *rest = rest
        outs, (planes,) = piece_refs(rest, whole, sz.group)
    else:
        outs, (ends, planes) = piece_refs(rest, whole, sz.group)
    body = slice(8, 8 + sz.block_rows)
    row = 2 * field(pl.program_id(0))
    for g in range(sz.lane_groups):
        at = pl.ds(g * LANES, LANES)
        planes[g, body, :] = dot3(
            jnp.concatenate([x_ref[0, 0, :, at], x_ref[1, 0, :, at]], axis=1), w_ref
        )
        if with_rims:
            step = low.shape[0] // 2 - 1
            planes[g, 6:8, :] = dot3(join_rows(low, (row, row + 1), step, at), w_ref)
            planes[g, 8 + sz.block_rows : 10 + sz.block_rows, :] = dot3(
                join_rows(high, (row, row + 1), step, at), w_ref
            )
    for k in range(sz.group):
        dest = partner(whole, me_ref[0], k)
        cut_pieces(sz, dest, planes, outs[k])
        if with_rims:
            cut_rims(sz, dest, planes, outs[k], sz.body, 2)
        else:
            for g in range(sz.lane_groups):
                for n, row in enumerate((0, 1, sz.rows - 1, sz.rows - 2)):
                    row = 8 + k * sz.rows + row
                    ends[0, n, g, k : k + 1, :] = planes[g, row : row + 1, :]


def adjoint_prep(sz, whole, me, adjoint, w, fields, after, edges=None):
    count = len(fields)
    field = field_at(fields)
    with_rims = edges is not None
    shapes = Pieces.shapes(whole, sz.group, count, sz.body + (2 * sz.rims if with_rims else 0))
    in_specs = [
        pl.BlockSpec((2, 1, sz.block_rows, sz.slots), lambda i, me: (0, field(i), 0, 0)),
        pl.BlockSpec(w.shape, lambda i, me: (0, 0, 0)),
        pl.BlockSpec(memory_space=pl.ANY),
    ]
    operands = [me, adjoint, w, after]
    out_specs, out_shape = Pieces(whole, shapes).specs(sz.group), list(shapes)
    if with_rims:
        in_specs += [pl.BlockSpec(x.shape, lambda i, me: (0, 0)) for x in edges]
        operands += edges
    else:
        ends = (4, sz.lane_groups, sz.group, 2 * LANES)
        out_specs.append(pl.BlockSpec((1,) + ends, lambda i, me: (i, 0, 0, 0, 0)))
        out_shape.append(jax.ShapeDtypeStruct((count,) + ends, F32))
    arrays = pl.pallas_call(
        functools.partial(adjoint_prep_kernel, sz, whole, with_rims, field),
        grid_spec=pltpu.PrefetchScalarGridSpec(
            num_scalar_prefetch=1,
            grid=(count,),
            in_specs=in_specs,
            out_specs=out_specs,
            scratch_shapes=[pltpu.VMEM((sz.lane_groups, sz.block_rows + 16, 2 * LANES), F32)],
        ),
        out_shape=out_shape,
        compiler_params=VMEM,
        name="adjoint_prep",
    )(*operands)
    return Pieces(whole, arrays[: len(shapes)]), arrays[len(shapes) :]


def forward_prep_kernel(
    sz, whole, chunk, me_ref, own, other, before, low, high, past, ends, freq, w_ref, *rest
):
    outs, (planes, rims) = piece_refs(rest, whole, sz.group)
    here = me_ref[1]
    body = slice(8, 8 + sz.block_rows)
    for g in range(sz.lane_groups):
        at = pl.ds(g * LANES, LANES)
        for x_ref, station in ((own, here), (other, 1 - here)):
            planes[station, g, body, :] = dot3(join(x_ref.at[0], at), w_ref)
        count = low.shape[0] - 2
        step = count // 2
        inner = here == 0
        row = [before[0, c, 7:8, at] for c in range(2)]
        row = jnp.concatenate(row, axis=1)
        row = jnp.where(inner, join_rows(low, (count,), 1, at), row)
        planes[1, g, 7:8, :] = dot3(row, w_ref)
        row = jnp.where(inner, join_rows(high, (count,), 1, at), join_rows(past, (0,), 1, at))
        planes[1, g, 8 + sz.block_rows : 9 + sz.block_rows, :] = dot3(row, w_ref)
        far_low, far_high = (
            dot3(jnp.concatenate([x_ref[c * step : (c + 1) * step, at] for c in range(2)], 1), w_ref)
            for x_ref in (low, high)
        )
        for i, field in enumerate(chunk):
            for depth in range(2):
                row = 2 * field + 1 - depth
                rims[i, depth, 0, g] = jnp.concatenate(
                    [far_low[row : row + 1], ends[i, 2 + depth, g][:-1]], 0
                )
                row = 2 * field + depth
                rims[i, depth, 1, g] = jnp.concatenate(
                    [ends[i, depth, g][1:], far_high[row : row + 1]], 0
                )
    for k in range(sz.group):
        dest = partner(whole, me_ref[0], k)
        outs[k][:8, :] = freq[...]
        for station in range(2):
            cut_pieces(sz, dest, planes.at[station], outs[k], 8 + station * sz.body)
        place = 8 + 2 * sz.body
        cut_rims(sz, dest, planes.at[1], outs[k], place, 1)
        row = pl.ds(dest, 1)
        for i in range(len(chunk)):
            for depth in range(2):
                place += sz.rims
                rows = [
                    (rims[i, depth, 0, g, row, :], rims[i, depth, 1, g, row, :])
                    for g in range(sz.lane_groups)
                ]
                put_rows(sz, outs[k], place, rows)


def forward_prep(sz, whole, me, forward, other, edges, ends, freq, w, chunk):
    length = (8 + 2 * sz.body + (1 + 2 * len(chunk)) * sz.rims + 7) // 8 * 8
    shapes = Pieces.shapes(whole, sz.group, 1, length)
    rows = (1, 2, sz.block_rows, sz.slots)
    rest = [*edges, ends, freq, w]
    before = sz.block_rows // 8 - 1
    arrays = pl.pallas_call(
        functools.partial(forward_prep_kernel, sz, whole, chunk),
        grid_spec=pltpu.PrefetchScalarGridSpec(
            num_scalar_prefetch=1,
            grid=(1,),
            in_specs=[
                pl.BlockSpec(rows, lambda i, me: (0, 0, me[1], 0)),
                pl.BlockSpec(rows, lambda i, me: (0, 0, 0, 0)),
                pl.BlockSpec((1, 2, 8, sz.slots), lambda i, me: (0, 0, before, 0)),
            ]
            + [pl.BlockSpec(x.shape, lambda i, me, zeros=(0,) * x.ndim: zeros) for x in rest],
            out_specs=Pieces(whole, shapes).specs(sz.group),
            scratch_shapes=[
                pltpu.VMEM((2, sz.lane_groups, sz.block_rows + 16, 2 * LANES), F32),
                pltpu.VMEM((len(chunk), 2, 2, sz.lane_groups, sz.group, 2 * LANES), F32),
            ],
        ),
        out_shape=shapes,
        compiler_params=VMEM,
        name="forward_prep",
    )(me, forward, other, forward, *rest)
    return Pieces(whole, arrays)


def frequency(sz, table_ref, whole, k, j):
    place = k ^ table_ref[sz.group * sz.blocks] if whole else k
    return table_ref[place * sz.blocks + j]


def gather_pieces(sz, table_ref, whole, pieces, state, lead, base=0):
    for k, piece in enumerate(pieces):
        for j in range(sz.blocks):
            freq = frequency(sz, table_ref, whole, k, j)
            for c in range(2):
                at = base + (c * sz.blocks + j) * sz.half
                state[c, freq, lead : lead + sz.half, :] = piece[at : at + sz.half, :]


def lead_first(sz, state, rows, work, out_rows):
    for a in range(8):
        x = [(state[0, a + 8 * b, rows, :], state[1, a + 8 * b, rows, :]) for b in range(8)]
        for t, pair in enumerate(dft8(x, 1)):
            re, im = turned(pair, a * t, 1)
            work[0, 8 * t + a, out_rows, :] = re
            work[1, 8 * t + a, out_rows, :] = im


def lead_second(work, t, rows):
    x = [(work[0, 8 * t + a, rows, :], work[1, 8 * t + a, rows, :]) for a in range(8)]
    return dft8(x, 1)


def couple(sz, state, rows, work, work_rows, phys, phys_rows, store):
    lead_first(sz, state, rows, work, work_rows)
    for t in range(8):
        product = []
        for u, (re, im) in enumerate(lead_second(work, t, work_rows)):
            wr, wi = phys[0, 8 * t + u, phys_rows, :], phys[1, 8 * t + u, phys_rows, :]
            product.append((wr * re + wi * im, wr * im - wi * re))
        for a, pair in enumerate(dft8(product, -1)):
            re, im = turned(pair, a * t, -1)
            work[0, 8 * t + a, work_rows, :] = re
            work[1, 8 * t + a, work_rows, :] = im
    for a in range(8):
        x = [
            (work[0, 8 * t + a, work_rows, :], work[1, 8 * t + a, work_rows, :]) for t in range(8)
        ]
        for b, pair in enumerate(dft8(x, -1)):
            store(a + 8 * b, pair)


def gather_rims(sz, table_ref, whole, pieces, rims, base):
    for k, piece in enumerate(pieces):
        for j in range(sz.blocks):
            freq = frequency(sz, table_ref, whole, k, j)
            for c in range(2):
                at = base + c * sz.blocks + j
                rims[c, pl.ds(freq, 1), :] = piece[at : at + 1, :]


def forward_kernel(sz, whole, chunk, me_ref, *rest):
    pieces, rest = piece_refs(rest, whole, sz.group)
    heads, rest = piece_refs(rest, whole, sz.group)
    out, next_out, rims, table_ref, state, work, next_state, next_work = rest
    count = sz.group * sz.blocks
    for k in range(sz.group):
        place = k ^ me_ref[0] if whole else k
        for j in range(sz.blocks):
            table_ref[place * sz.blocks + j] = heads[k][j, 0].astype(jnp.int32)
    for n in range(4):
        table_ref[count + n] = me_ref[n]
    for station in range(2):
        gather_pieces(sz, table_ref, whole, pieces, state, 0, 8 + station * sz.body)

        @pl.loop(0, sz.tiles)
        def _(s):
            rows = pl.ds(s * sz.tile, sz.tile)
            lead_first(sz, state, rows, work, rows)
            for t in range(8):
                for u, (re, im) in enumerate(lead_second(work, t, rows)):
                    out[station, 0, 8 * t + u, rows, :] = re
                    out[station, 1, 8 * t + u, rows, :] = im

    base = 8 + 2 * sz.body
    gather_rims(sz, table_ref, whole, pieces, rims.at[0, 0], base)
    spread_rims(rims[0, 0].reshape(2 * NF, LANES), next_state, 0)
    rows = slice(0, 8)
    lead_first(sz, next_state, rows, next_work, rows)
    for t in range(8):
        for u, (re, im) in enumerate(lead_second(next_work, t, rows)):
            next_out[0, 8 * t + u] = re[:1]
            next_out[1, 8 * t + u] = im[:1]
    for i in range(chunk):
        for depth in range(2):
            base += sz.rims
            gather_rims(sz, table_ref, whole, pieces, rims.at[i, depth], base)


def forward_physical(sz, me, pieces, chunk):
    full = (2, NF, sz.half, LANES)
    rims = (chunk, 2, 2, NF, LANES)
    if pieces.whole:
        heads = [
            pl.BlockSpec((sz.group, 1, 8, LANES), lambda i, t: (0, 0, 0, 0), memory_space=pltpu.SMEM)
        ]
    else:
        head = pl.BlockSpec((1, 8, LANES), lambda i, t: (0, 0, 0), memory_space=pltpu.SMEM)
        heads = [head] * sz.group
    return pl.pallas_call(
        functools.partial(forward_kernel, sz, pieces.whole, chunk),
        grid_spec=pltpu.PrefetchScalarGridSpec(
            num_scalar_prefetch=1,
            grid=(1,),
            in_specs=pieces.specs(sz.group) + heads,
            out_specs=[
                pl.BlockSpec((2,) + full, lambda i, t: (0, 0, 0, 0, 0)),
                pl.BlockSpec((2, NF, 1, LANES), lambda i, t: (0, 0, 0, 0)),
                pl.BlockSpec(rims, lambda i, t: (0, 0, 0, 0, 0)),
                pl.BlockSpec(memory_space=pltpu.SMEM),
            ],
            scratch_shapes=[
                pltpu.VMEM(full, F32),
                pltpu.VMEM(full, F32),
                pltpu.VMEM((2, NF, 8, LANES), F32),
                pltpu.VMEM((2, NF, 8, LANES), F32),
            ],
        ),
        out_shape=[
            jax.ShapeDtypeStruct((2,) + full, F32),
            jax.ShapeDtypeStruct((2, NF, 1, LANES), F32),
            jax.ShapeDtypeStruct(rims, F32),
            jax.ShapeDtypeStruct((sz.group * sz.blocks + 4,), jnp.int32),
        ],
        compiler_params=VMEM,
        name="forward_physical",
    )(me, *pieces.arrays, *pieces.arrays)


def spread_rims(rims, state, n):
    state.reshape(2 * NF * 8, LANES)[pl.ds(n, 2 * NF, stride=8), :] = rims


def place_edges(sz, state, rims):
    padded = sz.padded
    rows = state.reshape(2 * NF * padded, LANES)
    first = rows[pl.ds(8, 2 * NF, stride=padded), :]
    last = rows[pl.ds(8 + sz.half - 1, 2 * NF, stride=padded), :]
    low = low_half(first.shape)
    rows[pl.ds(7, 2 * NF, stride=padded), :] = jnp.where(low, rims, swap(last))
    rows[pl.ds(8 + sz.half, 2 * NF, stride=padded), :] = jnp.where(low, swap(first), rims)


def advance(sz, state, work, phys, out, lead):
    @pl.loop(0, sz.tiles)
    def _(s):
        rows = pl.ds(8 + s * sz.tile, sz.tile)
        at = pl.ds(s * sz.tile, sz.tile)

        def store(f, pair):
            for c in range(2):
                mid = state[c, f, rows, :]
                up = state[c, f, pl.ds(9 + s * sz.tile, sz.tile), :]
                down = state[c, f, pl.ds(7 + s * sz.tile, sz.tile), :]
                stepped = (1.0 - 2.0 * KAPPA) * mid + KAPPA * (up + down)
                out[c, f, pl.ds(lead + s * sz.tile, sz.tile), :] = (
                    stepped - (COUPLING / NF) * pair[c]
                )

        couple(sz, state, rows, work, at, phys, at, store)


def march_kernel(sz, whole_in, whole_out, row_scale, fields, table_ref, *rest):
    pieces, rest = piece_refs(rest, whole_in, sz.group)
    phys, next_phys, *rest = rest
    running = row_scale is not None
    if running:
        all_rims, rest = rim_refs(rest, whole_in, sz.group)
        pair, pair_rims, start, w_ref, *rest = rest
    else:
        rims_in, w_ref, *rest = rest
    outs, rest = piece_refs(rest, whole_out, sz.group)
    if not running:
        pair_out, pair_rims_out, total_out, *rest = rest
    state, work, middle, stepped, rims, next_state, next_work, next_coupling, sums = rest
    step = pl.program_id(0)
    count = sz.group * sz.blocks

    @pl.when(step == 0)
    def _():
        next_state[...] = jnp.zeros_like(next_state)
        for i in range(fields):
            for depth in range(2):
                if running:
                    views = [ref.at[i] for ref in all_rims]
                    gather_rims(sz, table_ref, whole_in, views, rims.at[i, depth], depth * sz.rims)
                else:
                    rims[i, depth] = rims_in[i, depth]
            spread_rims(rims[i, 0].reshape(2 * NF, LANES), next_state, i)
        rows = slice(0, 8)

        def store(f, pair):
            for c in range(2):
                next_coupling[c, f] = (COUPLING / NF) * pair[c]

        couple(sz, next_state, rows, next_work, rows, next_phys, slice(0, 1), store)

    gather_pieces(sz, table_ref, whole_in, pieces, state, 8)
    near = rims[step, 0].reshape(2 * NF, LANES)
    place_edges(sz, state, near)
    advance(sz, state, work, phys.at[1], middle, 8)

    low = low_half((2 * NF, LANES))
    flat = state.reshape(2 * NF * sz.padded, LANES)
    inner = jnp.where(
        low,
        flat[pl.ds(8, 2 * NF, stride=sz.padded), :],
        flat[pl.ds(8 + sz.half - 1, 2 * NF, stride=sz.padded), :],
    )
    far = rims[step, 1].reshape(2 * NF, LANES)
    coupled = next_coupling.reshape(2 * NF * 8, LANES)[pl.ds(step, 2 * NF, stride=8), :]
    near = (1.0 - 2.0 * KAPPA) * near + KAPPA * (inner + far) - coupled
    rims[step, 0] = near.reshape(2, NF, LANES)
    if running:

        @pl.when(step == fields - 1)
        def _():
            add_running(
                sz, row_scale, middle, rims.at[step, 0], pair, pair_rims, start, w_ref, next_work
            )

    first = table_ref[count + 2].astype(F32)
    last = table_ref[count + 3].astype(F32)
    near = rims[step, 0].reshape(2 * NF, LANES) * jnp.where(low, 1.0 - first, 1.0 - last)
    if not running:
        pair_rims_out[0] = near.reshape(2, NF, LANES)
        body = middle[:, :, 8 : 8 + sz.half, :]
        pair_out[0] = body
        value = jnp.sum(body, axis=2)
        value = value + swap(value)

        @pl.when(step == 0)
        def _():
            freq = lax.broadcasted_iota(jnp.int32, value.shape, 1)
            rate = 2.0 / NF * ((freq + NF // 2) % NF - NF // 2).astype(F32)
            sums[...] = rate * value

        @pl.when(step != 0)
        def _():
            turned = dot3(jnp.concatenate([value[0], value[1]], axis=1), w_ref)
            re, im = sums[0] + turned[:, :LANES], sums[1] + turned[:, LANES:]
            total = jnp.where(low_half((NF, LANES)), re, im)
            total_out[...] = total

    place_edges(sz, middle, near)
    advance(sz, middle, work, phys.at[0], stepped, 0)
    for k in range(sz.group):
        for j in range(sz.blocks):
            freq = frequency(sz, table_ref, whole_out, k, j)
            for c in range(2):
                at = (c * sz.blocks + j) * sz.half
                outs[k][at : at + sz.half, :] = stepped[c, freq]


def rim_refs(refs, whole, group):
    if whole:
        return [refs[0].at[k] for k in range(group)], refs[1:]
    return list(refs[:group]), refs[group:]


def march(sz, whole_out, table, pieces, phys, next_phys, fields, rims=None, row_scale=None, running=()):
    full = (2, NF, sz.half, LANES)
    shapes = Pieces.shapes(whole_out, sz.group, fields, sz.body)

    def constant(x):
        return pl.BlockSpec(x.shape, lambda i, t, zeros=(0,) * len(x.shape): zeros)

    def by_field(shape):
        return pl.BlockSpec((1,) + shape, lambda i, t, zeros=(0,) * len(shape): (i,) + zeros)

    body = Pieces(pieces.whole, Pieces.shapes(pieces.whole, sz.group, fields, sz.body))
    in_specs = body.specs(sz.group) + [constant(phys), constant(next_phys)]
    operands = [table, *pieces.arrays, phys, next_phys]
    out_specs, out_shape = Pieces(whole_out, shapes).specs(sz.group), list(shapes)
    if running:
        place = sz.body // (2 * sz.rims)
        if pieces.whole:
            block = (sz.group, fields, 2 * sz.rims, LANES)
            in_specs.append(pl.BlockSpec(block, lambda i, t: (0, 0, place, 0)))
        else:
            block = (fields, 2 * sz.rims, LANES)
            in_specs += [pl.BlockSpec(block, lambda i, t: (0, place, 0))] * sz.group
        in_specs += [constant(x) for x in running]
        operands += [*pieces.arrays, *running]
    else:
        in_specs += [constant(x) for x in rims]
        operands += rims
        for shape in (full, (2, NF, LANES)):
            out_specs.append(by_field(shape))
            out_shape.append(jax.ShapeDtypeStruct((fields,) + shape, F32))
        out_shape.append(jax.ShapeDtypeStruct((NF, LANES), F32))
        out_specs.append(constant(out_shape[-1]))
    padded = pltpu.VMEM((2, NF, sz.padded, LANES), F32)
    small = pltpu.VMEM((2, NF, 8, LANES), F32)
    arrays = pl.pallas_call(
        functools.partial(march_kernel, sz, pieces.whole, whole_out, row_scale, fields),
        grid_spec=pltpu.PrefetchScalarGridSpec(
            num_scalar_prefetch=1,
            grid=(fields,),
            in_specs=in_specs,
            out_specs=out_specs,
            scratch_shapes=[
                padded,
                pltpu.VMEM(full, F32),
                padded,
                pltpu.VMEM(full, F32),
                pltpu.VMEM((fields, 2, 2, NF, LANES), F32),
                small,
                small,
                small,
                pltpu.VMEM((2, NF, LANES), F32),
            ],
        ),
        out_shape=out_shape,
        compiler_params=VMEM,
        name="march",
    )(*operands)
    return Pieces(whole_out, arrays[: len(shapes)]), arrays[len(shapes) :]


def running_rows(sz, value, start):
    row = lax.broadcasted_iota(jnp.int32, value.shape, 0)
    reach = 1
    while reach < sz.half:
        value = value + jnp.where(row >= reach, pltpu.roll(value, reach, 0), 0.0)
        reach *= 2
    bottom = jnp.where(low_half((1, LANES)), 0.0, swap(value[sz.half - 1 :]))
    return value + (bottom + start)


def add_running(sz, row_scale, middle, near, pair, pair_rims, start, w_ref, work):
    both = jnp.concatenate([pair[1, 0], pair[1, 1]], axis=2).reshape(NF * sz.half, 2 * LANES)
    turned_two = dot3(both, w_ref)
    turned_rims = dot3(jnp.concatenate([pair_rims[1, 0], pair_rims[1, 1]], axis=1), w_ref)
    low = low_half((1, LANES))
    for f in range(NF):
        at = f * sz.half
        alpha = 2.0 / NF * ((f + NF // 2) % NF - NF // 2)
        spread = start[pl.ds(f, 1), :]
        starts = (jnp.where(low, spread, swap(spread)), jnp.where(low, swap(spread), spread))
        run = []
        for c in range(2):
            lanes = slice(c * LANES, (c + 1) * LANES)
            source = turned_two[at : at + sz.half, lanes] + alpha * pair[0, c, f]
            run.append(running_rows(sz, source, starts[c]))
            past = turned_rims[f : f + 1, lanes] + alpha * pair_rims[0, c, f : f + 1, :]
            work[c, f, 0:1, :] = jnp.where(low, starts[c], run[c][sz.half - 1 :] + past)
        rows = slice(8, 8 + sz.half)
        middle[0, f, rows, :] += row_scale * run[1]
        middle[1, f, rows, :] -= row_scale * run[0]
        near[0, f : f + 1, :] += row_scale * work[1, f, 0:1, :]
        near[1, f : f + 1, :] -= row_scale * work[0, f, 0:1, :]


def join_pieces(sz, whole, me, pieces, planes):
    for k, piece in enumerate(pieces):
        row = pl.multiple_of(partner(whole, me, k) * sz.rows, sz.rows)
        for g in range(sz.lane_groups):
            halves = []
            for c in range(2):
                at = (c * sz.blocks + 2 * g) * sz.half
                even = piece[at : at + sz.half, :]
                odd = piece[at + sz.half : at + 2 * sz.half, :]
                low = low_half(even.shape)
                top = jnp.where(low, even, swap(odd))
                bottom = jnp.where(low, swap(even), odd)
                halves.append(jnp.concatenate([top, bottom], axis=0))
            planes[g, pl.ds(row, sz.rows), :] = jnp.concatenate(halves, axis=1)


def post_kernel(sz, whole, running, row_scale, me_ref, *rest):
    pieces, rest = piece_refs(rest, whole, sz.group)
    w_ref, rest = rest[0], rest[1:]
    if running == "add":
        sums_ref, start_ref, rest = rest[0], rest[1], rest[2:]
    elif running == "make":
        alpha_ref, beta_ref, tri_ref, rest = rest[0], rest[1], rest[2], rest[3:]
        rest, source = rest[:-1], rest[-1]
    planes = rest[-1]
    outs = rest[:-1]
    if running != "make":
        outs = outs[1:]
    out = outs[0]
    join_pieces(sz, whole, me_ref[0], pieces, planes)
    for g in range(sz.lane_groups):
        at = pl.ds(g * LANES, LANES)
        back = dot3(planes[g], w_ref)
        halves = [back[:, :LANES], back[:, LANES:]]
        for c in range(2):
            out[c, 0, :, at] = halves[c]
        if running == "add":

            @pl.when(pl.program_id(0) == pl.num_programs(0) - 1)
            def _():
                sums = [sums_ref[c, :, at] + start_ref[pl.ds(c, 1), at] for c in range(2)]
                out[0, 0, :, at] += row_scale * sums[1]
                out[1, 0, :, at] -= row_scale * sums[0]

        if running == "make":

            @pl.when(pl.program_id(0) == 0)
            def _():
                for c in range(2):
                    source[g, :, c * LANES : (c + 1) * LANES] = halves[c] * alpha_ref[:, at]

            @pl.when(pl.program_id(0) != 0)
            def _():
                both = [
                    source[g, :, c * LANES : (c + 1) * LANES] + halves[c] * beta_ref[:, at]
                    for c in range(2)
                ]
                high, low = split(jnp.concatenate(both, axis=1))
                tri = tri_ref[...]
                total = jnp.dot(tri, low, preferred_element_type=F32)
                total = total + jnp.dot(tri, high, preferred_element_type=F32)
                for c in range(2):
                    outs[1][c, :, at] = total[:, c * LANES : (c + 1) * LANES]
                    outs[2][c : c + 1, at] = total[-1:, c * LANES : (c + 1) * LANES]


def post(sz, row_scale, me, pieces, fields, held, running=None, extra=()):
    count = len(fields)
    field = field_at(fields)
    w = halves_of(complex_lanes(span_matrix(-1) / NK))
    w_spec = pl.BlockSpec((2, 2 * LANES, 2 * LANES), lambda i, me: (0, 0, 0))
    in_specs = pieces.specs(sz.group) + [w_spec]
    row_spec = pl.BlockSpec((1, sz.slots), lambda i, me: (0, 0))
    sums_spec = pl.BlockSpec((2, sz.block_rows, sz.slots), lambda i, me: (0, 0, 0))
    if running == "add":
        in_specs += [sums_spec, pl.BlockSpec((2, sz.slots), lambda i, me: (0, 0))]
    elif running == "make":
        square = pl.BlockSpec((sz.block_rows, sz.block_rows), lambda i, me: (0, 0))
        in_specs += [row_spec, row_spec, square]
    out_specs = [
        pl.BlockSpec((2, 1, sz.block_rows, sz.slots), lambda i, me: (0, field(i), 0, 0))
    ]
    out_shape = [jax.ShapeDtypeStruct((2, 5, sz.block_rows, sz.slots), F32)]
    aliases = {}
    operands = [me, *pieces.arrays, w, *extra]
    plane = pltpu.VMEM((sz.lane_groups, sz.block_rows, 2 * LANES), F32)
    if running == "make":
        out_specs.append(sums_spec)
        out_shape.append(jax.ShapeDtypeStruct((2, sz.block_rows, sz.slots), F32))
        out_specs.append(pl.BlockSpec((2, sz.slots), lambda i, me: (0, 0)))
        out_shape.append(jax.ShapeDtypeStruct((2, sz.slots), F32))
    else:
        in_specs.append(pl.BlockSpec(memory_space=pl.ANY))
        operands.append(held)
        aliases = {len(operands) - 1: 0}
    return pl.pallas_call(
        functools.partial(post_kernel, sz, pieces.whole, running, row_scale),
        grid_spec=pltpu.PrefetchScalarGridSpec(
            num_scalar_prefetch=1,
            grid=(count,),
            in_specs=in_specs,
            out_specs=out_specs,
            scratch_shapes=[plane] * (2 if running == "make" else 1),
        ),
        out_shape=out_shape,
        input_output_aliases=aliases,
        compiler_params=VMEM,
        name="post",
    )(*operands)


def follow(pieces, earlier):
    def kernel(*refs):
        pass

    count = len(pieces.arrays)
    in_place = pl.BlockSpec(memory_space=pl.ANY)
    arrays = pl.pallas_call(
        kernel,
        in_specs=[in_place] * (count + len(earlier)),
        out_specs=[in_place] * count,
        out_shape=[jax.ShapeDtypeStruct(x.shape, x.dtype) for x in pieces.arrays],
        input_output_aliases={n: n for n in range(count)},
        name="follow",
    )(*pieces.arrays, *earlier)
    return Pieces(pieces.whole, arrays)


def edge_kernel(first_ref, last_ref, before, middle, after, token, low, high, past):
    rows = first_ref.shape[1] * 2
    for c in range(2):
        for field in range(first_ref.shape[1]):
            at = c * rows + 2 * field
            low[at : at + 2, :] = last_ref[c, field, 6:8, :]
            high[at : at + 2, :] = first_ref[c, field, 0:2, :]
        at = 2 * rows + c
        low[at : at + 1, :] = after[0, c, 7:8, :]
        high[at : at + 1, :] = middle[0, c, 0:1, :]
        past[c : c + 1, :] = before[0, c, 0:1, :]


def edge_rows(sz, adjoint, forward, after):
    parts, fields = adjoint.shape[:2]
    rows = (parts, fields, 8, sz.slots)
    stored = (1, parts, 8, sz.slots)
    tiles = sz.block_rows // 8
    last = forward.shape[2] // 8 - 1
    count = parts * fields * 2 + parts
    return pl.pallas_call(
        edge_kernel,
        grid=(1,),
        in_specs=[
            pl.BlockSpec(rows, lambda i: (0, 0, 0, 0)),
            pl.BlockSpec(rows, lambda i: (0, 0, tiles - 1, 0)),
            pl.BlockSpec(stored, lambda i: (0, 0, 0, 0)),
            pl.BlockSpec(stored, lambda i: (0, 0, tiles, 0)),
            pl.BlockSpec(stored, lambda i: (0, 0, last, 0)),
            pl.BlockSpec(memory_space=pl.ANY),
        ],
        out_specs=[pl.BlockSpec((n, sz.slots), lambda i: (0, 0)) for n in (count, count, parts)],
        out_shape=[jax.ShapeDtypeStruct((n, sz.slots), F32) for n in (count, count, parts)],
        name="edge_rows",
    )(adjoint, adjoint, forward, forward, forward, after)


def shifted(value, axes, step, count):
    return lax.ppermute(value, axes, [(i, i + step) for i in range(count) if 0 <= i + step < count])


def nearer_sum_by_pairs(value, axis):
    count, mine = lax.axis_size(axis), lax.axis_index(axis)
    other = lax.ppermute(value, axis, [(i, i ^ 1) for i in range(count)])
    before = jnp.where(mine & 1 != 0, other, 0.0)
    both = total = value + other
    for k in range(2, count, 2):
        other = lax.ppermute(both, axis, [(i, i ^ k) for i in range(count)])
        before = before + jnp.where(mine ^ k < mine, other, 0.0)
        total = total + other
    return before, total


def nearer_sum(value):
    blocks = lax.axis_size(ROW_BLOCKS)
    return sum(shifted(value, ROW_BLOCKS, step, blocks) for step in range(1, blocks))


def on_device(adjoint, forward, mode_map):
    sz = Sizes(adjoint.shape[2], adjoint.shape[3])
    stations = lax.axis_size("ckpt")
    row_scale = 1.0 / math.sqrt(sz.block_rows * lax.axis_size("wall") * stations)
    me = lax.axis_index("mode").astype(jnp.int32)
    here = lax.axis_index("ckpt").astype(jnp.int32)
    block, blocks = lax.axis_index(ROW_BLOCKS), lax.axis_size(ROW_BLOCKS)
    is_first = (block == 0) & (me == 0)
    is_last = (block == blocks - 1) & (me == sz.group - 1)
    place = jnp.stack([me, here, is_first.astype(jnp.int32), is_last.astype(jnp.int32)])
    spread = halves_of(complex_lanes(span_matrix(1)))
    chunks = CHUNKS

    other = lax.dynamic_slice_in_dim(forward, (1 - here) * sz.block_rows, sz.block_rows, 2)
    moved = lax.ppermute(other, "ckpt", [(i, stations - 1 - i) for i in range(stations)])

    pieces, (ends,) = adjoint_prep(sz, INWARD[0], place, adjoint, spread, chunks[0], other)
    inward = [pieces.exchange()]

    low, high, past = edge_rows(sz, adjoint, forward, ends)
    low = shifted(low, ROW_BLOCKS, 1, blocks)
    high = shifted(high, ROW_BLOCKS, -1, blocks)
    past = shifted(past, ROW_BLOCKS, -stations, blocks)

    freq_index = lax.div(mode_map, jnp.int32(NK))
    span_index = lax.rem(mode_map, jnp.int32(NK))
    alpha = 2.0 / NF * ((freq_index + NF // 2) % NF - NF // 2).astype(F32)
    beta = 2.0 / NK * ((span_index + NK // 2) % NK - NK // 2).astype(F32)
    freq = freq_index.reshape(sz.blocks, NK)[:, :1].astype(F32)
    freq = jnp.pad(jnp.broadcast_to(freq, (sz.blocks, LANES)), ((0, 8 - sz.blocks), (0, 0)))

    stored = forward_prep(
        sz, STORED, place, forward, moved, (low, high, past), ends, freq, spread, chunks[0]
    )
    pieces, _ = adjoint_prep(
        sz, INWARD[1], place, adjoint, spread, chunks[1], stored.arrays[0], (low, high)
    )
    stored = follow(stored, inward[0].arrays).exchange()
    inward.append(follow(pieces, stored.arrays).exchange())

    phys, next_phys, rims, table = forward_physical(sz, place, stored, len(chunks[0]))
    turn = halves_of(complex_lanes(beta_matrix()))
    out, (pair, pair_rims, total) = march(
        sz, OUTWARD[0], table, inward[0], phys, next_phys, len(chunks[0]), (rims, turn)
    )
    start, whole = nearer_sum_by_pairs(total, "mode")
    start = start + nearer_sum(whole)
    running = (pair, pair_rims, start, turn)
    back = [follow(out, [start, inward[1].arrays[0]]).exchange()]
    out, _ = march(
        sz,
        OUTWARD[1],
        table,
        inward[1],
        phys,
        next_phys,
        len(chunks[1]),
        row_scale=row_scale,
        running=running,
    )
    back.append(out.exchange())

    tri = jnp.asarray(np.tril(np.ones((sz.block_rows, sz.block_rows))), jnp.bfloat16)
    out, sums, total = post(
        sz, row_scale, place, back[0], chunks[0], None, "make", (alpha[None], beta[None], tri)
    )
    start = nearer_sum(total)
    (out,) = post(sz, row_scale, place, back[1], chunks[1], out, "add", (sums, start))
    return out


def solution(mesh):
    placed = (P(None, None, ROW_BLOCKS, "mode"), P("ckpt", None, "wall", "mode"), P("mode"))
    return jax.shard_map(
        on_device,
        mesh=mesh,
        in_specs=placed,
        out_specs=P(None, None, ROW_BLOCKS, "mode"),
        check_vma=False,
    )
```

```python
import functools
import math

import jax
import jax.numpy as jnp
import numpy as np
from jax import lax
from jax.experimental import pallas as pl
from jax.experimental.pallas import tpu as pltpu
from jax.sharding import PartitionSpec as P

NF = 64
NK = 64
LANES = 2 * NK
KAPPA = 0.2
COUPLING = 0.5
HIGHEST = lax.Precision.HIGHEST
ROW_BLOCKS = ("wall", "ckpt")
VMEM = pltpu.CompilerParams(vmem_limit_bytes=64 * 1024 * 1024)
F32 = jnp.float32
COST = pl.CostEstimate(flops=1, bytes_accessed=1, transcendentals=0)
CHUNKS = ((0, 2, 3), (4, 1))
INWARD = (True, True)
STORED = False
WINDOW = 4
OUTWARD = (True, True)


def complex_lanes(matrix):
    twice = np.kron(np.eye(2), matrix)
    return np.block([[twice.real, twice.imag], [-twice.imag, twice.real]]).astype(np.float32)


def span_matrix(direction):
    ids = np.arange(NK)
    return np.exp(2j * math.pi * direction * (np.outer(ids, ids) % NK) / NK)


def beta_matrix():
    ids = np.arange(NK)
    signed = (ids + NK // 2) % NK - NK // 2
    return span_matrix(-1) @ np.diag(2.0 / NK * signed) @ span_matrix(1) / NK


def split(value):
    high = value.astype(jnp.bfloat16)
    return high, (value - high.astype(F32)).astype(jnp.bfloat16)


def halves_of(matrix):
    high, low = split(jnp.asarray(matrix))
    return jnp.stack([high, low])


def dot3(x, w_ref):
    high, low = split(x)
    dot = functools.partial(jnp.dot, preferred_element_type=F32)
    return (dot(low, w_ref[0]) + dot(high, w_ref[1])) + dot(high, w_ref[0])


def low_half(shape):
    return lax.broadcasted_iota(jnp.int32, shape, len(shape) - 1) < NK


def swap(value):
    return pltpu.roll(value, NK, value.ndim - 1)


def dft4(x, sign):
    (ar, ai), (br, bi), (cr, ci), (dr, di) = x
    pr, pi, mr, mi = ar + cr, ai + ci, ar - cr, ai - ci
    qr, qi, nr, ni = br + dr, bi + di, br - dr, bi - di
    if sign > 0:
        nr, ni = -ni, nr
    else:
        nr, ni = ni, -nr
    return [(pr + qr, pi + qi), (mr + nr, mi + ni), (pr - qr, pi - qi), (mr - nr, mi - ni)]


def dft8(x, sign):
    even = dft4(x[0::2], sign)
    odd = dft4(x[1::2], sign)
    half = math.sqrt(0.5)
    (r1, i1), (r2, i2), (r3, i3) = odd[1], odd[2], odd[3]
    if sign > 0:
        odd[1] = (half * (r1 - i1), half * (i1 + r1))
        odd[2] = (-i2, r2)
        odd[3] = (-half * (r3 + i3), half * (r3 - i3))
    else:
        odd[1] = (half * (r1 + i1), half * (i1 - r1))
        odd[2] = (i2, -r2)
        odd[3] = (half * (i3 - r3), -half * (i3 + r3))
    first = [(a + c, b + d) for (a, b), (c, d) in zip(even, odd)]
    second = [(a - c, b - d) for (a, b), (c, d) in zip(even, odd)]
    return first + second


def turned(pair, power, sign):
    power %= NF
    if power == 0:
        return pair
    angle = 2.0 * math.pi * power / NF
    c, s = math.cos(angle), sign * math.sin(angle)
    re, im = pair
    return (c * re - s * im, c * im + s * re)


class Sizes:
    def __init__(self, rows, slots):
        self.group = lax.axis_size("mode")
        self.block_rows = rows
        self.slots = slots
        self.lane_groups = slots // LANES
        self.blocks = slots // NK
        self.rows = rows // self.group
        self.half = self.rows // 2
        self.tile = min(8, self.half)
        self.tiles = self.half // self.tile
        self.padded = (self.half + 7) // 8 * 8 + 16
        self.body = 2 * self.blocks * self.half
        self.rims = 2 * self.blocks


class Pieces:
    def __init__(self, whole, arrays):
        self.whole, self.arrays = whole, arrays

    def specs(self, group):
        if self.whole:
            length = self.arrays[0].shape[2]
            return [pl.BlockSpec((group, 1, length, LANES), lambda i, *_: (0, i, 0, 0))]
        length = self.arrays[0].shape[1]
        return [pl.BlockSpec((1, length, LANES), lambda i, *_: (i, 0, 0))] * group

    @staticmethod
    def shapes(whole, group, count, length):
        if whole:
            return [jax.ShapeDtypeStruct((group, count, length, LANES), F32)]
        return [jax.ShapeDtypeStruct((count, length, LANES), F32)] * group

    def exchange(self, earlier=()):
        if self.whole:
            array = after(self.arrays[0], *earlier)
            return Pieces(True, [lax.all_to_all(array, "mode", 0, 0, tiled=True)])
        group = len(self.arrays)
        moved = list(self.arrays)
        for n, k in enumerate(partners(group)):
            array = after(moved[k], *earlier[n : n + 1])
            moved[k] = lax.ppermute(array, "mode", [(i, i ^ k) for i in range(group)])
        return Pieces(False, moved)

    def in_order(self):
        if self.whole:
            return list(self.arrays)
        return [self.arrays[k] for k in partners(len(self.arrays))]


def partners(group):
    return sorted(range(1, group), key=lambda k: (-bin(k >> 1).count("1"), k & 1, k))


def field_at(fields):
    return lambda i: sum(jnp.where(i == n, f, 0) for n, f in enumerate(fields))


def piece_refs(refs, whole, group):
    if whole:
        return [refs[0].at[k, 0] for k in range(group)], refs[1:]
    return [ref.at[0] for ref in refs[:group]], refs[group:]


def partner(whole, me, k):
    return k if whole else me ^ k


def pair_rows(top, bottom):
    low = low_half(top.shape)
    return jnp.where(low, top, swap(bottom)), jnp.where(low, swap(top), bottom)


def cut_pieces(sz, dest, planes, out, base=0):
    row = pl.multiple_of(8 + dest * sz.rows, 8)
    for g in range(sz.lane_groups):
        whole = planes[g, pl.ds(row, sz.rows), :]
        for c in range(2):
            part = whole[:, c * LANES : (c + 1) * LANES]
            for odd, value in enumerate(pair_rows(part[: sz.half], part[sz.half :])):
                place = base + (c * sz.blocks + 2 * g + odd) * sz.half
                out[place : place + sz.half, :] = value


def join(x_ref, at):
    return jnp.concatenate([x_ref[c, ..., at].reshape(-1, LANES) for c in range(2)], axis=1)


def join_rows(x_ref, rows, step, at):
    parts = [
        jnp.concatenate([x_ref[pl.ds(r + c * step, 1), :] for r in rows], axis=0) for c in range(2)
    ]
    at = slice(at.start, at.start + at.size)
    return jnp.concatenate([part[:, at] for part in parts], axis=1)


def put_rows(sz, out, place, rows):
    for c in range(2):
        at = slice(c * LANES, (c + 1) * LANES)
        for g, (down, up) in enumerate(rows):
            for odd, value in enumerate(pair_rows(down[:, at], up[:, at])):
                row = place + c * sz.blocks + 2 * g + odd
                out[row : row + 1, :] = value


def cut_rims(sz, dest, planes, out, place, depths):
    for depth in range(depths):
        down = pl.ds(8 - 1 - depth + dest * sz.rows, 1)
        up = pl.ds(8 + depth + (dest + 1) * sz.rows, 1)
        rows = [(planes[g, down, :], planes[g, up, :]) for g in range(sz.lane_groups)]
        put_rows(sz, out, place + depth * sz.rims, rows)


def adjoint_prep_kernel(sz, whole, with_rims, field, me_ref, x_ref, w_ref, *rest):
    _, *rest = rest
    if with_rims:
        low, high, *rest = rest
        outs, (planes,) = piece_refs(rest, whole, sz.group)
    else:
        outs, (ends, planes) = piece_refs(rest, whole, sz.group)
    body = slice(8, 8 + sz.block_rows)
    row = 2 * field(pl.program_id(0))
    for g in range(sz.lane_groups):
        at = pl.ds(g * LANES, LANES)
        planes[g, body, :] = dot3(
            jnp.concatenate([x_ref[0, 0, :, at], x_ref[1, 0, :, at]], axis=1), w_ref
        )
        if with_rims:
            step = low.shape[0] // 2 - 1
            planes[g, 6:8, :] = dot3(join_rows(low, (row, row + 1), step, at), w_ref)
            planes[g, 8 + sz.block_rows : 10 + sz.block_rows, :] = dot3(
                join_rows(high, (row, row + 1), step, at), w_ref
            )
    for k in range(sz.group):
        dest = partner(whole, me_ref[0], k)
        cut_pieces(sz, dest, planes, outs[k])
        if with_rims:
            cut_rims(sz, dest, planes, outs[k], sz.body, 2)
        else:
            for g in range(sz.lane_groups):
                for n, row in enumerate((0, 1, sz.rows - 1, sz.rows - 2)):
                    row = 8 + k * sz.rows + row
                    ends[0, n, g, k : k + 1, :] = planes[g, row : row + 1, :]


def adjoint_prep(sz, whole, me, adjoint, w, fields, after, edges=None):
    count = len(fields)
    field = field_at(fields)
    with_rims = edges is not None
    shapes = Pieces.shapes(whole, sz.group, count, sz.body + (2 * sz.rims if with_rims else 0))
    in_specs = [
        pl.BlockSpec((2, 1, sz.block_rows, sz.slots), lambda i, me: (0, field(i), 0, 0)),
        pl.BlockSpec(w.shape, lambda i, me: (0, 0, 0)),
        pl.BlockSpec(memory_space=pl.ANY),
    ]
    operands = [me, adjoint, w, after]
    out_specs, out_shape = Pieces(whole, shapes).specs(sz.group), list(shapes)
    if with_rims:
        in_specs += [pl.BlockSpec(x.shape, lambda i, me: (0, 0)) for x in edges]
        operands += edges
    else:
        ends = (4, sz.lane_groups, sz.group, 2 * LANES)
        out_specs.append(pl.BlockSpec((1,) + ends, lambda i, me: (i, 0, 0, 0, 0)))
        out_shape.append(jax.ShapeDtypeStruct((count,) + ends, F32))
    arrays = pl.pallas_call(
        functools.partial(adjoint_prep_kernel, sz, whole, with_rims, field),
        grid_spec=pltpu.PrefetchScalarGridSpec(
            num_scalar_prefetch=1,
            grid=(count,),
            in_specs=in_specs,
            out_specs=out_specs,
            scratch_shapes=[pltpu.VMEM((sz.lane_groups, sz.block_rows + 16, 2 * LANES), F32)],
        ),
        out_shape=out_shape,
        compiler_params=VMEM,
        cost_estimate=COST,
        name="adjoint_prep",
    )(*operands)
    return Pieces(whole, arrays[: len(shapes)]), arrays[len(shapes) :]


def forward_prep_kernel(
    sz, whole, chunk, me_ref, own, other, before, low, high, past, ends, freq, w_ref, *rest
):
    outs, (done, planes, rims) = piece_refs(rest, whole, sz.group)
    done[...] = jnp.zeros_like(done)
    here = me_ref[1]
    body = slice(8, 8 + sz.block_rows)
    for g in range(sz.lane_groups):
        at = pl.ds(g * LANES, LANES)
        for x_ref, station in ((own, here), (other, 1 - here)):
            planes[station, g, body, :] = dot3(join(x_ref.at[0], at), w_ref)
        count = low.shape[0] - 2
        step = count // 2
        inner = here == 0
        row = [before[0, c, 7:8, at] for c in range(2)]
        row = jnp.concatenate(row, axis=1)
        row = jnp.where(inner, join_rows(low, (count,), 1, at), row)
        planes[1, g, 7:8, :] = dot3(row, w_ref)
        row = jnp.where(inner, join_rows(high, (count,), 1, at), join_rows(past, (0,), 1, at))
        planes[1, g, 8 + sz.block_rows : 9 + sz.block_rows, :] = dot3(row, w_ref)
        far_low, far_high = (
            dot3(jnp.concatenate([x_ref[c * step : (c + 1) * step, at] for c in range(2)], 1), w_ref)
            for x_ref in (low, high)
        )
        for i, field in enumerate(chunk):
            for depth in range(2):
                row = 2 * field + 1 - depth
                rims[i, depth, 0, g] = jnp.concatenate(
                    [far_low[row : row + 1], ends[i, 2 + depth, g][:-1]], 0
                )
                row = 2 * field + depth
                rims[i, depth, 1, g] = jnp.concatenate(
                    [ends[i, depth, g][1:], far_high[row : row + 1]], 0
                )
    for k in range(sz.group):
        dest = partner(whole, me_ref[0], k)
        outs[k][:8, :] = freq[...]
        for station in range(2):
            cut_pieces(sz, dest, planes.at[station], outs[k], 8 + station * sz.body)
        place = 8 + 2 * sz.body
        cut_rims(sz, dest, planes.at[1], outs[k], place, 1)
        row = pl.ds(dest, 1)
        for i in range(len(chunk)):
            for depth in range(2):
                place += sz.rims
                rows = [
                    (rims[i, depth, 0, g, row, :], rims[i, depth, 1, g, row, :])
                    for g in range(sz.lane_groups)
                ]
                put_rows(sz, outs[k], place, rows)


def forward_prep(sz, whole, me, forward, other, edges, ends, freq, w, chunk):
    length = (8 + 2 * sz.body + (1 + 2 * len(chunk)) * sz.rims + 7) // 8 * 8
    shapes = Pieces.shapes(whole, sz.group, 1, length)
    rows = (1, 2, sz.block_rows, sz.slots)
    rest = [*edges, ends, freq, w]
    before = sz.block_rows // 8 - 1
    arrays = pl.pallas_call(
        functools.partial(forward_prep_kernel, sz, whole, chunk),
        grid_spec=pltpu.PrefetchScalarGridSpec(
            num_scalar_prefetch=1,
            grid=(1,),
            in_specs=[
                pl.BlockSpec(rows, lambda i, me: (0, 0, me[1], 0)),
                pl.BlockSpec(rows, lambda i, me: (0, 0, 0, 0)),
                pl.BlockSpec((1, 2, 8, sz.slots), lambda i, me: (0, 0, before, 0)),
            ]
            + [pl.BlockSpec(x.shape, lambda i, me, zeros=(0,) * x.ndim: zeros) for x in rest],
            out_specs=Pieces(whole, shapes).specs(sz.group)
            + [pl.BlockSpec((8, LANES), lambda i, me: (0, 0))],
            scratch_shapes=[
                pltpu.VMEM((2, sz.lane_groups, sz.block_rows + 16, 2 * LANES), F32),
                pltpu.VMEM((len(chunk), 2, 2, sz.lane_groups, sz.group, 2 * LANES), F32),
            ],
        ),
        out_shape=shapes + [jax.ShapeDtypeStruct((8, LANES), F32)],
        compiler_params=VMEM,
        cost_estimate=COST,
        name="forward_prep",
    )(me, forward, other, forward, *rest)
    return Pieces(whole, arrays[:-1]), arrays[-1]


def frequency(sz, table_ref, whole, k, j):
    place = k ^ table_ref[sz.group * sz.blocks] if whole else k
    return table_ref[place * sz.blocks + j]


def gather_pieces(sz, table_ref, whole, pieces, state, lead, base=0):
    for k, piece in enumerate(pieces):
        for j in range(sz.blocks):
            freq = frequency(sz, table_ref, whole, k, j)
            for c in range(2):
                at = base + (c * sz.blocks + j) * sz.half
                state[c, freq, lead : lead + sz.half, :] = piece[at : at + sz.half, :]


def lead_first(sz, state, rows, work, out_rows):
    for a in range(8):
        x = [(state[0, a + 8 * b, rows, :], state[1, a + 8 * b, rows, :]) for b in range(8)]
        for t, pair in enumerate(dft8(x, 1)):
            re, im = turned(pair, a * t, 1)
            work[0, 8 * t + a, out_rows, :] = re
            work[1, 8 * t + a, out_rows, :] = im


def lead_second(work, t, rows):
    x = [(work[0, 8 * t + a, rows, :], work[1, 8 * t + a, rows, :]) for a in range(8)]
    return dft8(x, 1)


def couple(sz, state, rows, work, work_rows, phys, phys_rows, store):
    lead_first(sz, state, rows, work, work_rows)
    for t in range(8):
        product = []
        for u, (re, im) in enumerate(lead_second(work, t, work_rows)):
            wr, wi = phys[0, 8 * t + u, phys_rows, :], phys[1, 8 * t + u, phys_rows, :]
            product.append((wr * re + wi * im, wr * im - wi * re))
        for a, pair in enumerate(dft8(product, -1)):
            re, im = turned(pair, a * t, -1)
            work[0, 8 * t + a, work_rows, :] = re
            work[1, 8 * t + a, work_rows, :] = im
    for a in range(8):
        x = [
            (work[0, 8 * t + a, work_rows, :], work[1, 8 * t + a, work_rows, :]) for t in range(8)
        ]
        for b, pair in enumerate(dft8(x, -1)):
            store(a + 8 * b, pair)


def gather_rims(sz, table_ref, whole, pieces, rims, base):
    for k, piece in enumerate(pieces):
        for j in range(sz.blocks):
            freq = frequency(sz, table_ref, whole, k, j)
            for c in range(2):
                at = base + c * sz.blocks + j
                rims[c, pl.ds(freq, 1), :] = piece[at : at + 1, :]


def forward_kernel(sz, whole, chunk, me_ref, *rest):
    pieces, rest = piece_refs(rest, whole, sz.group)
    heads, rest = piece_refs(rest, whole, sz.group)
    out, next_out, rims, table_ref, state, work, next_state, next_work = rest
    count = sz.group * sz.blocks
    for k in range(sz.group):
        place = k ^ me_ref[0] if whole else k
        for j in range(sz.blocks):
            table_ref[place * sz.blocks + j] = heads[k][j, 0].astype(jnp.int32)
    for n in range(4):
        table_ref[count + n] = me_ref[n]
    for station in range(2):
        gather_pieces(sz, table_ref, whole, pieces, state, 0, 8 + station * sz.body)

        @pl.loop(0, sz.tiles)
        def _(s):
            rows = pl.ds(s * sz.tile, sz.tile)
            lead_first(sz, state, rows, work, rows)
            for t in range(8):
                for u, (re, im) in enumerate(lead_second(work, t, rows)):
                    out[station, 0, 8 * t + u, rows, :] = re
                    out[station, 1, 8 * t + u, rows, :] = im

    base = 8 + 2 * sz.body
    gather_rims(sz, table_ref, whole, pieces, rims.at[0, 0], base)
    spread_rims(rims[0, 0].reshape(2 * NF, LANES), next_state, 0)
    rows = slice(0, 8)
    lead_first(sz, next_state, rows, next_work, rows)
    for t in range(8):
        for u, (re, im) in enumerate(lead_second(next_work, t, rows)):
            next_out[0, 8 * t + u] = re[:1]
            next_out[1, 8 * t + u] = im[:1]
    for i in range(chunk):
        for depth in range(2):
            base += sz.rims
            gather_rims(sz, table_ref, whole, pieces, rims.at[i, depth], base)


def forward_physical(sz, me, pieces, chunk):
    full = (2, NF, sz.half, LANES)
    rims = (chunk, 2, 2, NF, LANES)
    if pieces.whole:
        heads = [
            pl.BlockSpec((sz.group, 1, 8, LANES), lambda i, t: (0, 0, 0, 0), memory_space=pltpu.SMEM)
        ]
    else:
        head = pl.BlockSpec((1, 8, LANES), lambda i, t: (0, 0, 0), memory_space=pltpu.SMEM)
        heads = [head] * sz.group
    return pl.pallas_call(
        functools.partial(forward_kernel, sz, pieces.whole, chunk),
        grid_spec=pltpu.PrefetchScalarGridSpec(
            num_scalar_prefetch=1,
            grid=(1,),
            in_specs=pieces.specs(sz.group) + heads,
            out_specs=[
                pl.BlockSpec((2,) + full, lambda i, t: (0, 0, 0, 0, 0)),
                pl.BlockSpec((2, NF, 1, LANES), lambda i, t: (0, 0, 0, 0)),
                pl.BlockSpec(rims, lambda i, t: (0, 0, 0, 0, 0)),
                pl.BlockSpec(memory_space=pltpu.SMEM),
            ],
            scratch_shapes=[
                pltpu.VMEM(full, F32),
                pltpu.VMEM(full, F32),
                pltpu.VMEM((2, NF, 8, LANES), F32),
                pltpu.VMEM((2, NF, 8, LANES), F32),
            ],
        ),
        out_shape=[
            jax.ShapeDtypeStruct((2,) + full, F32),
            jax.ShapeDtypeStruct((2, NF, 1, LANES), F32),
            jax.ShapeDtypeStruct(rims, F32),
            jax.ShapeDtypeStruct((sz.group * sz.blocks + 4,), jnp.int32),
        ],
        compiler_params=VMEM,
        cost_estimate=COST,
        name="forward_physical",
    )(me, *pieces.arrays, *pieces.arrays)


def spread_rims(rims, state, n):
    state.reshape(2 * NF * 8, LANES)[pl.ds(n, 2 * NF, stride=8), :] = rims


def place_edges(sz, state, rims):
    padded = sz.padded
    rows = state.reshape(2 * NF * padded, LANES)
    first = rows[pl.ds(8, 2 * NF, stride=padded), :]
    last = rows[pl.ds(8 + sz.half - 1, 2 * NF, stride=padded), :]
    low = low_half(first.shape)
    rows[pl.ds(7, 2 * NF, stride=padded), :] = jnp.where(low, rims, swap(last))
    rows[pl.ds(8 + sz.half, 2 * NF, stride=padded), :] = jnp.where(low, swap(first), rims)


def advance(sz, state, work, phys, out, lead):
    @pl.loop(0, sz.tiles)
    def _(s):
        rows = pl.ds(8 + s * sz.tile, sz.tile)
        at = pl.ds(s * sz.tile, sz.tile)

        def store(f, pair):
            for c in range(2):
                mid = state[c, f, rows, :]
                up = state[c, f, pl.ds(9 + s * sz.tile, sz.tile), :]
                down = state[c, f, pl.ds(7 + s * sz.tile, sz.tile), :]
                stepped = (1.0 - 2.0 * KAPPA) * mid + KAPPA * (up + down)
                out[c, f, pl.ds(lead + s * sz.tile, sz.tile), :] = (
                    stepped - (COUPLING / NF) * pair[c]
                )

        couple(sz, state, rows, work, at, phys, at, store)


def march_kernel(sz, whole_in, whole_out, row_scale, fields, table_ref, *rest):
    pieces, rest = piece_refs(rest, whole_in, sz.group)
    phys, next_phys, *rest = rest
    running = row_scale is not None
    if running:
        all_rims, rest = rim_refs(rest, whole_in, sz.group)
        pair, pair_rims, start, w_ref, *rest = rest
    else:
        rims_in, w_ref, *rest = rest
    outs, rest = piece_refs(rest, whole_out, sz.group)
    if not running:
        pair_out, pair_rims_out, total_out, *rest = rest
    state, work, middle, stepped, rims, next_state, next_work, next_coupling, sums = rest
    step = pl.program_id(0)
    count = sz.group * sz.blocks

    @pl.when(step == 0)
    def _():
        next_state[...] = jnp.zeros_like(next_state)
        for i in range(fields):
            for depth in range(2):
                if running:
                    views = [ref.at[i] for ref in all_rims]
                    gather_rims(sz, table_ref, whole_in, views, rims.at[i, depth], depth * sz.rims)
                else:
                    rims[i, depth] = rims_in[i, depth]
            spread_rims(rims[i, 0].reshape(2 * NF, LANES), next_state, i)
        rows = slice(0, 8)

        def store(f, pair):
            for c in range(2):
                next_coupling[c, f] = (COUPLING / NF) * pair[c]

        couple(sz, next_state, rows, next_work, rows, next_phys, slice(0, 1), store)

    gather_pieces(sz, table_ref, whole_in, pieces, state, 8)
    near = rims[step, 0].reshape(2 * NF, LANES)
    place_edges(sz, state, near)
    advance(sz, state, work, phys.at[1], middle, 8)

    low = low_half((2 * NF, LANES))
    flat = state.reshape(2 * NF * sz.padded, LANES)
    inner = jnp.where(
        low,
        flat[pl.ds(8, 2 * NF, stride=sz.padded), :],
        flat[pl.ds(8 + sz.half - 1, 2 * NF, stride=sz.padded), :],
    )
    far = rims[step, 1].reshape(2 * NF, LANES)
    coupled = next_coupling.reshape(2 * NF * 8, LANES)[pl.ds(step, 2 * NF, stride=8), :]
    near = (1.0 - 2.0 * KAPPA) * near + KAPPA * (inner + far) - coupled
    rims[step, 0] = near.reshape(2, NF, LANES)
    if running:

        @pl.when(step == fields - 1)
        def _():
            add_running(
                sz, row_scale, middle, rims.at[step, 0], pair, pair_rims, start, w_ref, next_work
            )

    first = table_ref[count + 2].astype(F32)
    last = table_ref[count + 3].astype(F32)
    near = rims[step, 0].reshape(2 * NF, LANES) * jnp.where(low, 1.0 - first, 1.0 - last)
    if not running:

        def sums_of():
            pair_rims_out[0] = near.reshape(2, NF, LANES)
            body = middle[:, :, 8 : 8 + sz.half, :]
            pair_out[0] = body
            value = jnp.sum(body, axis=2)
            return value + swap(value)

        @pl.when(step == 0)
        def _():
            value = sums_of()
            freq = lax.broadcasted_iota(jnp.int32, value.shape, 1)
            rate = 2.0 / NF * ((freq + NF // 2) % NF - NF // 2).astype(F32)
            sums[...] = rate * value

        @pl.when(step == 1)
        def _():
            value = sums_of()
            turned = dot3(jnp.concatenate([value[0], value[1]], axis=1), w_ref)
            re, im = sums[0] + turned[:, :LANES], sums[1] + turned[:, LANES:]
            total = jnp.where(low_half((NF, LANES)), re, im)
            total_out[...] = total

    place_edges(sz, middle, near)
    advance(sz, middle, work, phys.at[0], stepped, 0)
    for k in range(sz.group):
        for j in range(sz.blocks):
            freq = frequency(sz, table_ref, whole_out, k, j)
            for c in range(2):
                at = (c * sz.blocks + j) * sz.half
                outs[k][at : at + sz.half, :] = stepped[c, freq]


def rim_refs(refs, whole, group):
    if whole:
        return [refs[0].at[k] for k in range(group)], refs[1:]
    return list(refs[:group]), refs[group:]


def march(sz, whole_out, table, pieces, phys, next_phys, fields, rims=None, row_scale=None, running=()):
    full = (2, NF, sz.half, LANES)
    shapes = Pieces.shapes(whole_out, sz.group, fields, sz.body)

    def constant(x):
        return pl.BlockSpec(x.shape, lambda i, t, zeros=(0,) * len(x.shape): zeros)

    def by_field(shape):
        return pl.BlockSpec(
            (1,) + shape, lambda i, t, zeros=(0,) * len(shape): (jnp.minimum(i, 1),) + zeros
        )

    body = Pieces(pieces.whole, Pieces.shapes(pieces.whole, sz.group, fields, sz.body))
    in_specs = body.specs(sz.group) + [constant(phys), constant(next_phys)]
    operands = [table, *pieces.arrays, phys, next_phys]
    out_specs, out_shape = Pieces(whole_out, shapes).specs(sz.group), list(shapes)
    if running:
        place = sz.body // (2 * sz.rims)
        if pieces.whole:
            block = (sz.group, fields, 2 * sz.rims, LANES)
            in_specs.append(pl.BlockSpec(block, lambda i, t: (0, 0, place, 0)))
        else:
            block = (fields, 2 * sz.rims, LANES)
            in_specs += [pl.BlockSpec(block, lambda i, t: (0, place, 0))] * sz.group
        in_specs += [constant(x) for x in running]
        operands += [*pieces.arrays, *running]
    else:
        in_specs += [constant(x) for x in rims]
        operands += rims
        for shape in (full, (2, NF, LANES)):
            out_specs.append(by_field(shape))
            out_shape.append(jax.ShapeDtypeStruct((2,) + shape, F32))
        out_shape.append(jax.ShapeDtypeStruct((NF, LANES), F32))
        out_specs.append(constant(out_shape[-1]))
    padded = pltpu.VMEM((2, NF, sz.padded, LANES), F32)
    small = pltpu.VMEM((2, NF, 8, LANES), F32)
    arrays = pl.pallas_call(
        functools.partial(march_kernel, sz, pieces.whole, whole_out, row_scale, fields),
        grid_spec=pltpu.PrefetchScalarGridSpec(
            num_scalar_prefetch=1,
            grid=(fields,),
            in_specs=in_specs,
            out_specs=out_specs,
            scratch_shapes=[
                padded,
                pltpu.VMEM(full, F32),
                padded,
                pltpu.VMEM(full, F32),
                pltpu.VMEM((fields, 2, 2, NF, LANES), F32),
                small,
                small,
                small,
                pltpu.VMEM((2, NF, LANES), F32),
            ],
        ),
        out_shape=out_shape,
        compiler_params=VMEM,
        cost_estimate=COST,
        name="march",
    )(*operands)
    return Pieces(whole_out, arrays[: len(shapes)]), arrays[len(shapes) :]


def running_rows(sz, value, start):
    row = lax.broadcasted_iota(jnp.int32, value.shape, 0)
    reach = 1
    while reach < sz.half:
        value = value + jnp.where(row >= reach, pltpu.roll(value, reach, 0), 0.0)
        reach *= 2
    bottom = jnp.where(low_half((1, LANES)), 0.0, swap(value[sz.half - 1 :]))
    return value + (bottom + start)


def add_running(sz, row_scale, middle, near, pair, pair_rims, start, w_ref, work):
    both = jnp.concatenate([pair[1, 0], pair[1, 1]], axis=2).reshape(NF * sz.half, 2 * LANES)
    turned_two = dot3(both, w_ref)
    turned_rims = dot3(jnp.concatenate([pair_rims[1, 0], pair_rims[1, 1]], axis=1), w_ref)
    low = low_half((1, LANES))
    for f in range(NF):
        at = f * sz.half
        alpha = 2.0 / NF * ((f + NF // 2) % NF - NF // 2)
        spread = start[pl.ds(f, 1), :]
        starts = (jnp.where(low, spread, swap(spread)), jnp.where(low, swap(spread), spread))
        run = []
        for c in range(2):
            lanes = slice(c * LANES, (c + 1) * LANES)
            source = turned_two[at : at + sz.half, lanes] + alpha * pair[0, c, f]
            run.append(running_rows(sz, source, starts[c]))
            past = turned_rims[f : f + 1, lanes] + alpha * pair_rims[0, c, f : f + 1, :]
            work[c, f, 0:1, :] = jnp.where(low, starts[c], run[c][sz.half - 1 :] + past)
        rows = slice(8, 8 + sz.half)
        middle[0, f, rows, :] += row_scale * run[1]
        middle[1, f, rows, :] -= row_scale * run[0]
        near[0, f : f + 1, :] += row_scale * work[1, f, 0:1, :]
        near[1, f : f + 1, :] -= row_scale * work[0, f, 0:1, :]


def join_pieces(sz, whole, me, pieces, planes):
    for k, piece in enumerate(pieces):
        row = pl.multiple_of(partner(whole, me, k) * sz.rows, sz.rows)
        for g in range(sz.lane_groups):
            halves = []
            for c in range(2):
                at = (c * sz.blocks + 2 * g) * sz.half
                even = piece[at : at + sz.half, :]
                odd = piece[at + sz.half : at + 2 * sz.half, :]
                low = low_half(even.shape)
                top = jnp.where(low, even, swap(odd))
                bottom = jnp.where(low, swap(even), odd)
                halves.append(jnp.concatenate([top, bottom], axis=0))
            planes[g, pl.ds(row, sz.rows), :] = jnp.concatenate(halves, axis=1)


def post_kernel(sz, whole, running, row_scale, me_ref, *rest):
    pieces, rest = piece_refs(rest, whole, sz.group)
    w_ref, rest = rest[0], rest[1:]
    if running == "add":
        sums_ref, start_ref, rest = rest[0], rest[1], rest[2:]
    elif running == "make":
        alpha_ref, beta_ref, tri_ref, rest = rest[0], rest[1], rest[2], rest[3:]
        rest, source = rest[:-1], rest[-1]
    planes = rest[-1]
    outs = rest[:-1]
    if running != "make":
        outs = outs[1:]
    out = outs[0]
    join_pieces(sz, whole, me_ref[0], pieces, planes)
    for g in range(sz.lane_groups):
        at = pl.ds(g * LANES, LANES)
        back = dot3(planes[g], w_ref)
        halves = [back[:, :LANES], back[:, LANES:]]
        for c in range(2):
            out[c, 0, :, at] = halves[c]
        if running == "add":

            @pl.when(pl.program_id(0) == pl.num_programs(0) - 1)
            def _():
                sums = [sums_ref[c, :, at] + start_ref[pl.ds(c, 1), at] for c in range(2)]
                out[0, 0, :, at] += row_scale * sums[1]
                out[1, 0, :, at] -= row_scale * sums[0]

        if running == "make":

            @pl.when(pl.program_id(0) == 0)
            def _():
                for c in range(2):
                    source[g, :, c * LANES : (c + 1) * LANES] = halves[c] * alpha_ref[:, at]

            @pl.when(pl.program_id(0) == 1)
            def _():
                both = [
                    source[g, :, c * LANES : (c + 1) * LANES] + halves[c] * beta_ref[:, at]
                    for c in range(2)
                ]
                high, low = split(jnp.concatenate(both, axis=1))
                tri = tri_ref[...]
                total = jnp.dot(tri, low, preferred_element_type=F32)
                total = total + jnp.dot(tri, high, preferred_element_type=F32)
                for c in range(2):
                    outs[1][c, :, at] = total[:, c * LANES : (c + 1) * LANES]
                    outs[2][c : c + 1, at] = total[-1:, c * LANES : (c + 1) * LANES]


def post(sz, row_scale, me, pieces, fields, held, running=None, extra=()):
    count = len(fields)
    field = field_at(fields)
    w = halves_of(complex_lanes(span_matrix(-1) / NK))
    w_spec = pl.BlockSpec((2, 2 * LANES, 2 * LANES), lambda i, me: (0, 0, 0))
    in_specs = pieces.specs(sz.group) + [w_spec]
    row_spec = pl.BlockSpec((1, sz.slots), lambda i, me: (0, 0))
    sums_spec = pl.BlockSpec((2, sz.block_rows, sz.slots), lambda i, me: (0, 0, 0))
    if running == "add":
        in_specs += [sums_spec, pl.BlockSpec((2, sz.slots), lambda i, me: (0, 0))]
    elif running == "make":
        square = pl.BlockSpec((sz.block_rows, sz.block_rows), lambda i, me: (0, 0))
        in_specs += [row_spec, row_spec, square]
    out_specs = [
        pl.BlockSpec((2, 1, sz.block_rows, sz.slots), lambda i, me: (0, field(i), 0, 0))
    ]
    out_shape = [jax.ShapeDtypeStruct((2, 5, sz.block_rows, sz.slots), F32)]
    aliases = {}
    operands = [me, *pieces.arrays, w, *extra]
    plane = pltpu.VMEM((sz.lane_groups, sz.block_rows, 2 * LANES), F32)
    if running == "make":
        out_specs.append(sums_spec)
        out_shape.append(jax.ShapeDtypeStruct((2, sz.block_rows, sz.slots), F32))
        out_specs.append(pl.BlockSpec((2, sz.slots), lambda i, me: (0, 0)))
        out_shape.append(jax.ShapeDtypeStruct((2, sz.slots), F32))
    else:
        in_specs.append(pl.BlockSpec(memory_space=pl.ANY))
        operands.append(held)
        aliases = {len(operands) - 1: 0}
    return pl.pallas_call(
        functools.partial(post_kernel, sz, pieces.whole, running, row_scale),
        grid_spec=pltpu.PrefetchScalarGridSpec(
            num_scalar_prefetch=1,
            grid=(count,),
            in_specs=in_specs,
            out_specs=out_specs,
            scratch_shapes=[plane] * (2 if running == "make" else 1),
        ),
        out_shape=out_shape,
        input_output_aliases=aliases,
        compiler_params=VMEM,
        cost_estimate=COST,
        name="post",
    )(*operands)


def after(value, *earlier):
    return lax.optimization_barrier((value, *earlier))[0]


def edge_kernel(first_ref, last_ref, before, middle, after, token, low, high, past):
    rows = first_ref.shape[1] * 2
    for c in range(2):
        for field in range(first_ref.shape[1]):
            at = c * rows + 2 * field
            low[at : at + 2, :] = last_ref[c, field, 6:8, :]
            high[at : at + 2, :] = first_ref[c, field, 0:2, :]
        at = 2 * rows + c
        low[at : at + 1, :] = after[0, c, 7:8, :]
        high[at : at + 1, :] = middle[0, c, 0:1, :]
        past[c : c + 1, :] = before[0, c, 0:1, :]


def edge_rows(sz, adjoint, forward, after):
    parts, fields = adjoint.shape[:2]
    rows = (parts, fields, 8, sz.slots)
    stored = (1, parts, 8, sz.slots)
    tiles = sz.block_rows // 8
    last = forward.shape[2] // 8 - 1
    count = parts * fields * 2 + parts
    return pl.pallas_call(
        edge_kernel,
        grid=(1,),
        in_specs=[
            pl.BlockSpec(rows, lambda i: (0, 0, 0, 0)),
            pl.BlockSpec(rows, lambda i: (0, 0, tiles - 1, 0)),
            pl.BlockSpec(stored, lambda i: (0, 0, 0, 0)),
            pl.BlockSpec(stored, lambda i: (0, 0, tiles, 0)),
            pl.BlockSpec(stored, lambda i: (0, 0, last, 0)),
            pl.BlockSpec(memory_space=pl.ANY),
        ],
        out_specs=[pl.BlockSpec((n, sz.slots), lambda i: (0, 0)) for n in (count, count, parts)],
        out_shape=[jax.ShapeDtypeStruct((n, sz.slots), F32) for n in (count, count, parts)],
        name="edge_rows",
    )(adjoint, adjoint, forward, forward, forward, after)


def shifted(value, axes, step, count):
    return lax.ppermute(value, axes, [(i, i + step) for i in range(count) if 0 <= i + step < count])


def nearer_sum_by_pairs(value, axis):
    count, mine = lax.axis_size(axis), lax.axis_index(axis)
    other = lax.ppermute(value, axis, [(i, i ^ 1) for i in range(count)])
    before = jnp.where(mine & 1 != 0, other, 0.0)
    both = total = value + other
    for k in range(2, count, 2):
        other = lax.ppermute(both, axis, [(i, i ^ k) for i in range(count)])
        before = before + jnp.where(mine ^ k < mine, other, 0.0)
        total = total + other
    return before, total


def nearer_sum(value):
    blocks = lax.axis_size(ROW_BLOCKS)
    return sum(shifted(value, ROW_BLOCKS, step, blocks) for step in range(1, blocks))


def on_device(adjoint, forward, mode_map):
    sz = Sizes(adjoint.shape[2], adjoint.shape[3])
    stations = lax.axis_size("ckpt")
    row_scale = 1.0 / math.sqrt(sz.block_rows * lax.axis_size("wall") * stations)
    me = lax.axis_index("mode").astype(jnp.int32)
    here = lax.axis_index("ckpt").astype(jnp.int32)
    block, blocks = lax.axis_index(ROW_BLOCKS), lax.axis_size(ROW_BLOCKS)
    is_first = (block == 0) & (me == 0)
    is_last = (block == blocks - 1) & (me == sz.group - 1)
    place = jnp.stack([me, here, is_first.astype(jnp.int32), is_last.astype(jnp.int32)])
    spread = halves_of(complex_lanes(span_matrix(1)))
    chunks = CHUNKS

    other = lax.dynamic_slice_in_dim(forward, (1 - here) * sz.block_rows, sz.block_rows, 2)
    moved = lax.ppermute(other, "ckpt", [(i, stations - 1 - i) for i in range(stations)])

    free = jnp.zeros_like(place) if INWARD[0] else place
    pieces, (ends,) = adjoint_prep(sz, INWARD[0], free, adjoint, spread, chunks[0], spread)
    inward = [pieces.exchange()]

    low, high, past = edge_rows(sz, adjoint, forward, ends)
    low = shifted(low, ROW_BLOCKS, 1, blocks)
    high = shifted(high, ROW_BLOCKS, -1, blocks)
    past = shifted(past, ROW_BLOCKS, -stations, blocks)

    freq_index = lax.div(mode_map, jnp.int32(NK))
    span_index = lax.rem(mode_map, jnp.int32(NK))
    alpha = 2.0 / NF * ((freq_index + NF // 2) % NF - NF // 2).astype(F32)
    beta = 2.0 / NK * ((span_index + NK // 2) % NK - NK // 2).astype(F32)
    freq = freq_index.reshape(sz.blocks, NK)[:, :1].astype(F32)
    freq = jnp.pad(jnp.broadcast_to(freq, (sz.blocks, LANES)), ((0, 8 - sz.blocks), (0, 0)))

    stored, done = forward_prep(
        sz, STORED, place, forward, moved, (low, high, past), ends, freq, spread, chunks[0]
    )
    pieces, _ = adjoint_prep(
        sz, INWARD[1], place, adjoint, spread, chunks[1], done, (low, high)
    )
    stored = stored.exchange(inward[0].arrays if STORED else ())
    got = stored.in_order()
    inward.append(pieces.exchange(got if INWARD[1] else (got + got[-1:] * WINDOW)[WINDOW:]))

    phys, next_phys, rims, table = forward_physical(sz, place, stored, len(chunks[0]))
    turn = halves_of(complex_lanes(beta_matrix()))
    out, (pair, pair_rims, total) = march(
        sz, OUTWARD[0], table, inward[0], phys, next_phys, len(chunks[0]), (rims, turn)
    )
    start, whole = nearer_sum_by_pairs(total, "mode")
    got = inward[1].in_order()
    if OUTWARD[0]:
        back = [out.exchange([whole, *got])]
    else:
        back = [out.exchange([whole] * len(out.arrays))]
    start = start + nearer_sum(whole)
    running = (pair, pair_rims, start, turn)
    out, _ = march(
        sz,
        OUTWARD[1],
        table,
        inward[1],
        phys,
        next_phys,
        len(chunks[1]),
        row_scale=row_scale,
        running=running,
    )
    got = back[0].in_order()
    back.append(out.exchange(got if OUTWARD[1] else (got + got[-1:] * WINDOW)[WINDOW:]))

    tri = jnp.asarray(np.tril(np.ones((sz.block_rows, sz.block_rows))), jnp.bfloat16)
    out, sums, total = post(
        sz, row_scale, place, back[0], chunks[0], None, "make", (alpha[None], beta[None], tri)
    )
    start = nearer_sum(total)
    (out,) = post(sz, row_scale, place, back[1], chunks[1], out, "add", (sums, start))
    return out


def solution(mesh):
    placed = (P(None, None, ROW_BLOCKS, "mode"), P("ckpt", None, "wall", "mode"), P("mode"))
    return jax.shard_map(
        on_device,
        mesh=mesh,
        in_specs=placed,
        out_specs=P(None, None, ROW_BLOCKS, "mode"),
        check_vma=False,
    )
```

```python
import functools
import math

import jax
import jax.numpy as jnp
import numpy as np
from jax import lax
from jax.experimental import pallas as pl
from jax.experimental.pallas import tpu as pltpu
from jax.sharding import PartitionSpec as P

NF = 64
NK = 64
LANES = 2 * NK
KAPPA = 0.2
COUPLING = 0.5
HIGHEST = lax.Precision.HIGHEST
ROW_BLOCKS = ("wall", "ckpt")
VMEM = pltpu.CompilerParams(vmem_limit_bytes=64 * 1024 * 1024)
F32 = jnp.float32
COST = pl.CostEstimate(flops=1, bytes_accessed=1, transcendentals=0)
CHUNKS = ((0, 2, 3), (4, 1))
INWARD = (True, True)
STORED = False
WINDOW = 4
OUTWARD = (True, True)


def complex_lanes(matrix):
    twice = np.kron(np.eye(2), matrix)
    return np.block([[twice.real, twice.imag], [-twice.imag, twice.real]]).astype(np.float32)


def span_matrix(direction):
    ids = np.arange(NK)
    return np.exp(2j * math.pi * direction * (np.outer(ids, ids) % NK) / NK)


def beta_matrix():
    ids = np.arange(NK)
    signed = (ids + NK // 2) % NK - NK // 2
    return span_matrix(-1) @ np.diag(2.0 / NK * signed) @ span_matrix(1) / NK


def split(value):
    high = value.astype(jnp.bfloat16)
    return high, (value - high.astype(F32)).astype(jnp.bfloat16)


def halves_of(matrix):
    high, low = split(jnp.asarray(matrix))
    return jnp.stack([high, low])


def dot3(x, w_ref):
    high, low = split(x)
    dot = functools.partial(jnp.dot, preferred_element_type=F32)
    return (dot(low, w_ref[0]) + dot(high, w_ref[1])) + dot(high, w_ref[0])


def low_half(shape):
    return lax.broadcasted_iota(jnp.int32, shape, len(shape) - 1) < NK


def swap(value):
    return pltpu.roll(value, NK, value.ndim - 1)


def dft4(x, sign):
    (ar, ai), (br, bi), (cr, ci), (dr, di) = x
    pr, pi, mr, mi = ar + cr, ai + ci, ar - cr, ai - ci
    qr, qi, nr, ni = br + dr, bi + di, br - dr, bi - di
    if sign > 0:
        nr, ni = -ni, nr
    else:
        nr, ni = ni, -nr
    return [(pr + qr, pi + qi), (mr + nr, mi + ni), (pr - qr, pi - qi), (mr - nr, mi - ni)]


def dft8(x, sign):
    even = dft4(x[0::2], sign)
    odd = dft4(x[1::2], sign)
    half = math.sqrt(0.5)
    (r1, i1), (r2, i2), (r3, i3) = odd[1], odd[2], odd[3]
    if sign > 0:
        odd[1] = (half * (r1 - i1), half * (i1 + r1))
        odd[2] = (-i2, r2)
        odd[3] = (-half * (r3 + i3), half * (r3 - i3))
    else:
        odd[1] = (half * (r1 + i1), half * (i1 - r1))
        odd[2] = (i2, -r2)
        odd[3] = (half * (i3 - r3), -half * (i3 + r3))
    first = [(a + c, b + d) for (a, b), (c, d) in zip(even, odd)]
    second = [(a - c, b - d) for (a, b), (c, d) in zip(even, odd)]
    return first + second


def turned(pair, power, sign):
    power %= NF
    if power == 0:
        return pair
    angle = 2.0 * math.pi * power / NF
    c, s = math.cos(angle), sign * math.sin(angle)
    re, im = pair
    return (c * re - s * im, c * im + s * re)


class Sizes:
    def __init__(self, rows, slots):
        self.group = lax.axis_size("mode")
        self.block_rows = rows
        self.slots = slots
        self.lane_groups = slots // LANES
        self.blocks = slots // NK
        self.rows = rows // self.group
        self.half = self.rows // 2
        self.tile = min(8, self.half)
        self.tiles = self.half // self.tile
        self.padded = (self.half + 7) // 8 * 8 + 16
        self.body = 2 * self.blocks * self.half
        self.rims = 2 * self.blocks


class Pieces:
    def __init__(self, whole, arrays):
        self.whole, self.arrays = whole, arrays

    def specs(self, group):
        if self.whole:
            length = self.arrays[0].shape[2]
            return [pl.BlockSpec((group, 1, length, LANES), lambda i, *_: (0, i, 0, 0))]
        length = self.arrays[0].shape[1]
        return [pl.BlockSpec((1, length, LANES), lambda i, *_: (i, 0, 0))] * group

    @staticmethod
    def shapes(whole, group, count, length):
        if whole:
            return [jax.ShapeDtypeStruct((group, count, length, LANES), F32)]
        return [jax.ShapeDtypeStruct((count, length, LANES), F32)] * group

    def exchange(self, earlier=()):
        if self.whole:
            array = after(self.arrays[0], *earlier)
            return Pieces(True, [lax.all_to_all(array, "mode", 0, 0, tiled=True)])
        group = len(self.arrays)
        moved = list(self.arrays)
        for n, k in enumerate(partners(group)):
            array = after(moved[k], *earlier[n : n + 1])
            moved[k] = lax.ppermute(array, "mode", [(i, i ^ k) for i in range(group)])
        return Pieces(False, moved)

    def in_order(self):
        if self.whole:
            return list(self.arrays)
        return [self.arrays[k] for k in partners(len(self.arrays))]


def partners(group):
    return sorted(range(1, group), key=lambda k: (-bin(k >> 1).count("1"), k & 1, k))


def field_at(fields):
    return lambda i: sum(jnp.where(i == n, f, 0) for n, f in enumerate(fields))


def piece_refs(refs, whole, group):
    if whole:
        return [refs[0].at[k, 0] for k in range(group)], refs[1:]
    return [ref.at[0] for ref in refs[:group]], refs[group:]


def partner(whole, me, k):
    return k if whole else me ^ k


def pair_rows(top, bottom):
    low = low_half(top.shape)
    return jnp.where(low, top, swap(bottom)), jnp.where(low, swap(top), bottom)


def cut_pieces(sz, dest, planes, out, base=0):
    row = pl.multiple_of(8 + dest * sz.rows, 8)
    for g in range(sz.lane_groups):
        whole = planes[g, pl.ds(row, sz.rows), :]
        for c in range(2):
            part = whole[:, c * LANES : (c + 1) * LANES]
            for odd, value in enumerate(pair_rows(part[: sz.half], part[sz.half :])):
                place = base + (c * sz.blocks + 2 * g + odd) * sz.half
                out[place : place + sz.half, :] = value


def join(x_ref, at):
    return jnp.concatenate([x_ref[c, ..., at].reshape(-1, LANES) for c in range(2)], axis=1)


def join_rows(x_ref, rows, step, at):
    parts = [
        jnp.concatenate([x_ref[pl.ds(r + c * step, 1), :] for r in rows], axis=0) for c in range(2)
    ]
    at = slice(at.start, at.start + at.size)
    return jnp.concatenate([part[:, at] for part in parts], axis=1)


def put_rows(sz, out, place, rows):
    for c in range(2):
        at = slice(c * LANES, (c + 1) * LANES)
        for g, (down, up) in enumerate(rows):
            for odd, value in enumerate(pair_rows(down[:, at], up[:, at])):
                row = place + c * sz.blocks + 2 * g + odd
                out[row : row + 1, :] = value


def cut_rims(sz, dest, planes, out, place, depths):
    for depth in range(depths):
        down = pl.ds(8 - 1 - depth + dest * sz.rows, 1)
        up = pl.ds(8 + depth + (dest + 1) * sz.rows, 1)
        rows = [(planes[g, down, :], planes[g, up, :]) for g in range(sz.lane_groups)]
        put_rows(sz, out, place + depth * sz.rims, rows)


def adjoint_prep_kernel(sz, whole, with_rims, field, me_ref, x_ref, w_ref, *rest):
    _, *rest = rest
    if with_rims:
        low, high, *rest = rest
        outs, (planes,) = piece_refs(rest, whole, sz.group)
    else:
        outs, (ends, planes) = piece_refs(rest, whole, sz.group)
    body = slice(8, 8 + sz.block_rows)
    row = 2 * field(pl.program_id(0))
    groups = [pl.ds(g * LANES, LANES) for g in range(sz.lane_groups)]
    every = [jnp.concatenate([x_ref[c, 0, :, at] for c in range(2)], axis=1) for at in groups]
    every = dot3(jnp.concatenate(every, axis=0), w_ref)
    for g, at in enumerate(groups):
        planes[g, body, :] = every[g * sz.block_rows : (g + 1) * sz.block_rows]
        if with_rims:
            step = low.shape[0] // 2 - 1
            planes[g, 6:8, :] = dot3(join_rows(low, (row, row + 1), step, at), w_ref)
            planes[g, 8 + sz.block_rows : 10 + sz.block_rows, :] = dot3(
                join_rows(high, (row, row + 1), step, at), w_ref
            )
    for k in range(sz.group):
        dest = partner(whole, me_ref[0], k)
        cut_pieces(sz, dest, planes, outs[k])
        if with_rims:
            cut_rims(sz, dest, planes, outs[k], sz.body, 2)
        else:
            for g in range(sz.lane_groups):
                for n, row in enumerate((0, 1, sz.rows - 1, sz.rows - 2)):
                    row = 8 + k * sz.rows + row
                    ends[0, n, g, k : k + 1, :] = planes[g, row : row + 1, :]


def adjoint_prep(sz, whole, me, adjoint, w, fields, after, edges=None):
    count = len(fields)
    field = field_at(fields)
    with_rims = edges is not None
    shapes = Pieces.shapes(whole, sz.group, count, sz.body + (2 * sz.rims if with_rims else 0))
    in_specs = [
        pl.BlockSpec((2, 1, sz.block_rows, sz.slots), lambda i, me: (0, field(i), 0, 0)),
        pl.BlockSpec(w.shape, lambda i, me: (0, 0, 0)),
        pl.BlockSpec(memory_space=pl.ANY),
    ]
    operands = [me, adjoint, w, after]
    out_specs, out_shape = Pieces(whole, shapes).specs(sz.group), list(shapes)
    if with_rims:
        in_specs += [pl.BlockSpec(x.shape, lambda i, me: (0, 0)) for x in edges]
        operands += edges
    else:
        ends = (4, sz.lane_groups, sz.group, 2 * LANES)
        out_specs.append(pl.BlockSpec((1,) + ends, lambda i, me: (i, 0, 0, 0, 0)))
        out_shape.append(jax.ShapeDtypeStruct((count,) + ends, F32))
    arrays = pl.pallas_call(
        functools.partial(adjoint_prep_kernel, sz, whole, with_rims, field),
        grid_spec=pltpu.PrefetchScalarGridSpec(
            num_scalar_prefetch=1,
            grid=(count,),
            in_specs=in_specs,
            out_specs=out_specs,
            scratch_shapes=[pltpu.VMEM((sz.lane_groups, sz.block_rows + 16, 2 * LANES), F32)],
        ),
        out_shape=out_shape,
        compiler_params=VMEM,
        cost_estimate=COST,
        name="adjoint_prep",
    )(*operands)
    return Pieces(whole, arrays[: len(shapes)]), arrays[len(shapes) :]


def forward_prep_kernel(
    sz, whole, chunk, me_ref, own, other, before, low, high, past, ends, freq, w_ref, *rest
):
    outs, (done, planes, rims) = piece_refs(rest, whole, sz.group)
    done[...] = jnp.zeros_like(done)
    here = me_ref[1]
    body = slice(8, 8 + sz.block_rows)
    groups = [pl.ds(g * LANES, LANES) for g in range(sz.lane_groups)]
    for x_ref, station in ((own, here), (other, 1 - here)):
        every = dot3(jnp.concatenate([join(x_ref.at[0], at) for at in groups], axis=0), w_ref)
        for g in range(sz.lane_groups):
            rows = slice(g * sz.block_rows, (g + 1) * sz.block_rows)
            planes[station, g, body, :] = every[rows]
    for g, at in enumerate(groups):
        count = low.shape[0] - 2
        step = count // 2
        inner = here == 0
        row = [before[0, c, 7:8, at] for c in range(2)]
        row = jnp.concatenate(row, axis=1)
        row = jnp.where(inner, join_rows(low, (count,), 1, at), row)
        planes[1, g, 7:8, :] = dot3(row, w_ref)
        row = jnp.where(inner, join_rows(high, (count,), 1, at), join_rows(past, (0,), 1, at))
        planes[1, g, 8 + sz.block_rows : 9 + sz.block_rows, :] = dot3(row, w_ref)
        far_low, far_high = (
            dot3(jnp.concatenate([x_ref[c * step : (c + 1) * step, at] for c in range(2)], 1), w_ref)
            for x_ref in (low, high)
        )
        for i, field in enumerate(chunk):
            for depth in range(2):
                row = 2 * field + 1 - depth
                rims[i, depth, 0, g] = jnp.concatenate(
                    [far_low[row : row + 1], ends[i, 2 + depth, g][:-1]], 0
                )
                row = 2 * field + depth
                rims[i, depth, 1, g] = jnp.concatenate(
                    [ends[i, depth, g][1:], far_high[row : row + 1]], 0
                )
    for k in range(sz.group):
        dest = partner(whole, me_ref[0], k)
        outs[k][:8, :] = freq[...]
        for station in range(2):
            cut_pieces(sz, dest, planes.at[station], outs[k], 8 + station * sz.body)
        place = 8 + 2 * sz.body
        cut_rims(sz, dest, planes.at[1], outs[k], place, 1)
        row = pl.ds(dest, 1)
        for i in range(len(chunk)):
            for depth in range(2):
                place += sz.rims
                rows = [
                    (rims[i, depth, 0, g, row, :], rims[i, depth, 1, g, row, :])
                    for g in range(sz.lane_groups)
                ]
                put_rows(sz, outs[k], place, rows)


def forward_prep(sz, whole, me, forward, other, edges, ends, freq, w, chunk):
    length = (8 + 2 * sz.body + (1 + 2 * len(chunk)) * sz.rims + 7) // 8 * 8
    shapes = Pieces.shapes(whole, sz.group, 1, length)
    rows = (1, 2, sz.block_rows, sz.slots)
    rest = [*edges, ends, freq, w]
    before = sz.block_rows // 8 - 1
    arrays = pl.pallas_call(
        functools.partial(forward_prep_kernel, sz, whole, chunk),
        grid_spec=pltpu.PrefetchScalarGridSpec(
            num_scalar_prefetch=1,
            grid=(1,),
            in_specs=[
                pl.BlockSpec(rows, lambda i, me: (0, 0, me[1], 0)),
                pl.BlockSpec(rows, lambda i, me: (0, 0, 0, 0)),
                pl.BlockSpec((1, 2, 8, sz.slots), lambda i, me: (0, 0, before, 0)),
            ]
            + [pl.BlockSpec(x.shape, lambda i, me, zeros=(0,) * x.ndim: zeros) for x in rest],
            out_specs=Pieces(whole, shapes).specs(sz.group)
            + [pl.BlockSpec((8, LANES), lambda i, me: (0, 0))],
            scratch_shapes=[
                pltpu.VMEM((2, sz.lane_groups, sz.block_rows + 16, 2 * LANES), F32),
                pltpu.VMEM((len(chunk), 2, 2, sz.lane_groups, sz.group, 2 * LANES), F32),
            ],
        ),
        out_shape=shapes + [jax.ShapeDtypeStruct((8, LANES), F32)],
        compiler_params=VMEM,
        cost_estimate=COST,
        name="forward_prep",
    )(me, forward, other, forward, *rest)
    return Pieces(whole, arrays[:-1]), arrays[-1]


def frequency(sz, table_ref, whole, k, j):
    place = k ^ table_ref[sz.group * sz.blocks] if whole else k
    return table_ref[place * sz.blocks + j]


def gather_pieces(sz, table_ref, whole, pieces, state, lead, base=0):
    for k, piece in enumerate(pieces):
        for j in range(sz.blocks):
            freq = frequency(sz, table_ref, whole, k, j)
            for c in range(2):
                at = base + (c * sz.blocks + j) * sz.half
                state[c, freq, lead : lead + sz.half, :] = piece[at : at + sz.half, :]


def lead_first(sz, state, rows, work, out_rows):
    for a in range(8):
        x = [(state[0, a + 8 * b, rows, :], state[1, a + 8 * b, rows, :]) for b in range(8)]
        for t, pair in enumerate(dft8(x, 1)):
            re, im = turned(pair, a * t, 1)
            work[0, 8 * t + a, out_rows, :] = re
            work[1, 8 * t + a, out_rows, :] = im


def lead_second(work, t, rows):
    x = [(work[0, 8 * t + a, rows, :], work[1, 8 * t + a, rows, :]) for a in range(8)]
    return dft8(x, 1)


def couple(sz, state, rows, work, work_rows, phys, phys_rows, store):
    lead_first(sz, state, rows, work, work_rows)
    for t in range(8):
        product = []
        for u, (re, im) in enumerate(lead_second(work, t, work_rows)):
            wr, wi = phys[0, 8 * t + u, phys_rows, :], phys[1, 8 * t + u, phys_rows, :]
            product.append((wr * re + wi * im, wr * im - wi * re))
        for a, pair in enumerate(dft8(product, -1)):
            re, im = turned(pair, a * t, -1)
            work[0, 8 * t + a, work_rows, :] = re
            work[1, 8 * t + a, work_rows, :] = im
    for a in range(8):
        x = [
            (work[0, 8 * t + a, work_rows, :], work[1, 8 * t + a, work_rows, :]) for t in range(8)
        ]
        for b, pair in enumerate(dft8(x, -1)):
            store(a + 8 * b, pair)


def gather_rims(sz, table_ref, whole, pieces, rims, base):
    for k, piece in enumerate(pieces):
        for j in range(sz.blocks):
            freq = frequency(sz, table_ref, whole, k, j)
            for c in range(2):
                at = base + c * sz.blocks + j
                rims[c, pl.ds(freq, 1), :] = piece[at : at + 1, :]


def forward_kernel(sz, whole, chunk, me_ref, *rest):
    pieces, rest = piece_refs(rest, whole, sz.group)
    heads, rest = piece_refs(rest, whole, sz.group)
    out, next_out, rims, table_ref, state, work, next_state, next_work = rest
    count = sz.group * sz.blocks
    for k in range(sz.group):
        place = k ^ me_ref[0] if whole else k
        for j in range(sz.blocks):
            table_ref[place * sz.blocks + j] = heads[k][j, 0].astype(jnp.int32)
    for n in range(4):
        table_ref[count + n] = me_ref[n]
    for station in range(2):
        gather_pieces(sz, table_ref, whole, pieces, state, 0, 8 + station * sz.body)

        @pl.loop(0, sz.tiles)
        def _(s):
            rows = pl.ds(s * sz.tile, sz.tile)
            lead_first(sz, state, rows, work, rows)
            for t in range(8):
                for u, (re, im) in enumerate(lead_second(work, t, rows)):
                    out[station, 0, 8 * t + u, rows, :] = re
                    out[station, 1, 8 * t + u, rows, :] = im

    base = 8 + 2 * sz.body
    gather_rims(sz, table_ref, whole, pieces, rims.at[0, 0], base)
    spread_rims(rims[0, 0].reshape(2 * NF, LANES), next_state, 0)
    rows = slice(0, 8)
    lead_first(sz, next_state, rows, next_work, rows)
    for t in range(8):
        for u, (re, im) in enumerate(lead_second(next_work, t, rows)):
            next_out[0, 8 * t + u] = re[:1]
            next_out[1, 8 * t + u] = im[:1]
    for i in range(chunk):
        for depth in range(2):
            base += sz.rims
            gather_rims(sz, table_ref, whole, pieces, rims.at[i, depth], base)


def forward_physical(sz, me, pieces, chunk):
    full = (2, NF, sz.half, LANES)
    rims = (chunk, 2, 2, NF, LANES)
    if pieces.whole:
        heads = [
            pl.BlockSpec((sz.group, 1, 8, LANES), lambda i, t: (0, 0, 0, 0), memory_space=pltpu.SMEM)
        ]
    else:
        head = pl.BlockSpec((1, 8, LANES), lambda i, t: (0, 0, 0), memory_space=pltpu.SMEM)
        heads = [head] * sz.group
    return pl.pallas_call(
        functools.partial(forward_kernel, sz, pieces.whole, chunk),
        grid_spec=pltpu.PrefetchScalarGridSpec(
            num_scalar_prefetch=1,
            grid=(1,),
            in_specs=pieces.specs(sz.group) + heads,
            out_specs=[
                pl.BlockSpec((2,) + full, lambda i, t: (0, 0, 0, 0, 0)),
                pl.BlockSpec((2, NF, 1, LANES), lambda i, t: (0, 0, 0, 0)),
                pl.BlockSpec(rims, lambda i, t: (0, 0, 0, 0, 0)),
                pl.BlockSpec(memory_space=pltpu.SMEM),
            ],
            scratch_shapes=[
                pltpu.VMEM(full, F32),
                pltpu.VMEM(full, F32),
                pltpu.VMEM((2, NF, 8, LANES), F32),
                pltpu.VMEM((2, NF, 8, LANES), F32),
            ],
        ),
        out_shape=[
            jax.ShapeDtypeStruct((2,) + full, F32),
            jax.ShapeDtypeStruct((2, NF, 1, LANES), F32),
            jax.ShapeDtypeStruct(rims, F32),
            jax.ShapeDtypeStruct((sz.group * sz.blocks + 4,), jnp.int32),
        ],
        compiler_params=VMEM,
        cost_estimate=COST,
        name="forward_physical",
    )(me, *pieces.arrays, *pieces.arrays)


def spread_rims(rims, state, n):
    state.reshape(2 * NF * 8, LANES)[pl.ds(n, 2 * NF, stride=8), :] = rims


def place_edges(sz, state, rims):
    padded = sz.padded
    rows = state.reshape(2 * NF * padded, LANES)
    first = rows[pl.ds(8, 2 * NF, stride=padded), :]
    last = rows[pl.ds(8 + sz.half - 1, 2 * NF, stride=padded), :]
    low = low_half(first.shape)
    rows[pl.ds(7, 2 * NF, stride=padded), :] = jnp.where(low, rims, swap(last))
    rows[pl.ds(8 + sz.half, 2 * NF, stride=padded), :] = jnp.where(low, swap(first), rims)


def advance(sz, state, work, phys, out, lead):
    @pl.loop(0, sz.tiles)
    def _(s):
        rows = pl.ds(8 + s * sz.tile, sz.tile)
        at = pl.ds(s * sz.tile, sz.tile)

        def store(f, pair):
            for c in range(2):
                mid = state[c, f, rows, :]
                up = state[c, f, pl.ds(9 + s * sz.tile, sz.tile), :]
                down = state[c, f, pl.ds(7 + s * sz.tile, sz.tile), :]
                stepped = (1.0 - 2.0 * KAPPA) * mid + KAPPA * (up + down)
                out[c, f, pl.ds(lead + s * sz.tile, sz.tile), :] = (
                    stepped - (COUPLING / NF) * pair[c]
                )

        couple(sz, state, rows, work, at, phys, at, store)


def march_kernel(sz, whole_in, whole_out, row_scale, fields, table_ref, *rest):
    pieces, rest = piece_refs(rest, whole_in, sz.group)
    phys, next_phys, *rest = rest
    running = row_scale is not None
    if running:
        all_rims, rest = rim_refs(rest, whole_in, sz.group)
        pair, pair_rims, start, w_ref, *rest = rest
    else:
        rims_in, w_ref, *rest = rest
    outs, rest = piece_refs(rest, whole_out, sz.group)
    if not running:
        pair_out, pair_rims_out, total_out, *rest = rest
    state, work, middle, stepped, rims, next_state, next_work, next_coupling, sums = rest
    step = pl.program_id(0)
    count = sz.group * sz.blocks

    @pl.when(step == 0)
    def _():
        next_state[...] = jnp.zeros_like(next_state)
        for i in range(fields):
            for depth in range(2):
                if running:
                    views = [ref.at[i] for ref in all_rims]
                    gather_rims(sz, table_ref, whole_in, views, rims.at[i, depth], depth * sz.rims)
                else:
                    rims[i, depth] = rims_in[i, depth]
            spread_rims(rims[i, 0].reshape(2 * NF, LANES), next_state, i)
        rows = slice(0, 8)

        def store(f, pair):
            for c in range(2):
                next_coupling[c, f] = (COUPLING / NF) * pair[c]

        couple(sz, next_state, rows, next_work, rows, next_phys, slice(0, 1), store)

    gather_pieces(sz, table_ref, whole_in, pieces, state, 8)
    near = rims[step, 0].reshape(2 * NF, LANES)
    place_edges(sz, state, near)
    advance(sz, state, work, phys.at[1], middle, 8)

    low = low_half((2 * NF, LANES))
    flat = state.reshape(2 * NF * sz.padded, LANES)
    inner = jnp.where(
        low,
        flat[pl.ds(8, 2 * NF, stride=sz.padded), :],
        flat[pl.ds(8 + sz.half - 1, 2 * NF, stride=sz.padded), :],
    )
    far = rims[step, 1].reshape(2 * NF, LANES)
    coupled = next_coupling.reshape(2 * NF * 8, LANES)[pl.ds(step, 2 * NF, stride=8), :]
    near = (1.0 - 2.0 * KAPPA) * near + KAPPA * (inner + far) - coupled
    rims[step, 0] = near.reshape(2, NF, LANES)
    if running:

        @pl.when(step == fields - 1)
        def _():
            add_running(
                sz, row_scale, middle, rims.at[step, 0], pair, pair_rims, start, w_ref, next_work
            )

    first = table_ref[count + 2].astype(F32)
    last = table_ref[count + 3].astype(F32)
    near = rims[step, 0].reshape(2 * NF, LANES) * jnp.where(low, 1.0 - first, 1.0 - last)
    if not running:

        def sums_of():
            pair_rims_out[0] = near.reshape(2, NF, LANES)
            body = middle[:, :, 8 : 8 + sz.half, :]
            pair_out[0] = body
            value = jnp.sum(body, axis=2)
            return value + swap(value)

        @pl.when(step == 0)
        def _():
            value = sums_of()
            freq = lax.broadcasted_iota(jnp.int32, value.shape, 1)
            rate = 2.0 / NF * ((freq + NF // 2) % NF - NF // 2).astype(F32)
            sums[...] = rate * value

        @pl.when(step == 1)
        def _():
            value = sums_of()
            turned = dot3(jnp.concatenate([value[0], value[1]], axis=1), w_ref)
            re, im = sums[0] + turned[:, :LANES], sums[1] + turned[:, LANES:]
            total = jnp.where(low_half((NF, LANES)), re, im)
            total_out[...] = total

    place_edges(sz, middle, near)
    advance(sz, middle, work, phys.at[0], stepped, 0)
    for k in range(sz.group):
        for j in range(sz.blocks):
            freq = frequency(sz, table_ref, whole_out, k, j)
            for c in range(2):
                at = (c * sz.blocks + j) * sz.half
                outs[k][at : at + sz.half, :] = stepped[c, freq]


def rim_refs(refs, whole, group):
    if whole:
        return [refs[0].at[k] for k in range(group)], refs[1:]
    return list(refs[:group]), refs[group:]


def march(sz, whole_out, table, pieces, phys, next_phys, fields, rims=None, row_scale=None, running=()):
    full = (2, NF, sz.half, LANES)
    shapes = Pieces.shapes(whole_out, sz.group, fields, sz.body)

    def constant(x):
        return pl.BlockSpec(x.shape, lambda i, t, zeros=(0,) * len(x.shape): zeros)

    def by_field(shape):
        return pl.BlockSpec(
            (1,) + shape, lambda i, t, zeros=(0,) * len(shape): (jnp.minimum(i, 1),) + zeros
        )

    body = Pieces(pieces.whole, Pieces.shapes(pieces.whole, sz.group, fields, sz.body))
    in_specs = body.specs(sz.group) + [constant(phys), constant(next_phys)]
    operands = [table, *pieces.arrays, phys, next_phys]
    out_specs, out_shape = Pieces(whole_out, shapes).specs(sz.group), list(shapes)
    if running:
        place = sz.body // (2 * sz.rims)
        if pieces.whole:
            block = (sz.group, fields, 2 * sz.rims, LANES)
            in_specs.append(pl.BlockSpec(block, lambda i, t: (0, 0, place, 0)))
        else:
            block = (fields, 2 * sz.rims, LANES)
            in_specs += [pl.BlockSpec(block, lambda i, t: (0, place, 0))] * sz.group
        in_specs += [constant(x) for x in running]
        operands += [*pieces.arrays, *running]
    else:
        in_specs += [constant(x) for x in rims]
        operands += rims
        for shape in (full, (2, NF, LANES)):
            out_specs.append(by_field(shape))
            out_shape.append(jax.ShapeDtypeStruct((2,) + shape, F32))
        out_shape.append(jax.ShapeDtypeStruct((NF, LANES), F32))
        out_specs.append(constant(out_shape[-1]))
    padded = pltpu.VMEM((2, NF, sz.padded, LANES), F32)
    small = pltpu.VMEM((2, NF, 8, LANES), F32)
    arrays = pl.pallas_call(
        functools.partial(march_kernel, sz, pieces.whole, whole_out, row_scale, fields),
        grid_spec=pltpu.PrefetchScalarGridSpec(
            num_scalar_prefetch=1,
            grid=(fields,),
            in_specs=in_specs,
            out_specs=out_specs,
            scratch_shapes=[
                padded,
                pltpu.VMEM(full, F32),
                padded,
                pltpu.VMEM(full, F32),
                pltpu.VMEM((fields, 2, 2, NF, LANES), F32),
                small,
                small,
                small,
                pltpu.VMEM((2, NF, LANES), F32),
            ],
        ),
        out_shape=out_shape,
        compiler_params=VMEM,
        cost_estimate=COST,
        name="march",
    )(*operands)
    return Pieces(whole_out, arrays[: len(shapes)]), arrays[len(shapes) :]


def running_rows(sz, value, start):
    row = lax.broadcasted_iota(jnp.int32, value.shape, 0)
    reach = 1
    while reach < sz.half:
        value = value + jnp.where(row >= reach, pltpu.roll(value, reach, 0), 0.0)
        reach *= 2
    bottom = jnp.where(low_half((1, LANES)), 0.0, swap(value[sz.half - 1 :]))
    return value + (bottom + start)


def add_running(sz, row_scale, middle, near, pair, pair_rims, start, w_ref, work):
    both = jnp.concatenate([pair[1, 0], pair[1, 1]], axis=2).reshape(NF * sz.half, 2 * LANES)
    turned_two = dot3(both, w_ref)
    turned_rims = dot3(jnp.concatenate([pair_rims[1, 0], pair_rims[1, 1]], axis=1), w_ref)
    low = low_half((1, LANES))
    for f in range(NF):
        at = f * sz.half
        alpha = 2.0 / NF * ((f + NF // 2) % NF - NF // 2)
        spread = start[pl.ds(f, 1), :]
        starts = (jnp.where(low, spread, swap(spread)), jnp.where(low, swap(spread), spread))
        run = []
        for c in range(2):
            lanes = slice(c * LANES, (c + 1) * LANES)
            source = turned_two[at : at + sz.half, lanes] + alpha * pair[0, c, f]
            run.append(running_rows(sz, source, starts[c]))
            past = turned_rims[f : f + 1, lanes] + alpha * pair_rims[0, c, f : f + 1, :]
            work[c, f, 0:1, :] = jnp.where(low, starts[c], run[c][sz.half - 1 :] + past)
        rows = slice(8, 8 + sz.half)
        middle[0, f, rows, :] += row_scale * run[1]
        middle[1, f, rows, :] -= row_scale * run[0]
        near[0, f : f + 1, :] += row_scale * work[1, f, 0:1, :]
        near[1, f : f + 1, :] -= row_scale * work[0, f, 0:1, :]


def join_pieces(sz, whole, me, pieces, planes):
    for k, piece in enumerate(pieces):
        row = pl.multiple_of(partner(whole, me, k) * sz.rows, sz.rows)
        for g in range(sz.lane_groups):
            halves = []
            for c in range(2):
                at = (c * sz.blocks + 2 * g) * sz.half
                even = piece[at : at + sz.half, :]
                odd = piece[at + sz.half : at + 2 * sz.half, :]
                low = low_half(even.shape)
                top = jnp.where(low, even, swap(odd))
                bottom = jnp.where(low, swap(even), odd)
                halves.append(jnp.concatenate([top, bottom], axis=0))
            planes[g, pl.ds(row, sz.rows), :] = jnp.concatenate(halves, axis=1)


def post_kernel(sz, whole, running, row_scale, me_ref, *rest):
    pieces, rest = piece_refs(rest, whole, sz.group)
    w_ref, rest = rest[0], rest[1:]
    if running == "add":
        sums_ref, start_ref, rest = rest[0], rest[1], rest[2:]
    elif running == "make":
        alpha_ref, beta_ref, tri_ref, rest = rest[0], rest[1], rest[2], rest[3:]
        rest, source = rest[:-1], rest[-1]
    planes = rest[-1]
    outs = rest[:-1]
    if running != "make":
        outs = outs[1:]
    out = outs[0]
    join_pieces(sz, whole, me_ref[0], pieces, planes)
    every = dot3(planes[...].reshape(-1, 2 * LANES), w_ref)
    for g in range(sz.lane_groups):
        at = pl.ds(g * LANES, LANES)
        back = every[g * sz.block_rows : (g + 1) * sz.block_rows]
        halves = [back[:, :LANES], back[:, LANES:]]
        for c in range(2):
            out[c, 0, :, at] = halves[c]
        if running == "add":

            @pl.when(pl.program_id(0) == pl.num_programs(0) - 1)
            def _():
                sums = [sums_ref[c, :, at] + start_ref[pl.ds(c, 1), at] for c in range(2)]
                out[0, 0, :, at] += row_scale * sums[1]
                out[1, 0, :, at] -= row_scale * sums[0]

        if running == "make":

            @pl.when(pl.program_id(0) == 0)
            def _():
                for c in range(2):
                    source[g, :, c * LANES : (c + 1) * LANES] = halves[c] * alpha_ref[:, at]

            @pl.when(pl.program_id(0) == 1)
            def _():
                both = [
                    source[g, :, c * LANES : (c + 1) * LANES] + halves[c] * beta_ref[:, at]
                    for c in range(2)
                ]
                high, low = split(jnp.concatenate(both, axis=1))
                tri = tri_ref[...]
                total = jnp.dot(tri, low, preferred_element_type=F32)
                total = total + jnp.dot(tri, high, preferred_element_type=F32)
                for c in range(2):
                    outs[1][c, :, at] = total[:, c * LANES : (c + 1) * LANES]
                    outs[2][c : c + 1, at] = total[-1:, c * LANES : (c + 1) * LANES]


def post(sz, row_scale, me, pieces, fields, held, running=None, extra=()):
    count = len(fields)
    field = field_at(fields)
    w = halves_of(complex_lanes(span_matrix(-1) / NK))
    w_spec = pl.BlockSpec((2, 2 * LANES, 2 * LANES), lambda i, me: (0, 0, 0))
    in_specs = pieces.specs(sz.group) + [w_spec]
    row_spec = pl.BlockSpec((1, sz.slots), lambda i, me: (0, 0))
    sums_spec = pl.BlockSpec((2, sz.block_rows, sz.slots), lambda i, me: (0, 0, 0))
    if running == "add":
        in_specs += [sums_spec, pl.BlockSpec((2, sz.slots), lambda i, me: (0, 0))]
    elif running == "make":
        square = pl.BlockSpec((sz.block_rows, sz.block_rows), lambda i, me: (0, 0))
        in_specs += [row_spec, row_spec, square]
    out_specs = [
        pl.BlockSpec((2, 1, sz.block_rows, sz.slots), lambda i, me: (0, field(i), 0, 0))
    ]
    out_shape = [jax.ShapeDtypeStruct((2, 5, sz.block_rows, sz.slots), F32)]
    aliases = {}
    operands = [me, *pieces.arrays, w, *extra]
    plane = pltpu.VMEM((sz.lane_groups, sz.block_rows, 2 * LANES), F32)
    if running == "make":
        out_specs.append(sums_spec)
        out_shape.append(jax.ShapeDtypeStruct((2, sz.block_rows, sz.slots), F32))
        out_specs.append(pl.BlockSpec((2, sz.slots), lambda i, me: (0, 0)))
        out_shape.append(jax.ShapeDtypeStruct((2, sz.slots), F32))
    else:
        in_specs.append(pl.BlockSpec(memory_space=pl.ANY))
        operands.append(held)
        aliases = {len(operands) - 1: 0}
    return pl.pallas_call(
        functools.partial(post_kernel, sz, pieces.whole, running, row_scale),
        grid_spec=pltpu.PrefetchScalarGridSpec(
            num_scalar_prefetch=1,
            grid=(count,),
            in_specs=in_specs,
            out_specs=out_specs,
            scratch_shapes=[plane] * (2 if running == "make" else 1),
        ),
        out_shape=out_shape,
        input_output_aliases=aliases,
        compiler_params=VMEM,
        cost_estimate=COST,
        name="post",
    )(*operands)


def after(value, *earlier):
    return lax.optimization_barrier((value, *earlier))[0]


def edge_kernel(first_ref, last_ref, before, middle, after, token, low, high, past):
    rows = first_ref.shape[1] * 2
    for c in range(2):
        for field in range(first_ref.shape[1]):
            at = c * rows + 2 * field
            low[at : at + 2, :] = last_ref[c, field, 6:8, :]
            high[at : at + 2, :] = first_ref[c, field, 0:2, :]
        at = 2 * rows + c
        low[at : at + 1, :] = after[0, c, 7:8, :]
        high[at : at + 1, :] = middle[0, c, 0:1, :]
        past[c : c + 1, :] = before[0, c, 0:1, :]


def edge_rows(sz, adjoint, forward, after):
    parts, fields = adjoint.shape[:2]
    rows = (parts, fields, 8, sz.slots)
    stored = (1, parts, 8, sz.slots)
    tiles = sz.block_rows // 8
    last = forward.shape[2] // 8 - 1
    count = parts * fields * 2 + parts
    return pl.pallas_call(
        edge_kernel,
        grid=(1,),
        in_specs=[
            pl.BlockSpec(rows, lambda i: (0, 0, 0, 0)),
            pl.BlockSpec(rows, lambda i: (0, 0, tiles - 1, 0)),
            pl.BlockSpec(stored, lambda i: (0, 0, 0, 0)),
            pl.BlockSpec(stored, lambda i: (0, 0, tiles, 0)),
            pl.BlockSpec(stored, lambda i: (0, 0, last, 0)),
            pl.BlockSpec(memory_space=pl.ANY),
        ],
        out_specs=[pl.BlockSpec((n, sz.slots), lambda i: (0, 0)) for n in (count, count, parts)],
        out_shape=[jax.ShapeDtypeStruct((n, sz.slots), F32) for n in (count, count, parts)],
        name="edge_rows",
    )(adjoint, adjoint, forward, forward, forward, after)


def shifted(value, axes, step, count):
    return lax.ppermute(value, axes, [(i, i + step) for i in range(count) if 0 <= i + step < count])


def nearer_sum_by_pairs(value, axis):
    count, mine = lax.axis_size(axis), lax.axis_index(axis)
    other = lax.ppermute(value, axis, [(i, i ^ 1) for i in range(count)])
    before = jnp.where(mine & 1 != 0, other, 0.0)
    both = total = value + other
    for k in range(2, count, 2):
        other = lax.ppermute(both, axis, [(i, i ^ k) for i in range(count)])
        before = before + jnp.where(mine ^ k < mine, other, 0.0)
        total = total + other
    return before, total


def nearer_sum(value):
    blocks = lax.axis_size(ROW_BLOCKS)
    return sum(shifted(value, ROW_BLOCKS, step, blocks) for step in range(1, blocks))


def on_device(adjoint, forward, mode_map):
    sz = Sizes(adjoint.shape[2], adjoint.shape[3])
    stations = lax.axis_size("ckpt")
    row_scale = 1.0 / math.sqrt(sz.block_rows * lax.axis_size("wall") * stations)
    me = lax.axis_index("mode").astype(jnp.int32)
    here = lax.axis_index("ckpt").astype(jnp.int32)
    block, blocks = lax.axis_index(ROW_BLOCKS), lax.axis_size(ROW_BLOCKS)
    is_first = (block == 0) & (me == 0)
    is_last = (block == blocks - 1) & (me == sz.group - 1)
    place = jnp.stack([me, here, is_first.astype(jnp.int32), is_last.astype(jnp.int32)])
    spread = halves_of(complex_lanes(span_matrix(1)))
    chunks = CHUNKS

    other = lax.dynamic_slice_in_dim(forward, (1 - here) * sz.block_rows, sz.block_rows, 2)
    moved = lax.ppermute(other, "ckpt", [(i, stations - 1 - i) for i in range(stations)])

    free = jnp.asarray(np.arange(4, dtype=np.int32)) if INWARD[0] else place
    pieces, (ends,) = adjoint_prep(sz, INWARD[0], free, adjoint, spread, chunks[0], spread)
    inward = [pieces.exchange()]

    low, high, past = edge_rows(sz, adjoint, forward, ends)
    low = shifted(low, ROW_BLOCKS, 1, blocks)
    high = shifted(high, ROW_BLOCKS, -1, blocks)
    past = shifted(past, ROW_BLOCKS, -stations, blocks)

    freq_index = lax.div(mode_map, jnp.int32(NK))
    span_index = lax.rem(mode_map, jnp.int32(NK))
    alpha = 2.0 / NF * ((freq_index + NF // 2) % NF - NF // 2).astype(F32)
    beta = 2.0 / NK * ((span_index + NK // 2) % NK - NK // 2).astype(F32)
    freq = freq_index.reshape(sz.blocks, NK)[:, :1].astype(F32)
    freq = jnp.pad(jnp.broadcast_to(freq, (sz.blocks, LANES)), ((0, 8 - sz.blocks), (0, 0)))

    stored, done = forward_prep(
        sz, STORED, place, forward, moved, (low, high, past), ends, freq, spread, chunks[0]
    )
    pieces, _ = adjoint_prep(
        sz, INWARD[1], place, adjoint, spread, chunks[1], done, (low, high)
    )
    stored = stored.exchange(inward[0].arrays if STORED else ())
    got = stored.in_order()
    inward.append(pieces.exchange(got if INWARD[1] else (got + got[-1:] * WINDOW)[WINDOW:]))

    phys, next_phys, rims, table = forward_physical(sz, place, stored, len(chunks[0]))
    turn = halves_of(complex_lanes(beta_matrix()))
    out, (pair, pair_rims, total) = march(
        sz, OUTWARD[0], table, inward[0], phys, next_phys, len(chunks[0]), (rims, turn)
    )
    start, whole = nearer_sum_by_pairs(total, "mode")
    got = inward[1].in_order()
    if OUTWARD[0]:
        back = [out.exchange([whole, *got])]
    else:
        back = [out.exchange([whole] * len(out.arrays))]
    start = start + nearer_sum(whole)
    running = (pair, pair_rims, start, turn)
    out, _ = march(
        sz,
        OUTWARD[1],
        table,
        inward[1],
        phys,
        next_phys,
        len(chunks[1]),
        row_scale=row_scale,
        running=running,
    )
    got = back[0].in_order()
    back.append(out.exchange(got if OUTWARD[1] else (got + got[-1:] * WINDOW)[WINDOW:]))

    tri = jnp.asarray(np.tril(np.ones((sz.block_rows, sz.block_rows))), jnp.bfloat16)
    out, sums, total = post(
        sz, row_scale, place, back[0], chunks[0], None, "make", (alpha[None], beta[None], tri)
    )
    start = nearer_sum(total)
    (out,) = post(sz, row_scale, place, back[1], chunks[1], out, "add", (sums, start))
    return out


def solution(mesh):
    placed = (P(None, None, ROW_BLOCKS, "mode"), P("ckpt", None, "wall", "mode"), P("mode"))
    return jax.shard_map(
        on_device,
        mesh=mesh,
        in_specs=placed,
        out_specs=P(None, None, ROW_BLOCKS, "mode"),
        check_vma=False,
    )
```

```python
import functools
import math

import jax
import jax.numpy as jnp
import numpy as np
from jax import lax
from jax.experimental import pallas as pl
from jax.experimental.pallas import tpu as pltpu
from jax.sharding import PartitionSpec as P

NF = 64
NK = 64
LANES = 2 * NK
KAPPA = 0.2
COUPLING = 0.5
HIGHEST = lax.Precision.HIGHEST
ROW_BLOCKS = ("wall", "ckpt")
VMEM = pltpu.CompilerParams(vmem_limit_bytes=64 * 1024 * 1024)
F32 = jnp.float32
COST = pl.CostEstimate(flops=1, bytes_accessed=1, transcendentals=0)
CHUNKS = ((0, 2, 3), (4, 1))
INWARD = (True, True)
STORED = False
WINDOW = 4
OUTWARD = (True, True)


def complex_lanes(matrix):
    twice = np.kron(np.eye(2), matrix)
    return np.block([[twice.real, twice.imag], [-twice.imag, twice.real]]).astype(np.float32)


def span_matrix(direction):
    ids = np.arange(NK)
    return np.exp(2j * math.pi * direction * (np.outer(ids, ids) % NK) / NK)


def beta_matrix():
    ids = np.arange(NK)
    signed = (ids + NK // 2) % NK - NK // 2
    return span_matrix(-1) @ np.diag(2.0 / NK * signed) @ span_matrix(1) / NK


def split(value):
    high = value.astype(jnp.bfloat16)
    return high, (value - high.astype(F32)).astype(jnp.bfloat16)


def halves_of(matrix):
    high, low = split(jnp.asarray(matrix))
    return jnp.stack([high, low])


def dot3(x, w_ref):
    high, low = split(x)
    dot = functools.partial(jnp.dot, preferred_element_type=F32)
    return (dot(low, w_ref[0]) + dot(high, w_ref[1])) + dot(high, w_ref[0])


def low_half(shape):
    return lax.broadcasted_iota(jnp.int32, shape, len(shape) - 1) < NK


def swap(value):
    return pltpu.roll(value, NK, value.ndim - 1)


def dft4(x, sign):
    (ar, ai), (br, bi), (cr, ci), (dr, di) = x
    pr, pi, mr, mi = ar + cr, ai + ci, ar - cr, ai - ci
    qr, qi, nr, ni = br + dr, bi + di, br - dr, bi - di
    if sign > 0:
        nr, ni = -ni, nr
    else:
        nr, ni = ni, -nr
    return [(pr + qr, pi + qi), (mr + nr, mi + ni), (pr - qr, pi - qi), (mr - nr, mi - ni)]


def dft8(x, sign):
    even = dft4(x[0::2], sign)
    odd = dft4(x[1::2], sign)
    half = math.sqrt(0.5)
    (r1, i1), (r2, i2), (r3, i3) = odd[1], odd[2], odd[3]
    if sign > 0:
        odd[1] = (half * (r1 - i1), half * (i1 + r1))
        odd[2] = (-i2, r2)
        odd[3] = (-half * (r3 + i3), half * (r3 - i3))
    else:
        odd[1] = (half * (r1 + i1), half * (i1 - r1))
        odd[2] = (i2, -r2)
        odd[3] = (half * (i3 - r3), -half * (i3 + r3))
    first = [(a + c, b + d) for (a, b), (c, d) in zip(even, odd)]
    second = [(a - c, b - d) for (a, b), (c, d) in zip(even, odd)]
    return first + second


def turned(pair, power, sign):
    power %= NF
    if power == 0:
        return pair
    angle = 2.0 * math.pi * power / NF
    c, s = math.cos(angle), sign * math.sin(angle)
    re, im = pair
    return (c * re - s * im, c * im + s * re)


class Sizes:
    def __init__(self, rows, slots):
        self.group = lax.axis_size("mode")
        self.block_rows = rows
        self.slots = slots
        self.lane_groups = slots // LANES
        self.blocks = slots // NK
        self.rows = rows // self.group
        self.half = self.rows // 2
        self.tile = min(8, self.half)
        self.tiles = self.half // self.tile
        self.padded = (self.half + 7) // 8 * 8 + 16
        self.body = 2 * self.blocks * self.half
        self.rims = 2 * self.blocks


class Pieces:
    def __init__(self, whole, arrays):
        self.whole, self.arrays = whole, arrays

    def specs(self, group):
        if self.whole:
            length = self.arrays[0].shape[2]
            return [pl.BlockSpec((group, 1, length, LANES), lambda i, *_: (0, i, 0, 0))]
        length = self.arrays[0].shape[1]
        return [pl.BlockSpec((1, length, LANES), lambda i, *_: (i, 0, 0))] * group

    @staticmethod
    def shapes(whole, group, count, length):
        if whole:
            return [jax.ShapeDtypeStruct((group, count, length, LANES), F32)]
        return [jax.ShapeDtypeStruct((count, length, LANES), F32)] * group

    def exchange(self, earlier=()):
        if self.whole:
            array = after(self.arrays[0], *earlier)
            return Pieces(True, [lax.all_to_all(array, "mode", 0, 0, tiled=True)])
        group = len(self.arrays)
        moved = list(self.arrays)
        for n, k in enumerate(partners(group)):
            array = after(moved[k], *earlier[n : n + 1])
            moved[k] = lax.ppermute(array, "mode", [(i, i ^ k) for i in range(group)])
        return Pieces(False, moved)

    def in_order(self):
        if self.whole:
            return list(self.arrays)
        return [self.arrays[k] for k in partners(len(self.arrays))]


def partners(group):
    return sorted(range(1, group), key=lambda k: (-bin(k >> 1).count("1"), k & 1, k))


def field_at(fields):
    return lambda i: sum(jnp.where(i == n, f, 0) for n, f in enumerate(fields))


def piece_refs(refs, whole, group):
    if whole:
        return [refs[0].at[k, 0] for k in range(group)], refs[1:]
    return [ref.at[0] for ref in refs[:group]], refs[group:]


def partner(whole, me, k):
    return k if whole else me ^ k


def pair_rows(top, bottom):
    low = low_half(top.shape)
    return jnp.where(low, top, swap(bottom)), jnp.where(low, swap(top), bottom)


def cut_pieces(sz, dest, planes, out, base=0):
    row = pl.multiple_of(8 + dest * sz.rows, 8)
    for g in range(sz.lane_groups):
        whole = planes[g, pl.ds(row, sz.rows), :]
        for c in range(2):
            part = whole[:, c * LANES : (c + 1) * LANES]
            for odd, value in enumerate(pair_rows(part[: sz.half], part[sz.half :])):
                place = base + (c * sz.blocks + 2 * g + odd) * sz.half
                out[place : place + sz.half, :] = value


def join(x_ref, at):
    return jnp.concatenate([x_ref[c, ..., at].reshape(-1, LANES) for c in range(2)], axis=1)


def join_rows(x_ref, rows, step, at):
    parts = [
        jnp.concatenate([x_ref[pl.ds(r + c * step, 1), :] for r in rows], axis=0) for c in range(2)
    ]
    at = slice(at.start, at.start + at.size)
    return jnp.concatenate([part[:, at] for part in parts], axis=1)


def put_rows(sz, out, place, rows):
    for c in range(2):
        at = slice(c * LANES, (c + 1) * LANES)
        for g, (down, up) in enumerate(rows):
            for odd, value in enumerate(pair_rows(down[:, at], up[:, at])):
                row = place + c * sz.blocks + 2 * g + odd
                out[row : row + 1, :] = value


def cut_rims(sz, dest, planes, out, place, depths):
    for depth in range(depths):
        down = pl.ds(8 - 1 - depth + dest * sz.rows, 1)
        up = pl.ds(8 + depth + (dest + 1) * sz.rows, 1)
        rows = [(planes[g, down, :], planes[g, up, :]) for g in range(sz.lane_groups)]
        put_rows(sz, out, place + depth * sz.rims, rows)


def adjoint_prep_kernel(sz, whole, with_rims, field, me_ref, x_ref, w_ref, *rest):
    _, *rest = rest
    if with_rims:
        low, high, *rest = rest
        outs, (planes,) = piece_refs(rest, whole, sz.group)
    else:
        outs, (ends, planes) = piece_refs(rest, whole, sz.group)
    body = slice(8, 8 + sz.block_rows)
    row = 2 * field(pl.program_id(0))
    groups = [pl.ds(g * LANES, LANES) for g in range(sz.lane_groups)]
    every = [jnp.concatenate([x_ref[c, 0, :, at] for c in range(2)], axis=1) for at in groups]
    every = jnp.concatenate(every, axis=0)
    if with_rims:
        every = dot3(every, w_ref)
    for g, at in enumerate(groups):
        planes[g, body, :] = every[g * sz.block_rows : (g + 1) * sz.block_rows]
        if with_rims:
            step = low.shape[0] // 2 - 1
            planes[g, 6:8, :] = dot3(join_rows(low, (row, row + 1), step, at), w_ref)
            planes[g, 8 + sz.block_rows : 10 + sz.block_rows, :] = dot3(
                join_rows(high, (row, row + 1), step, at), w_ref
            )
    for k in range(sz.group):
        dest = partner(whole, me_ref[0], k)
        cut_pieces(sz, dest, planes, outs[k])
        if with_rims:
            cut_rims(sz, dest, planes, outs[k], sz.body, 2)
        else:
            for g in range(sz.lane_groups):
                for n, row in enumerate((0, 1, sz.rows - 1, sz.rows - 2)):
                    row = 8 + k * sz.rows + row
                    ends[0, n, g, k : k + 1, :] = planes[g, row : row + 1, :]


def adjoint_prep(sz, whole, me, adjoint, w, fields, after, edges=None):
    count = len(fields)
    field = field_at(fields)
    with_rims = edges is not None
    shapes = Pieces.shapes(whole, sz.group, count, sz.body + (2 * sz.rims if with_rims else 0))
    in_specs = [
        pl.BlockSpec((2, 1, sz.block_rows, sz.slots), lambda i, me: (0, field(i), 0, 0)),
        pl.BlockSpec(w.shape, lambda i, me: (0, 0, 0)),
        pl.BlockSpec(memory_space=pl.ANY),
    ]
    operands = [me, adjoint, w, after]
    out_specs, out_shape = Pieces(whole, shapes).specs(sz.group), list(shapes)
    if with_rims:
        in_specs += [pl.BlockSpec(x.shape, lambda i, me: (0, 0)) for x in edges]
        operands += edges
    else:
        ends = (4, sz.lane_groups, sz.group, 2 * LANES)
        out_specs.append(pl.BlockSpec((1,) + ends, lambda i, me: (i, 0, 0, 0, 0)))
        out_shape.append(jax.ShapeDtypeStruct((count,) + ends, F32))
    arrays = pl.pallas_call(
        functools.partial(adjoint_prep_kernel, sz, whole, with_rims, field),
        grid_spec=pltpu.PrefetchScalarGridSpec(
            num_scalar_prefetch=1,
            grid=(count,),
            in_specs=in_specs,
            out_specs=out_specs,
            scratch_shapes=[pltpu.VMEM((sz.lane_groups, sz.block_rows + 16, 2 * LANES), F32)],
        ),
        out_shape=out_shape,
        compiler_params=VMEM,
        cost_estimate=COST,
        name="adjoint_prep",
    )(*operands)
    return Pieces(whole, arrays[: len(shapes)]), arrays[len(shapes) :]


def forward_prep_kernel(
    sz, whole, chunk, me_ref, own, other, before, low, high, past, ends, freq, w_ref, *rest
):
    outs, (done, planes, rims) = piece_refs(rest, whole, sz.group)
    done[...] = jnp.zeros_like(done)
    here = me_ref[1]
    body = slice(8, 8 + sz.block_rows)
    groups = [pl.ds(g * LANES, LANES) for g in range(sz.lane_groups)]
    for x_ref, station in ((own, here), (other, 1 - here)):
        every = dot3(jnp.concatenate([join(x_ref.at[0], at) for at in groups], axis=0), w_ref)
        for g in range(sz.lane_groups):
            rows = slice(g * sz.block_rows, (g + 1) * sz.block_rows)
            planes[station, g, body, :] = every[rows]
    for g, at in enumerate(groups):
        count = low.shape[0] - 2
        step = count // 2
        inner = here == 0
        row = [before[0, c, 7:8, at] for c in range(2)]
        row = jnp.concatenate(row, axis=1)
        row = jnp.where(inner, join_rows(low, (count,), 1, at), row)
        planes[1, g, 7:8, :] = dot3(row, w_ref)
        row = jnp.where(inner, join_rows(high, (count,), 1, at), join_rows(past, (0,), 1, at))
        planes[1, g, 8 + sz.block_rows : 9 + sz.block_rows, :] = dot3(row, w_ref)
        far_low, far_high = (
            jnp.concatenate([x_ref[c * step : (c + 1) * step, at] for c in range(2)], 1)
            for x_ref in (low, high)
        )
        for i, field in enumerate(chunk):
            for depth in range(2):
                row = 2 * field + 1 - depth
                rims[i, depth, 0, g] = jnp.concatenate(
                    [far_low[row : row + 1], ends[i, 2 + depth, g][:-1]], 0
                )
                row = 2 * field + depth
                rims[i, depth, 1, g] = jnp.concatenate(
                    [ends[i, depth, g][1:], far_high[row : row + 1]], 0
                )
    for k in range(sz.group):
        dest = partner(whole, me_ref[0], k)
        outs[k][:8, :] = freq[...]
        for station in range(2):
            cut_pieces(sz, dest, planes.at[station], outs[k], 8 + station * sz.body)
        place = 8 + 2 * sz.body
        cut_rims(sz, dest, planes.at[1], outs[k], place, 1)
        row = pl.ds(dest, 1)
        for i in range(len(chunk)):
            for depth in range(2):
                place += sz.rims
                rows = [
                    (rims[i, depth, 0, g, row, :], rims[i, depth, 1, g, row, :])
                    for g in range(sz.lane_groups)
                ]
                put_rows(sz, outs[k], place, rows)


def forward_prep(sz, whole, me, forward, other, edges, ends, freq, w, chunk):
    length = (8 + 2 * sz.body + (1 + 2 * len(chunk)) * sz.rims + 7) // 8 * 8
    shapes = Pieces.shapes(whole, sz.group, 1, length)
    rows = (1, 2, sz.block_rows, sz.slots)
    rest = [*edges, ends, freq, w]
    before = sz.block_rows // 8 - 1
    arrays = pl.pallas_call(
        functools.partial(forward_prep_kernel, sz, whole, chunk),
        grid_spec=pltpu.PrefetchScalarGridSpec(
            num_scalar_prefetch=1,
            grid=(1,),
            in_specs=[
                pl.BlockSpec(rows, lambda i, me: (0, 0, me[1], 0)),
                pl.BlockSpec(rows, lambda i, me: (0, 0, 0, 0)),
                pl.BlockSpec((1, 2, 8, sz.slots), lambda i, me: (0, 0, before, 0)),
            ]
            + [pl.BlockSpec(x.shape, lambda i, me, zeros=(0,) * x.ndim: zeros) for x in rest],
            out_specs=Pieces(whole, shapes).specs(sz.group)
            + [pl.BlockSpec((8, LANES), lambda i, me: (0, 0))],
            scratch_shapes=[
                pltpu.VMEM((2, sz.lane_groups, sz.block_rows + 16, 2 * LANES), F32),
                pltpu.VMEM((len(chunk), 2, 2, sz.lane_groups, sz.group, 2 * LANES), F32),
            ],
        ),
        out_shape=shapes + [jax.ShapeDtypeStruct((8, LANES), F32)],
        compiler_params=VMEM,
        cost_estimate=COST,
        name="forward_prep",
    )(me, forward, other, forward, *rest)
    return Pieces(whole, arrays[:-1]), arrays[-1]


def frequency(sz, table_ref, whole, k, j):
    place = k ^ table_ref[sz.group * sz.blocks] if whole else k
    return table_ref[place * sz.blocks + j]


def gather_pieces(sz, table_ref, whole, pieces, state, lead, base=0):
    for k, piece in enumerate(pieces):
        for j in range(sz.blocks):
            freq = frequency(sz, table_ref, whole, k, j)
            for c in range(2):
                at = base + (c * sz.blocks + j) * sz.half
                state[c, freq, lead : lead + sz.half, :] = piece[at : at + sz.half, :]


def lead_first(sz, state, rows, work, out_rows):
    for a in range(8):
        x = [(state[0, a + 8 * b, rows, :], state[1, a + 8 * b, rows, :]) for b in range(8)]
        for t, pair in enumerate(dft8(x, 1)):
            re, im = turned(pair, a * t, 1)
            work[0, 8 * t + a, out_rows, :] = re
            work[1, 8 * t + a, out_rows, :] = im


def lead_second(work, t, rows):
    x = [(work[0, 8 * t + a, rows, :], work[1, 8 * t + a, rows, :]) for a in range(8)]
    return dft8(x, 1)


def couple(sz, state, rows, work, work_rows, phys, phys_rows, store):
    lead_first(sz, state, rows, work, work_rows)
    for t in range(8):
        product = []
        for u, (re, im) in enumerate(lead_second(work, t, work_rows)):
            wr, wi = phys[0, 8 * t + u, phys_rows, :], phys[1, 8 * t + u, phys_rows, :]
            product.append((wr * re + wi * im, wr * im - wi * re))
        for a, pair in enumerate(dft8(product, -1)):
            re, im = turned(pair, a * t, -1)
            work[0, 8 * t + a, work_rows, :] = re
            work[1, 8 * t + a, work_rows, :] = im
    for a in range(8):
        x = [
            (work[0, 8 * t + a, work_rows, :], work[1, 8 * t + a, work_rows, :]) for t in range(8)
        ]
        for b, pair in enumerate(dft8(x, -1)):
            store(a + 8 * b, pair)


def gather_rims(sz, table_ref, whole, pieces, rims, base):
    for k, piece in enumerate(pieces):
        for j in range(sz.blocks):
            freq = frequency(sz, table_ref, whole, k, j)
            for c in range(2):
                at = base + c * sz.blocks + j
                rims[c, pl.ds(freq, 1), :] = piece[at : at + 1, :]


def forward_kernel(sz, whole, chunk, me_ref, *rest):
    pieces, rest = piece_refs(rest, whole, sz.group)
    heads, rest = piece_refs(rest, whole, sz.group)
    w_ref, out, next_out, rims, table_ref, state, work, next_state, next_work = rest
    count = sz.group * sz.blocks
    for k in range(sz.group):
        place = k ^ me_ref[0] if whole else k
        for j in range(sz.blocks):
            table_ref[place * sz.blocks + j] = heads[k][j, 0].astype(jnp.int32)
    for n in range(4):
        table_ref[count + n] = me_ref[n]
    for station in range(2):
        gather_pieces(sz, table_ref, whole, pieces, state, 0, 8 + station * sz.body)

        @pl.loop(0, sz.tiles)
        def _(s):
            rows = pl.ds(s * sz.tile, sz.tile)
            lead_first(sz, state, rows, work, rows)
            for t in range(8):
                for u, (re, im) in enumerate(lead_second(work, t, rows)):
                    out[station, 0, 8 * t + u, rows, :] = re
                    out[station, 1, 8 * t + u, rows, :] = im

    base = 8 + 2 * sz.body
    gather_rims(sz, table_ref, whole, pieces, rims.at[0, 0], base)
    spread_rims(rims[0, 0].reshape(2 * NF, LANES), next_state, 0)
    rows = slice(0, 8)
    lead_first(sz, next_state, rows, next_work, rows)
    for t in range(8):
        for u, (re, im) in enumerate(lead_second(next_work, t, rows)):
            next_out[0, 8 * t + u] = re[:1]
            next_out[1, 8 * t + u] = im[:1]
    for i in range(chunk):
        for depth in range(2):
            base += sz.rims
            gather_rims(sz, table_ref, whole, pieces, rims.at[i, depth], base)
            every = dot3(jnp.concatenate([rims[i, depth, 0], rims[i, depth, 1]], axis=1), w_ref)
            for c in range(2):
                rims[i, depth, c] = every[:, c * LANES : (c + 1) * LANES]


def forward_physical(sz, me, pieces, chunk, w):
    full = (2, NF, sz.half, LANES)
    rims = (chunk, 2, 2, NF, LANES)
    if pieces.whole:
        heads = [
            pl.BlockSpec((sz.group, 1, 8, LANES), lambda i, t: (0, 0, 0, 0), memory_space=pltpu.SMEM)
        ]
    else:
        head = pl.BlockSpec((1, 8, LANES), lambda i, t: (0, 0, 0), memory_space=pltpu.SMEM)
        heads = [head] * sz.group
    return pl.pallas_call(
        functools.partial(forward_kernel, sz, pieces.whole, chunk),
        grid_spec=pltpu.PrefetchScalarGridSpec(
            num_scalar_prefetch=1,
            grid=(1,),
            in_specs=pieces.specs(sz.group)
            + heads
            + [pl.BlockSpec(w.shape, lambda i, t: (0, 0, 0))],
            out_specs=[
                pl.BlockSpec((2,) + full, lambda i, t: (0, 0, 0, 0, 0)),
                pl.BlockSpec((2, NF, 1, LANES), lambda i, t: (0, 0, 0, 0)),
                pl.BlockSpec(rims, lambda i, t: (0, 0, 0, 0, 0)),
                pl.BlockSpec(memory_space=pltpu.SMEM),
            ],
            scratch_shapes=[
                pltpu.VMEM(full, F32),
                pltpu.VMEM(full, F32),
                pltpu.VMEM((2, NF, 8, LANES), F32),
                pltpu.VMEM((2, NF, 8, LANES), F32),
            ],
        ),
        out_shape=[
            jax.ShapeDtypeStruct((2,) + full, F32),
            jax.ShapeDtypeStruct((2, NF, 1, LANES), F32),
            jax.ShapeDtypeStruct(rims, F32),
            jax.ShapeDtypeStruct((sz.group * sz.blocks + 4,), jnp.int32),
        ],
        compiler_params=VMEM,
        cost_estimate=COST,
        name="forward_physical",
    )(me, *pieces.arrays, *pieces.arrays, w)


def spread_rims(rims, state, n):
    state.reshape(2 * NF * 8, LANES)[pl.ds(n, 2 * NF, stride=8), :] = rims


def place_edges(sz, state, rims):
    padded = sz.padded
    rows = state.reshape(2 * NF * padded, LANES)
    first = rows[pl.ds(8, 2 * NF, stride=padded), :]
    last = rows[pl.ds(8 + sz.half - 1, 2 * NF, stride=padded), :]
    low = low_half(first.shape)
    rows[pl.ds(7, 2 * NF, stride=padded), :] = jnp.where(low, rims, swap(last))
    rows[pl.ds(8 + sz.half, 2 * NF, stride=padded), :] = jnp.where(low, swap(first), rims)


def advance(sz, state, work, phys, out, lead):
    @pl.loop(0, sz.tiles)
    def _(s):
        rows = pl.ds(8 + s * sz.tile, sz.tile)
        at = pl.ds(s * sz.tile, sz.tile)

        def store(f, pair):
            for c in range(2):
                mid = state[c, f, rows, :]
                up = state[c, f, pl.ds(9 + s * sz.tile, sz.tile), :]
                down = state[c, f, pl.ds(7 + s * sz.tile, sz.tile), :]
                stepped = (1.0 - 2.0 * KAPPA) * mid + KAPPA * (up + down)
                out[c, f, pl.ds(lead + s * sz.tile, sz.tile), :] = (
                    stepped - (COUPLING / NF) * pair[c]
                )

        couple(sz, state, rows, work, at, phys, at, store)


def march_kernel(sz, whole_in, whole_out, row_scale, fields, table_ref, *rest):
    pieces, rest = piece_refs(rest, whole_in, sz.group)
    phys, next_phys, *rest = rest
    running = row_scale is not None
    if running:
        all_rims, rest = rim_refs(rest, whole_in, sz.group)
        pair, pair_rims, start, w_ref, back_ref, *rest = rest
    else:
        rims_in, w_ref, spread_ref, *rest = rest
    outs, rest = piece_refs(rest, whole_out, sz.group)
    if not running:
        pair_out, pair_rims_out, total_out, *rest = rest
    state, work, middle, stepped, rims, next_state, next_work, next_coupling, sums = rest
    step = pl.program_id(0)
    count = sz.group * sz.blocks

    @pl.when(step == 0)
    def _():
        next_state[...] = jnp.zeros_like(next_state)
        for i in range(fields):
            for depth in range(2):
                if running:
                    views = [ref.at[i] for ref in all_rims]
                    gather_rims(sz, table_ref, whole_in, views, rims.at[i, depth], depth * sz.rims)
                else:
                    rims[i, depth] = rims_in[i, depth]
            spread_rims(rims[i, 0].reshape(2 * NF, LANES), next_state, i)
        rows = slice(0, 8)

        def store(f, pair):
            for c in range(2):
                next_coupling[c, f] = (COUPLING / NF) * pair[c]

        couple(sz, next_state, rows, next_work, rows, next_phys, slice(0, 1), store)

    gather_pieces(sz, table_ref, whole_in, pieces, state, 8)
    body = slice(8, 8 + sz.half)
    if not running:
        both = jnp.concatenate([state[0, :, body, :], state[1, :, body, :]], axis=2)
        both = dot3(both.reshape(NF * sz.half, 2 * LANES), spread_ref)
        for c in range(2):
            lanes = slice(c * LANES, (c + 1) * LANES)
            state[c, :, body, :] = both[:, lanes].reshape(NF, sz.half, LANES)
    near = rims[step, 0].reshape(2 * NF, LANES)
    place_edges(sz, state, near)
    advance(sz, state, work, phys.at[1], middle, 8)

    low = low_half((2 * NF, LANES))
    flat = state.reshape(2 * NF * sz.padded, LANES)
    inner = jnp.where(
        low,
        flat[pl.ds(8, 2 * NF, stride=sz.padded), :],
        flat[pl.ds(8 + sz.half - 1, 2 * NF, stride=sz.padded), :],
    )
    far = rims[step, 1].reshape(2 * NF, LANES)
    coupled = next_coupling.reshape(2 * NF * 8, LANES)[pl.ds(step, 2 * NF, stride=8), :]
    near = (1.0 - 2.0 * KAPPA) * near + KAPPA * (inner + far) - coupled
    rims[step, 0] = near.reshape(2, NF, LANES)
    if running:

        @pl.when(step == fields - 1)
        def _():
            add_running(
                sz, row_scale, middle, rims.at[step, 0], pair, pair_rims, start, w_ref, next_work
            )

    first = table_ref[count + 2].astype(F32)
    last = table_ref[count + 3].astype(F32)
    near = rims[step, 0].reshape(2 * NF, LANES) * jnp.where(low, 1.0 - first, 1.0 - last)
    if not running:

        def sums_of():
            pair_rims_out[0] = near.reshape(2, NF, LANES)
            rows = middle[:, :, body, :]
            pair_out[0] = rows
            value = jnp.sum(rows, axis=2)
            return value + swap(value)

        @pl.when(step == 0)
        def _():
            value = sums_of()
            freq = lax.broadcasted_iota(jnp.int32, value.shape, 1)
            rate = 2.0 / NF * ((freq + NF // 2) % NF - NF // 2).astype(F32)
            sums[...] = rate * value

        @pl.when(step == 1)
        def _():
            value = sums_of()
            turned = dot3(jnp.concatenate([value[0], value[1]], axis=1), w_ref)
            re, im = sums[0] + turned[:, :LANES], sums[1] + turned[:, LANES:]
            total = jnp.where(low_half((NF, LANES)), re, im)
            total_out[...] = total

    place_edges(sz, middle, near)
    advance(sz, middle, work, phys.at[0], stepped, 0)
    if running:
        both = jnp.concatenate([stepped[0], stepped[1]], axis=2).reshape(NF * sz.half, 2 * LANES)
        both = dot3(both, back_ref)
        for c in range(2):
            stepped[c] = both[:, c * LANES : (c + 1) * LANES].reshape(NF, sz.half, LANES)
    for k in range(sz.group):
        for j in range(sz.blocks):
            freq = frequency(sz, table_ref, whole_out, k, j)
            for c in range(2):
                at = (c * sz.blocks + j) * sz.half
                outs[k][at : at + sz.half, :] = stepped[c, freq]


def rim_refs(refs, whole, group):
    if whole:
        return [refs[0].at[k] for k in range(group)], refs[1:]
    return list(refs[:group]), refs[group:]


def march(sz, whole_out, table, pieces, phys, next_phys, fields, rims=None, row_scale=None, running=()):
    full = (2, NF, sz.half, LANES)
    shapes = Pieces.shapes(whole_out, sz.group, fields, sz.body)

    def constant(x):
        return pl.BlockSpec(x.shape, lambda i, t, zeros=(0,) * len(x.shape): zeros)

    def by_field(shape):
        return pl.BlockSpec(
            (1,) + shape, lambda i, t, zeros=(0,) * len(shape): (jnp.minimum(i, 1),) + zeros
        )

    body = Pieces(pieces.whole, Pieces.shapes(pieces.whole, sz.group, fields, sz.body))
    in_specs = body.specs(sz.group) + [constant(phys), constant(next_phys)]
    operands = [table, *pieces.arrays, phys, next_phys]
    out_specs, out_shape = Pieces(whole_out, shapes).specs(sz.group), list(shapes)
    if running:
        place = sz.body // (2 * sz.rims)
        if pieces.whole:
            block = (sz.group, fields, 2 * sz.rims, LANES)
            in_specs.append(pl.BlockSpec(block, lambda i, t: (0, 0, place, 0)))
        else:
            block = (fields, 2 * sz.rims, LANES)
            in_specs += [pl.BlockSpec(block, lambda i, t: (0, place, 0))] * sz.group
        in_specs += [constant(x) for x in running]
        operands += [*pieces.arrays, *running]
    else:
        in_specs += [constant(x) for x in rims]
        operands += rims
        for shape in (full, (2, NF, LANES)):
            out_specs.append(by_field(shape))
            out_shape.append(jax.ShapeDtypeStruct((2,) + shape, F32))
        out_shape.append(jax.ShapeDtypeStruct((NF, LANES), F32))
        out_specs.append(constant(out_shape[-1]))
    padded = pltpu.VMEM((2, NF, sz.padded, LANES), F32)
    small = pltpu.VMEM((2, NF, 8, LANES), F32)
    arrays = pl.pallas_call(
        functools.partial(march_kernel, sz, pieces.whole, whole_out, row_scale, fields),
        grid_spec=pltpu.PrefetchScalarGridSpec(
            num_scalar_prefetch=1,
            grid=(fields,),
            in_specs=in_specs,
            out_specs=out_specs,
            scratch_shapes=[
                padded,
                pltpu.VMEM(full, F32),
                padded,
                pltpu.VMEM(full, F32),
                pltpu.VMEM((fields, 2, 2, NF, LANES), F32),
                small,
                small,
                small,
                pltpu.VMEM((2, NF, LANES), F32),
            ],
        ),
        out_shape=out_shape,
        compiler_params=VMEM,
        cost_estimate=COST,
        name="march",
    )(*operands)
    return Pieces(whole_out, arrays[: len(shapes)]), arrays[len(shapes) :]


def running_rows(sz, value, start):
    row = lax.broadcasted_iota(jnp.int32, value.shape, 0)
    reach = 1
    while reach < sz.half:
        value = value + jnp.where(row >= reach, pltpu.roll(value, reach, 0), 0.0)
        reach *= 2
    bottom = jnp.where(low_half((1, LANES)), 0.0, swap(value[sz.half - 1 :]))
    return value + (bottom + start)


def add_running(sz, row_scale, middle, near, pair, pair_rims, start, w_ref, work):
    both = jnp.concatenate([pair[1, 0], pair[1, 1]], axis=2).reshape(NF * sz.half, 2 * LANES)
    turned_two = dot3(both, w_ref)
    turned_rims = dot3(jnp.concatenate([pair_rims[1, 0], pair_rims[1, 1]], axis=1), w_ref)
    low = low_half((1, LANES))
    for f in range(NF):
        at = f * sz.half
        alpha = 2.0 / NF * ((f + NF // 2) % NF - NF // 2)
        spread = start[pl.ds(f, 1), :]
        starts = (jnp.where(low, spread, swap(spread)), jnp.where(low, swap(spread), spread))
        run = []
        for c in range(2):
            lanes = slice(c * LANES, (c + 1) * LANES)
            source = turned_two[at : at + sz.half, lanes] + alpha * pair[0, c, f]
            run.append(running_rows(sz, source, starts[c]))
            past = turned_rims[f : f + 1, lanes] + alpha * pair_rims[0, c, f : f + 1, :]
            work[c, f, 0:1, :] = jnp.where(low, starts[c], run[c][sz.half - 1 :] + past)
        rows = slice(8, 8 + sz.half)
        middle[0, f, rows, :] += row_scale * run[1]
        middle[1, f, rows, :] -= row_scale * run[0]
        near[0, f : f + 1, :] += row_scale * work[1, f, 0:1, :]
        near[1, f : f + 1, :] -= row_scale * work[0, f, 0:1, :]


def join_pieces(sz, whole, me, pieces, planes):
    for k, piece in enumerate(pieces):
        row = pl.multiple_of(partner(whole, me, k) * sz.rows, sz.rows)
        for g in range(sz.lane_groups):
            halves = []
            for c in range(2):
                at = (c * sz.blocks + 2 * g) * sz.half
                even = piece[at : at + sz.half, :]
                odd = piece[at + sz.half : at + 2 * sz.half, :]
                low = low_half(even.shape)
                top = jnp.where(low, even, swap(odd))
                bottom = jnp.where(low, swap(even), odd)
                halves.append(jnp.concatenate([top, bottom], axis=0))
            planes[g, pl.ds(row, sz.rows), :] = jnp.concatenate(halves, axis=1)


def post_kernel(sz, whole, running, row_scale, me_ref, *rest):
    pieces, rest = piece_refs(rest, whole, sz.group)
    if running != "add":
        w_ref, rest = rest[0], rest[1:]
    if running == "add":
        sums_ref, start_ref, rest = rest[0], rest[1], rest[2:]
    elif running == "make":
        alpha_ref, beta_ref, tri_ref, rest = rest[0], rest[1], rest[2], rest[3:]
        rest, source = rest[:-1], rest[-1]
    planes = rest[-1]
    outs = rest[:-1]
    if running != "make":
        outs = outs[1:]
    out = outs[0]
    join_pieces(sz, whole, me_ref[0], pieces, planes)
    every = planes[...].reshape(-1, 2 * LANES)
    if running != "add":
        every = dot3(every, w_ref)
    for g in range(sz.lane_groups):
        at = pl.ds(g * LANES, LANES)
        back = every[g * sz.block_rows : (g + 1) * sz.block_rows]
        halves = [back[:, :LANES], back[:, LANES:]]
        for c in range(2):
            out[c, 0, :, at] = halves[c]
        if running == "add":

            @pl.when(pl.program_id(0) == pl.num_programs(0) - 1)
            def _():
                sums = [sums_ref[c, :, at] + start_ref[pl.ds(c, 1), at] for c in range(2)]
                out[0, 0, :, at] += row_scale * sums[1]
                out[1, 0, :, at] -= row_scale * sums[0]

        if running == "make":

            @pl.when(pl.program_id(0) == 0)
            def _():
                for c in range(2):
                    source[g, :, c * LANES : (c + 1) * LANES] = halves[c] * alpha_ref[:, at]

            @pl.when(pl.program_id(0) == 1)
            def _():
                both = [
                    source[g, :, c * LANES : (c + 1) * LANES] + halves[c] * beta_ref[:, at]
                    for c in range(2)
                ]
                high, low = split(jnp.concatenate(both, axis=1))
                tri = tri_ref[...]
                total = jnp.dot(tri, low, preferred_element_type=F32)
                total = total + jnp.dot(tri, high, preferred_element_type=F32)
                for c in range(2):
                    outs[1][c, :, at] = total[:, c * LANES : (c + 1) * LANES]
                    outs[2][c : c + 1, at] = total[-1:, c * LANES : (c + 1) * LANES]


def post(sz, row_scale, me, pieces, fields, held, running=None, extra=()):
    count = len(fields)
    field = field_at(fields)
    w = halves_of(complex_lanes(span_matrix(-1) / NK))
    w_spec = pl.BlockSpec((2, 2 * LANES, 2 * LANES), lambda i, me: (0, 0, 0))
    in_specs = pieces.specs(sz.group) + [w_spec] * (running != "add")
    row_spec = pl.BlockSpec((1, sz.slots), lambda i, me: (0, 0))
    sums_spec = pl.BlockSpec((2, sz.block_rows, sz.slots), lambda i, me: (0, 0, 0))
    if running == "add":
        in_specs += [sums_spec, pl.BlockSpec((2, sz.slots), lambda i, me: (0, 0))]
    elif running == "make":
        square = pl.BlockSpec((sz.block_rows, sz.block_rows), lambda i, me: (0, 0))
        in_specs += [row_spec, row_spec, square]
    out_specs = [
        pl.BlockSpec((2, 1, sz.block_rows, sz.slots), lambda i, me: (0, field(i), 0, 0))
    ]
    out_shape = [jax.ShapeDtypeStruct((2, 5, sz.block_rows, sz.slots), F32)]
    aliases = {}
    operands = [me, *pieces.arrays, *([] if running == "add" else [w]), *extra]
    plane = pltpu.VMEM((sz.lane_groups, sz.block_rows, 2 * LANES), F32)
    if running == "make":
        out_specs.append(sums_spec)
        out_shape.append(jax.ShapeDtypeStruct((2, sz.block_rows, sz.slots), F32))
        out_specs.append(pl.BlockSpec((2, sz.slots), lambda i, me: (0, 0)))
        out_shape.append(jax.ShapeDtypeStruct((2, sz.slots), F32))
    else:
        in_specs.append(pl.BlockSpec(memory_space=pl.ANY))
        operands.append(held)
        aliases = {len(operands) - 1: 0}
    return pl.pallas_call(
        functools.partial(post_kernel, sz, pieces.whole, running, row_scale),
        grid_spec=pltpu.PrefetchScalarGridSpec(
            num_scalar_prefetch=1,
            grid=(count,),
            in_specs=in_specs,
            out_specs=out_specs,
            scratch_shapes=[plane] * (2 if running == "make" else 1),
        ),
        out_shape=out_shape,
        input_output_aliases=aliases,
        compiler_params=VMEM,
        cost_estimate=COST,
        name="post",
    )(*operands)


def after(value, *earlier):
    return lax.optimization_barrier((value, *earlier))[0]


def edge_kernel(first_ref, last_ref, before, middle, after, token, low, high, past):
    rows = first_ref.shape[1] * 2
    for c in range(2):
        for field in range(first_ref.shape[1]):
            at = c * rows + 2 * field
            low[at : at + 2, :] = last_ref[c, field, 6:8, :]
            high[at : at + 2, :] = first_ref[c, field, 0:2, :]
        at = 2 * rows + c
        low[at : at + 1, :] = after[0, c, 7:8, :]
        high[at : at + 1, :] = middle[0, c, 0:1, :]
        past[c : c + 1, :] = before[0, c, 0:1, :]


def edge_rows(sz, adjoint, forward, after):
    parts, fields = adjoint.shape[:2]
    rows = (parts, fields, 8, sz.slots)
    stored = (1, parts, 8, sz.slots)
    tiles = sz.block_rows // 8
    last = forward.shape[2] // 8 - 1
    count = parts * fields * 2 + parts
    return pl.pallas_call(
        edge_kernel,
        grid=(1,),
        in_specs=[
            pl.BlockSpec(rows, lambda i: (0, 0, 0, 0)),
            pl.BlockSpec(rows, lambda i: (0, 0, tiles - 1, 0)),
            pl.BlockSpec(stored, lambda i: (0, 0, 0, 0)),
            pl.BlockSpec(stored, lambda i: (0, 0, tiles, 0)),
            pl.BlockSpec(stored, lambda i: (0, 0, last, 0)),
            pl.BlockSpec(memory_space=pl.ANY),
        ],
        out_specs=[pl.BlockSpec((n, sz.slots), lambda i: (0, 0)) for n in (count, count, parts)],
        out_shape=[jax.ShapeDtypeStruct((n, sz.slots), F32) for n in (count, count, parts)],
        name="edge_rows",
    )(adjoint, adjoint, forward, forward, forward, after)


def shifted(value, axes, step, count):
    return lax.ppermute(value, axes, [(i, i + step) for i in range(count) if 0 <= i + step < count])


def nearer_sum_by_pairs(value, axis):
    count, mine = lax.axis_size(axis), lax.axis_index(axis)
    other = lax.ppermute(value, axis, [(i, i ^ 1) for i in range(count)])
    before = jnp.where(mine & 1 != 0, other, 0.0)
    both = total = value + other
    for k in range(2, count, 2):
        other = lax.ppermute(both, axis, [(i, i ^ k) for i in range(count)])
        before = before + jnp.where(mine ^ k < mine, other, 0.0)
        total = total + other
    return before, total


def nearer_sum(value):
    blocks = lax.axis_size(ROW_BLOCKS)
    return sum(shifted(value, ROW_BLOCKS, step, blocks) for step in range(1, blocks))


def on_device(adjoint, forward, mode_map):
    sz = Sizes(adjoint.shape[2], adjoint.shape[3])
    stations = lax.axis_size("ckpt")
    row_scale = 1.0 / math.sqrt(sz.block_rows * lax.axis_size("wall") * stations)
    me = lax.axis_index("mode").astype(jnp.int32)
    here = lax.axis_index("ckpt").astype(jnp.int32)
    block, blocks = lax.axis_index(ROW_BLOCKS), lax.axis_size(ROW_BLOCKS)
    is_first = (block == 0) & (me == 0)
    is_last = (block == blocks - 1) & (me == sz.group - 1)
    place = jnp.stack([me, here, is_first.astype(jnp.int32), is_last.astype(jnp.int32)])
    spread = halves_of(complex_lanes(span_matrix(1)))
    chunks = CHUNKS

    other = lax.dynamic_slice_in_dim(forward, (1 - here) * sz.block_rows, sz.block_rows, 2)
    moved = lax.ppermute(other, "ckpt", [(i, stations - 1 - i) for i in range(stations)])

    free = jnp.asarray(np.arange(4, dtype=np.int32)) if INWARD[0] else place
    pieces, (ends,) = adjoint_prep(sz, INWARD[0], free, adjoint, spread, chunks[0], spread)
    inward = [pieces.exchange()]

    low, high, past = edge_rows(sz, adjoint, forward, ends)
    low = shifted(low, ROW_BLOCKS, 1, blocks)
    high = shifted(high, ROW_BLOCKS, -1, blocks)
    past = shifted(past, ROW_BLOCKS, -stations, blocks)

    freq_index = lax.div(mode_map, jnp.int32(NK))
    span_index = lax.rem(mode_map, jnp.int32(NK))
    alpha = 2.0 / NF * ((freq_index + NF // 2) % NF - NF // 2).astype(F32)
    beta = 2.0 / NK * ((span_index + NK // 2) % NK - NK // 2).astype(F32)
    freq = freq_index.reshape(sz.blocks, NK)[:, :1].astype(F32)
    freq = jnp.pad(jnp.broadcast_to(freq, (sz.blocks, LANES)), ((0, 8 - sz.blocks), (0, 0)))

    stored, done = forward_prep(
        sz, STORED, place, forward, moved, (low, high, past), ends, freq, spread, chunks[0]
    )
    pieces, _ = adjoint_prep(
        sz, INWARD[1], place, adjoint, spread, chunks[1], done, (low, high)
    )
    stored = stored.exchange(inward[0].arrays if STORED else ())
    got = stored.in_order()
    inward.append(pieces.exchange(got if INWARD[1] else (got + got[-1:] * WINDOW)[WINDOW:]))

    phys, next_phys, rims, table = forward_physical(sz, place, stored, len(chunks[0]), spread)
    turn = halves_of(complex_lanes(beta_matrix()))
    out, (pair, pair_rims, total) = march(
        sz, OUTWARD[0], table, inward[0], phys, next_phys, len(chunks[0]), (rims, turn, spread)
    )
    start, whole = nearer_sum_by_pairs(total, "mode")
    got = inward[1].in_order()
    if OUTWARD[0]:
        back = [out.exchange([whole, *got])]
    else:
        back = [out.exchange([whole] * len(out.arrays))]
    start = start + nearer_sum(whole)
    back_span = halves_of(complex_lanes(span_matrix(-1) / NK))
    running = (pair, pair_rims, start, turn, back_span)
    out, _ = march(
        sz,
        OUTWARD[1],
        table,
        inward[1],
        phys,
        next_phys,
        len(chunks[1]),
        row_scale=row_scale,
        running=running,
    )
    got = back[0].in_order()
    back.append(out.exchange(got if OUTWARD[1] else (got + got[-1:] * WINDOW)[WINDOW:]))

    tri = jnp.asarray(np.tril(np.ones((sz.block_rows, sz.block_rows))), jnp.bfloat16)
    out, sums, total = post(
        sz, row_scale, place, back[0], chunks[0], None, "make", (alpha[None], beta[None], tri)
    )
    start = nearer_sum(total)
    (out,) = post(sz, row_scale, place, back[1], chunks[1], out, "add", (sums, start))
    return out


def solution(mesh):
    placed = (P(None, None, ROW_BLOCKS, "mode"), P("ckpt", None, "wall", "mode"), P("mode"))
    return jax.shard_map(
        on_device,
        mesh=mesh,
        in_specs=placed,
        out_specs=P(None, None, ROW_BLOCKS, "mode"),
        check_vma=False,
    )
```

```python
import functools
import math

import jax
import jax.numpy as jnp
import numpy as np
from jax import lax
from jax.experimental import pallas as pl
from jax.experimental.pallas import tpu as pltpu
from jax.sharding import PartitionSpec as P

NF = 64
NK = 64
LANES = 2 * NK
KAPPA = 0.2
COUPLING = 0.5
HIGHEST = lax.Precision.HIGHEST
ROW_BLOCKS = ("wall", "ckpt")
VMEM = pltpu.CompilerParams(vmem_limit_bytes=64 * 1024 * 1024)
F32 = jnp.float32
COST = pl.CostEstimate(flops=1, bytes_accessed=1, transcendentals=0)
CHUNKS = ((0, 2, 3), (4, 1))
INWARD = (True, True)
STORED = False
WINDOW = 4
OUTWARD = (True, True)


def complex_lanes(matrix):
    twice = np.kron(np.eye(2), matrix)
    return np.block([[twice.real, twice.imag], [-twice.imag, twice.real]]).astype(np.float32)


def span_matrix(direction):
    ids = np.arange(NK)
    return np.exp(2j * math.pi * direction * (np.outer(ids, ids) % NK) / NK)


def beta_matrix():
    ids = np.arange(NK)
    signed = (ids + NK // 2) % NK - NK // 2
    return span_matrix(-1) @ np.diag(2.0 / NK * signed) @ span_matrix(1) / NK


def split(value):
    high = value.astype(jnp.bfloat16)
    return high, (value - high.astype(F32)).astype(jnp.bfloat16)


def halves_of(matrix):
    high, low = split(jnp.asarray(matrix))
    return jnp.stack([high, low])


def dot3(x, w_ref):
    high, low = split(x)
    dot = functools.partial(jnp.dot, preferred_element_type=F32)
    return (dot(low, w_ref[0]) + dot(high, w_ref[1])) + dot(high, w_ref[0])


def low_half(shape):
    return lax.broadcasted_iota(jnp.int32, shape, len(shape) - 1) < NK


def swap(value):
    return pltpu.roll(value, NK, value.ndim - 1)


def dft4(x, sign):
    (ar, ai), (br, bi), (cr, ci), (dr, di) = x
    pr, pi, mr, mi = ar + cr, ai + ci, ar - cr, ai - ci
    qr, qi, nr, ni = br + dr, bi + di, br - dr, bi - di
    if sign > 0:
        nr, ni = -ni, nr
    else:
        nr, ni = ni, -nr
    return [(pr + qr, pi + qi), (mr + nr, mi + ni), (pr - qr, pi - qi), (mr - nr, mi - ni)]


def dft8(x, sign):
    even = dft4(x[0::2], sign)
    odd = dft4(x[1::2], sign)
    half = math.sqrt(0.5)
    (r1, i1), (r2, i2), (r3, i3) = odd[1], odd[2], odd[3]
    if sign > 0:
        odd[1] = (half * (r1 - i1), half * (i1 + r1))
        odd[2] = (-i2, r2)
        odd[3] = (-half * (r3 + i3), half * (r3 - i3))
    else:
        odd[1] = (half * (r1 + i1), half * (i1 - r1))
        odd[2] = (i2, -r2)
        odd[3] = (half * (i3 - r3), -half * (i3 + r3))
    first = [(a + c, b + d) for (a, b), (c, d) in zip(even, odd)]
    second = [(a - c, b - d) for (a, b), (c, d) in zip(even, odd)]
    return first + second


def turned(pair, power, sign):
    power %= NF
    if power == 0:
        return pair
    angle = 2.0 * math.pi * power / NF
    c, s = math.cos(angle), sign * math.sin(angle)
    re, im = pair
    return (c * re - s * im, c * im + s * re)


class Sizes:
    def __init__(self, rows, slots):
        self.group = lax.axis_size("mode")
        self.block_rows = rows
        self.slots = slots
        self.lane_groups = slots // LANES
        self.blocks = slots // NK
        self.rows = rows // self.group
        self.half = self.rows // 2
        self.tile = min(8, self.half)
        self.tiles = self.half // self.tile
        self.padded = (self.half + 7) // 8 * 8 + 16
        self.body = 2 * self.blocks * self.half
        self.rims = 2 * self.blocks


class Pieces:
    def __init__(self, whole, arrays):
        self.whole, self.arrays = whole, arrays

    def specs(self, group):
        if self.whole:
            length = self.arrays[0].shape[2]
            return [pl.BlockSpec((group, 1, length, LANES), lambda i, *_: (0, i, 0, 0))]
        length = self.arrays[0].shape[1]
        return [pl.BlockSpec((1, length, LANES), lambda i, *_: (i, 0, 0))] * group

    @staticmethod
    def shapes(whole, group, count, length):
        if whole:
            return [jax.ShapeDtypeStruct((group, count, length, LANES), F32)]
        return [jax.ShapeDtypeStruct((count, length, LANES), F32)] * group

    def exchange(self, earlier=()):
        if self.whole:
            array = after(self.arrays[0], *earlier)
            return Pieces(True, [lax.all_to_all(array, "mode", 0, 0, tiled=True)])
        group = len(self.arrays)
        moved = list(self.arrays)
        for n, k in enumerate(partners(group)):
            array = after(moved[k], *earlier[n : n + 1])
            moved[k] = lax.ppermute(array, "mode", [(i, i ^ k) for i in range(group)])
        return Pieces(False, moved)

    def in_order(self):
        if self.whole:
            return list(self.arrays)
        return [self.arrays[k] for k in partners(len(self.arrays))]


def partners(group):
    return sorted(range(1, group), key=lambda k: (-bin(k >> 1).count("1"), k & 1, k))


def field_at(fields):
    return lambda i: sum(jnp.where(i == n, f, 0) for n, f in enumerate(fields))


def piece_refs(refs, whole, group):
    if whole:
        return [refs[0].at[k, 0] for k in range(group)], refs[1:]
    return [ref.at[0] for ref in refs[:group]], refs[group:]


def partner(whole, me, k):
    return k if whole else me ^ k


def pair_rows(top, bottom):
    low = low_half(top.shape)
    return jnp.where(low, top, swap(bottom)), jnp.where(low, swap(top), bottom)


def cut_pieces(sz, dest, planes, out, base=0):
    row = pl.multiple_of(8 + dest * sz.rows, 8)
    for g in range(sz.lane_groups):
        whole = planes[g, pl.ds(row, sz.rows), :]
        for c in range(2):
            part = whole[:, c * LANES : (c + 1) * LANES]
            for odd, value in enumerate(pair_rows(part[: sz.half], part[sz.half :])):
                place = base + (c * sz.blocks + 2 * g + odd) * sz.half
                out[place : place + sz.half, :] = value


def join(x_ref, at):
    return jnp.concatenate([x_ref[c, ..., at].reshape(-1, LANES) for c in range(2)], axis=1)


def join_rows(x_ref, rows, step, at):
    parts = [
        jnp.concatenate([x_ref[pl.ds(r + c * step, 1), :] for r in rows], axis=0) for c in range(2)
    ]
    at = slice(at.start, at.start + at.size)
    return jnp.concatenate([part[:, at] for part in parts], axis=1)


def put_rows(sz, out, place, rows):
    for c in range(2):
        at = slice(c * LANES, (c + 1) * LANES)
        for g, (down, up) in enumerate(rows):
            for odd, value in enumerate(pair_rows(down[:, at], up[:, at])):
                row = place + c * sz.blocks + 2 * g + odd
                out[row : row + 1, :] = value


def cut_rims(sz, dest, planes, out, place, depths):
    for depth in range(depths):
        down = pl.ds(8 - 1 - depth + dest * sz.rows, 1)
        up = pl.ds(8 + depth + (dest + 1) * sz.rows, 1)
        rows = [(planes[g, down, :], planes[g, up, :]) for g in range(sz.lane_groups)]
        put_rows(sz, out, place + depth * sz.rims, rows)


def adjoint_prep_kernel(sz, whole, with_rims, field, me_ref, x_ref, _, *rest):
    if with_rims:
        w_ref, low, high, *rest = rest
        outs, (planes,) = piece_refs(rest, whole, sz.group)
    else:
        outs, (ends, planes) = piece_refs(rest, whole, sz.group)
    body = slice(8, 8 + sz.block_rows)
    row = 2 * field(pl.program_id(0))
    groups = [pl.ds(g * LANES, LANES) for g in range(sz.lane_groups)]
    every = [jnp.concatenate([x_ref[c, 0, :, at] for c in range(2)], axis=1) for at in groups]
    every = jnp.concatenate(every, axis=0)
    if with_rims:
        every = dot3(every, w_ref)
    for g, at in enumerate(groups):
        planes[g, body, :] = every[g * sz.block_rows : (g + 1) * sz.block_rows]
        if with_rims:
            step = low.shape[0] // 2 - 1
            planes[g, 6:8, :] = dot3(join_rows(low, (row, row + 1), step, at), w_ref)
            planes[g, 8 + sz.block_rows : 10 + sz.block_rows, :] = dot3(
                join_rows(high, (row, row + 1), step, at), w_ref
            )
    for k in range(sz.group):
        dest = partner(whole, me_ref[0], k)
        cut_pieces(sz, dest, planes, outs[k])
        if with_rims:
            cut_rims(sz, dest, planes, outs[k], sz.body, 2)
        else:
            for g in range(sz.lane_groups):
                for n, row in enumerate((0, 1, sz.rows - 1, sz.rows - 2)):
                    row = 8 + k * sz.rows + row
                    ends[0, n, g, k : k + 1, :] = planes[g, row : row + 1, :]


def adjoint_prep(sz, whole, me, adjoint, w, fields, after, edges=None):
    count = len(fields)
    field = field_at(fields)
    with_rims = edges is not None
    shapes = Pieces.shapes(whole, sz.group, count, sz.body + (2 * sz.rims if with_rims else 0))
    in_specs = [
        pl.BlockSpec((2, 1, sz.block_rows, sz.slots), lambda i, me: (0, field(i), 0, 0)),
        pl.BlockSpec(memory_space=pl.ANY),
    ]
    operands = [me, adjoint, after]
    out_specs, out_shape = Pieces(whole, shapes).specs(sz.group), list(shapes)
    if with_rims:
        in_specs.append(pl.BlockSpec(w.shape, lambda i, me: (0, 0, 0)))
        in_specs += [pl.BlockSpec(x.shape, lambda i, me: (0, 0)) for x in edges]
        operands += [w, *edges]
    else:
        ends = (4, sz.lane_groups, sz.group, 2 * LANES)
        out_specs.append(pl.BlockSpec((1,) + ends, lambda i, me: (i, 0, 0, 0, 0)))
        out_shape.append(jax.ShapeDtypeStruct((count,) + ends, F32))
    arrays = pl.pallas_call(
        functools.partial(adjoint_prep_kernel, sz, whole, with_rims, field),
        grid_spec=pltpu.PrefetchScalarGridSpec(
            num_scalar_prefetch=1,
            grid=(count,),
            in_specs=in_specs,
            out_specs=out_specs,
            scratch_shapes=[pltpu.VMEM((sz.lane_groups, sz.block_rows + 16, 2 * LANES), F32)],
        ),
        out_shape=out_shape,
        compiler_params=VMEM,
        cost_estimate=COST,
        name="adjoint_prep",
    )(*operands)
    return Pieces(whole, arrays[: len(shapes)]), arrays[len(shapes) :]


def forward_prep_kernel(
    sz, whole, chunk, me_ref, own, other, before, low, high, past, ends, freq, w_ref, *rest
):
    outs, (done, planes, rims) = piece_refs(rest, whole, sz.group)
    done[...] = jnp.zeros_like(done)
    here = me_ref[1]
    body = slice(8, 8 + sz.block_rows)
    groups = [pl.ds(g * LANES, LANES) for g in range(sz.lane_groups)]
    for x_ref, station in ((own, here), (other, 1 - here)):
        every = dot3(jnp.concatenate([join(x_ref.at[0], at) for at in groups], axis=0), w_ref)
        for g in range(sz.lane_groups):
            rows = slice(g * sz.block_rows, (g + 1) * sz.block_rows)
            planes[station, g, body, :] = every[rows]
    for g, at in enumerate(groups):
        count = low.shape[0] - 2
        step = count // 2
        inner = here == 0
        row = [before[0, c, 7:8, at] for c in range(2)]
        row = jnp.concatenate(row, axis=1)
        row = jnp.where(inner, join_rows(low, (count,), 1, at), row)
        planes[1, g, 7:8, :] = dot3(row, w_ref)
        row = jnp.where(inner, join_rows(high, (count,), 1, at), join_rows(past, (0,), 1, at))
        planes[1, g, 8 + sz.block_rows : 9 + sz.block_rows, :] = dot3(row, w_ref)
        far_low, far_high = (
            jnp.concatenate([x_ref[c * step : (c + 1) * step, at] for c in range(2)], 1)
            for x_ref in (low, high)
        )
        for i, field in enumerate(chunk):
            for depth in range(2):
                row = 2 * field + 1 - depth
                rims[i, depth, 0, g] = jnp.concatenate(
                    [far_low[row : row + 1], ends[i, 2 + depth, g][:-1]], 0
                )
                row = 2 * field + depth
                rims[i, depth, 1, g] = jnp.concatenate(
                    [ends[i, depth, g][1:], far_high[row : row + 1]], 0
                )
    for k in range(sz.group):
        dest = partner(whole, me_ref[0], k)
        outs[k][:8, :] = freq[...]
        for station in range(2):
            cut_pieces(sz, dest, planes.at[station], outs[k], 8 + station * sz.body)
        place = 8 + 2 * sz.body
        cut_rims(sz, dest, planes.at[1], outs[k], place, 1)
        row = pl.ds(dest, 1)
        for i in range(len(chunk)):
            for depth in range(2):
                place += sz.rims
                rows = [
                    (rims[i, depth, 0, g, row, :], rims[i, depth, 1, g, row, :])
                    for g in range(sz.lane_groups)
                ]
                put_rows(sz, outs[k], place, rows)


def forward_prep(sz, whole, me, forward, other, edges, ends, freq, w, chunk):
    length = (8 + 2 * sz.body + (1 + 2 * len(chunk)) * sz.rims + 7) // 8 * 8
    shapes = Pieces.shapes(whole, sz.group, 1, length)
    rows = (1, 2, sz.block_rows, sz.slots)
    rest = [*edges, ends, freq, w]
    before = sz.block_rows // 8 - 1
    arrays = pl.pallas_call(
        functools.partial(forward_prep_kernel, sz, whole, chunk),
        grid_spec=pltpu.PrefetchScalarGridSpec(
            num_scalar_prefetch=1,
            grid=(1,),
            in_specs=[
                pl.BlockSpec(rows, lambda i, me: (0, 0, me[1], 0)),
                pl.BlockSpec(rows, lambda i, me: (0, 0, 0, 0)),
                pl.BlockSpec((1, 2, 8, sz.slots), lambda i, me: (0, 0, before, 0)),
            ]
            + [pl.BlockSpec(x.shape, lambda i, me, zeros=(0,) * x.ndim: zeros) for x in rest],
            out_specs=Pieces(whole, shapes).specs(sz.group)
            + [pl.BlockSpec((8, LANES), lambda i, me: (0, 0))],
            scratch_shapes=[
                pltpu.VMEM((2, sz.lane_groups, sz.block_rows + 16, 2 * LANES), F32),
                pltpu.VMEM((len(chunk), 2, 2, sz.lane_groups, sz.group, 2 * LANES), F32),
            ],
        ),
        out_shape=shapes + [jax.ShapeDtypeStruct((8, LANES), F32)],
        compiler_params=VMEM,
        cost_estimate=COST,
        name="forward_prep",
    )(me, forward, other, forward, *rest)
    return Pieces(whole, arrays[:-1]), arrays[-1]


def frequency(sz, table_ref, whole, k, j):
    place = k ^ table_ref[sz.group * sz.blocks] if whole else k
    return table_ref[place * sz.blocks + j]


def gather_pieces(sz, table_ref, whole, pieces, state, lead, base=0):
    for k, piece in enumerate(pieces):
        for j in range(sz.blocks):
            freq = frequency(sz, table_ref, whole, k, j)
            for c in range(2):
                at = base + (c * sz.blocks + j) * sz.half
                state[c, freq, lead : lead + sz.half, :] = piece[at : at + sz.half, :]


def lead_first(sz, state, rows, work, out_rows):
    for a in range(8):
        x = [(state[0, a + 8 * b, rows, :], state[1, a + 8 * b, rows, :]) for b in range(8)]
        for t, pair in enumerate(dft8(x, 1)):
            re, im = turned(pair, a * t, 1)
            work[0, 8 * t + a, out_rows, :] = re
            work[1, 8 * t + a, out_rows, :] = im


def lead_second(work, t, rows):
    x = [(work[0, 8 * t + a, rows, :], work[1, 8 * t + a, rows, :]) for a in range(8)]
    return dft8(x, 1)


def couple(sz, state, rows, work, work_rows, phys, phys_rows, store):
    lead_first(sz, state, rows, work, work_rows)
    for t in range(8):
        product = []
        for u, (re, im) in enumerate(lead_second(work, t, work_rows)):
            wr, wi = phys[0, 8 * t + u, phys_rows, :], phys[1, 8 * t + u, phys_rows, :]
            product.append((wr * re + wi * im, wr * im - wi * re))
        for a, pair in enumerate(dft8(product, -1)):
            re, im = turned(pair, a * t, -1)
            work[0, 8 * t + a, work_rows, :] = re
            work[1, 8 * t + a, work_rows, :] = im
    for a in range(8):
        x = [
            (work[0, 8 * t + a, work_rows, :], work[1, 8 * t + a, work_rows, :]) for t in range(8)
        ]
        for b, pair in enumerate(dft8(x, -1)):
            store(a + 8 * b, pair)


def gather_rims(sz, table_ref, whole, pieces, rims, base):
    for k, piece in enumerate(pieces):
        for j in range(sz.blocks):
            freq = frequency(sz, table_ref, whole, k, j)
            for c in range(2):
                at = base + c * sz.blocks + j
                rims[c, pl.ds(freq, 1), :] = piece[at : at + 1, :]


def forward_kernel(sz, whole, chunk, me_ref, *rest):
    pieces, rest = piece_refs(rest, whole, sz.group)
    heads, rest = piece_refs(rest, whole, sz.group)
    w_ref, out, next_out, rims, table_ref, state, work, next_state, next_work = rest
    count = sz.group * sz.blocks
    for k in range(sz.group):
        place = k ^ me_ref[0] if whole else k
        for j in range(sz.blocks):
            table_ref[place * sz.blocks + j] = heads[k][j, 0].astype(jnp.int32)
    for n in range(4):
        table_ref[count + n] = me_ref[n]
    for station in range(2):
        gather_pieces(sz, table_ref, whole, pieces, state, 0, 8 + station * sz.body)

        @pl.loop(0, sz.tiles)
        def _(s):
            rows = pl.ds(s * sz.tile, sz.tile)
            lead_first(sz, state, rows, work, rows)
            for t in range(8):
                for u, (re, im) in enumerate(lead_second(work, t, rows)):
                    out[station, 0, 8 * t + u, rows, :] = re
                    out[station, 1, 8 * t + u, rows, :] = im

    base = 8 + 2 * sz.body
    gather_rims(sz, table_ref, whole, pieces, rims.at[0, 0], base)
    spread_rims(rims[0, 0].reshape(2 * NF, LANES), next_state, 0)
    rows = slice(0, 8)
    lead_first(sz, next_state, rows, next_work, rows)
    for t in range(8):
        for u, (re, im) in enumerate(lead_second(next_work, t, rows)):
            next_out[0, 8 * t + u] = re[:1]
            next_out[1, 8 * t + u] = im[:1]
    for i in range(chunk):
        for depth in range(2):
            base += sz.rims
            gather_rims(sz, table_ref, whole, pieces, rims.at[i, depth], base)
            every = dot3(jnp.concatenate([rims[i, depth, 0], rims[i, depth, 1]], axis=1), w_ref)
            for c in range(2):
                rims[i, depth, c] = every[:, c * LANES : (c + 1) * LANES]


def forward_physical(sz, me, pieces, chunk, w):
    full = (2, NF, sz.half, LANES)
    rims = (chunk, 2, 2, NF, LANES)
    if pieces.whole:
        heads = [
            pl.BlockSpec((sz.group, 1, 8, LANES), lambda i, t: (0, 0, 0, 0), memory_space=pltpu.SMEM)
        ]
    else:
        head = pl.BlockSpec((1, 8, LANES), lambda i, t: (0, 0, 0), memory_space=pltpu.SMEM)
        heads = [head] * sz.group
    return pl.pallas_call(
        functools.partial(forward_kernel, sz, pieces.whole, chunk),
        grid_spec=pltpu.PrefetchScalarGridSpec(
            num_scalar_prefetch=1,
            grid=(1,),
            in_specs=pieces.specs(sz.group)
            + heads
            + [pl.BlockSpec(w.shape, lambda i, t: (0, 0, 0))],
            out_specs=[
                pl.BlockSpec((2,) + full, lambda i, t: (0, 0, 0, 0, 0)),
                pl.BlockSpec((2, NF, 1, LANES), lambda i, t: (0, 0, 0, 0)),
                pl.BlockSpec(rims, lambda i, t: (0, 0, 0, 0, 0)),
                pl.BlockSpec(memory_space=pltpu.SMEM),
            ],
            scratch_shapes=[
                pltpu.VMEM(full, F32),
                pltpu.VMEM(full, F32),
                pltpu.VMEM((2, NF, 8, LANES), F32),
                pltpu.VMEM((2, NF, 8, LANES), F32),
            ],
        ),
        out_shape=[
            jax.ShapeDtypeStruct((2,) + full, F32),
            jax.ShapeDtypeStruct((2, NF, 1, LANES), F32),
            jax.ShapeDtypeStruct(rims, F32),
            jax.ShapeDtypeStruct((sz.group * sz.blocks + 4,), jnp.int32),
        ],
        compiler_params=VMEM,
        cost_estimate=COST,
        name="forward_physical",
    )(me, *pieces.arrays, *pieces.arrays, w)


def spread_rims(rims, state, n):
    state.reshape(2 * NF * 8, LANES)[pl.ds(n, 2 * NF, stride=8), :] = rims


def place_edges(sz, state, rims):
    padded = sz.padded
    rows = state.reshape(2 * NF * padded, LANES)
    first = rows[pl.ds(8, 2 * NF, stride=padded), :]
    last = rows[pl.ds(8 + sz.half - 1, 2 * NF, stride=padded), :]
    low = low_half(first.shape)
    rows[pl.ds(7, 2 * NF, stride=padded), :] = jnp.where(low, rims, swap(last))
    rows[pl.ds(8 + sz.half, 2 * NF, stride=padded), :] = jnp.where(low, swap(first), rims)


def advance(sz, state, work, phys, out, lead):
    @pl.loop(0, sz.tiles)
    def _(s):
        rows = pl.ds(8 + s * sz.tile, sz.tile)
        at = pl.ds(s * sz.tile, sz.tile)

        def store(f, pair):
            for c in range(2):
                mid = state[c, f, rows, :]
                up = state[c, f, pl.ds(9 + s * sz.tile, sz.tile), :]
                down = state[c, f, pl.ds(7 + s * sz.tile, sz.tile), :]
                stepped = (1.0 - 2.0 * KAPPA) * mid + KAPPA * (up + down)
                out[c, f, pl.ds(lead + s * sz.tile, sz.tile), :] = (
                    stepped - (COUPLING / NF) * pair[c]
                )

        couple(sz, state, rows, work, at, phys, at, store)


def march_kernel(sz, whole_in, whole_out, row_scale, fields, table_ref, *rest):
    pieces, rest = piece_refs(rest, whole_in, sz.group)
    phys, next_phys, *rest = rest
    running = row_scale is not None
    if running:
        all_rims, rest = rim_refs(rest, whole_in, sz.group)
        pair, pair_rims, start, w_ref, back_ref, *rest = rest
    else:
        rims_in, w_ref, spread_ref, *rest = rest
    outs, rest = piece_refs(rest, whole_out, sz.group)
    if not running:
        pair_out, pair_rims_out, total_out, *rest = rest
    state, work, middle, stepped, rims, next_state, next_work, next_coupling, sums = rest
    step = pl.program_id(0)
    count = sz.group * sz.blocks

    @pl.when(step == 0)
    def _():
        next_state[...] = jnp.zeros_like(next_state)
        for i in range(fields):
            for depth in range(2):
                if running:
                    views = [ref.at[i] for ref in all_rims]
                    gather_rims(sz, table_ref, whole_in, views, rims.at[i, depth], depth * sz.rims)
                else:
                    rims[i, depth] = rims_in[i, depth]
            spread_rims(rims[i, 0].reshape(2 * NF, LANES), next_state, i)
        rows = slice(0, 8)

        def store(f, pair):
            for c in range(2):
                next_coupling[c, f] = (COUPLING / NF) * pair[c]

        couple(sz, next_state, rows, next_work, rows, next_phys, slice(0, 1), store)

    gather_pieces(sz, table_ref, whole_in, pieces, state, 8)
    body = slice(8, 8 + sz.half)
    if not running:
        both = jnp.concatenate([state[0, :, body, :], state[1, :, body, :]], axis=2)
        both = dot3(both.reshape(NF * sz.half, 2 * LANES), spread_ref)
        for c in range(2):
            lanes = slice(c * LANES, (c + 1) * LANES)
            state[c, :, body, :] = both[:, lanes].reshape(NF, sz.half, LANES)
    near = rims[step, 0].reshape(2 * NF, LANES)
    place_edges(sz, state, near)
    advance(sz, state, work, phys.at[1], middle, 8)

    low = low_half((2 * NF, LANES))
    flat = state.reshape(2 * NF * sz.padded, LANES)
    inner = jnp.where(
        low,
        flat[pl.ds(8, 2 * NF, stride=sz.padded), :],
        flat[pl.ds(8 + sz.half - 1, 2 * NF, stride=sz.padded), :],
    )
    far = rims[step, 1].reshape(2 * NF, LANES)
    coupled = next_coupling.reshape(2 * NF * 8, LANES)[pl.ds(step, 2 * NF, stride=8), :]
    near = (1.0 - 2.0 * KAPPA) * near + KAPPA * (inner + far) - coupled
    rims[step, 0] = near.reshape(2, NF, LANES)
    if running:

        @pl.when(step == fields - 1)
        def _():
            add_running(
                sz, row_scale, middle, rims.at[step, 0], pair, pair_rims, start, w_ref, next_work
            )

    first = table_ref[count + 2].astype(F32)
    last = table_ref[count + 3].astype(F32)
    near = rims[step, 0].reshape(2 * NF, LANES) * jnp.where(low, 1.0 - first, 1.0 - last)
    if not running:

        def sums_of():
            pair_rims_out[0] = near.reshape(2, NF, LANES)
            rows = middle[:, :, body, :]
            pair_out[0] = rows
            value = jnp.sum(rows, axis=2)
            return value + swap(value)

        @pl.when(step == 0)
        def _():
            value = sums_of()
            freq = lax.broadcasted_iota(jnp.int32, value.shape, 1)
            rate = 2.0 / NF * ((freq + NF // 2) % NF - NF // 2).astype(F32)
            sums[...] = rate * value

        @pl.when(step == 1)
        def _():
            value = sums_of()
            turned = dot3(jnp.concatenate([value[0], value[1]], axis=1), w_ref)
            re, im = sums[0] + turned[:, :LANES], sums[1] + turned[:, LANES:]
            total = jnp.where(low_half((NF, LANES)), re, im)
            total_out[...] = total

    place_edges(sz, middle, near)
    advance(sz, middle, work, phys.at[0], stepped, 0)
    if running:
        both = jnp.concatenate([stepped[0], stepped[1]], axis=2).reshape(NF * sz.half, 2 * LANES)
        both = dot3(both, back_ref)
        for c in range(2):
            stepped[c] = both[:, c * LANES : (c + 1) * LANES].reshape(NF, sz.half, LANES)
    for k in range(sz.group):
        for j in range(sz.blocks):
            freq = frequency(sz, table_ref, whole_out, k, j)
            for c in range(2):
                at = (c * sz.blocks + j) * sz.half
                outs[k][at : at + sz.half, :] = stepped[c, freq]


def rim_refs(refs, whole, group):
    if whole:
        return [refs[0].at[k] for k in range(group)], refs[1:]
    return list(refs[:group]), refs[group:]


def march(sz, whole_out, table, pieces, phys, next_phys, fields, rims=None, row_scale=None, running=()):
    full = (2, NF, sz.half, LANES)
    shapes = Pieces.shapes(whole_out, sz.group, fields, sz.body)

    def constant(x):
        return pl.BlockSpec(x.shape, lambda i, t, zeros=(0,) * len(x.shape): zeros)

    def by_field(shape):
        return pl.BlockSpec(
            (1,) + shape, lambda i, t, zeros=(0,) * len(shape): (jnp.minimum(i, 1),) + zeros
        )

    body = Pieces(pieces.whole, Pieces.shapes(pieces.whole, sz.group, fields, sz.body))
    in_specs = body.specs(sz.group) + [constant(phys), constant(next_phys)]
    operands = [table, *pieces.arrays, phys, next_phys]
    out_specs, out_shape = Pieces(whole_out, shapes).specs(sz.group), list(shapes)
    if running:
        place = sz.body // (2 * sz.rims)
        if pieces.whole:
            block = (sz.group, fields, 2 * sz.rims, LANES)
            in_specs.append(pl.BlockSpec(block, lambda i, t: (0, 0, place, 0)))
        else:
            block = (fields, 2 * sz.rims, LANES)
            in_specs += [pl.BlockSpec(block, lambda i, t: (0, place, 0))] * sz.group
        in_specs += [constant(x) for x in running]
        operands += [*pieces.arrays, *running]
    else:
        in_specs += [constant(x) for x in rims]
        operands += rims
        for shape in (full, (2, NF, LANES)):
            out_specs.append(by_field(shape))
            out_shape.append(jax.ShapeDtypeStruct((2,) + shape, F32))
        out_shape.append(jax.ShapeDtypeStruct((NF, LANES), F32))
        out_specs.append(constant(out_shape[-1]))
    padded = pltpu.VMEM((2, NF, sz.padded, LANES), F32)
    small = pltpu.VMEM((2, NF, 8, LANES), F32)
    arrays = pl.pallas_call(
        functools.partial(march_kernel, sz, pieces.whole, whole_out, row_scale, fields),
        grid_spec=pltpu.PrefetchScalarGridSpec(
            num_scalar_prefetch=1,
            grid=(fields,),
            in_specs=in_specs,
            out_specs=out_specs,
            scratch_shapes=[
                padded,
                pltpu.VMEM(full, F32),
                padded,
                pltpu.VMEM(full, F32),
                pltpu.VMEM((fields, 2, 2, NF, LANES), F32),
                small,
                small,
                small,
                pltpu.VMEM((2, NF, LANES), F32),
            ],
        ),
        out_shape=out_shape,
        compiler_params=VMEM,
        cost_estimate=COST,
        name="march",
    )(*operands)
    return Pieces(whole_out, arrays[: len(shapes)]), arrays[len(shapes) :]


def running_rows(sz, value, start):
    row = lax.broadcasted_iota(jnp.int32, value.shape, 0)
    reach = 1
    while reach < sz.half:
        value = value + jnp.where(row >= reach, pltpu.roll(value, reach, 0), 0.0)
        reach *= 2
    bottom = jnp.where(low_half((1, LANES)), 0.0, swap(value[sz.half - 1 :]))
    return value + (bottom + start)


def add_running(sz, row_scale, middle, near, pair, pair_rims, start, w_ref, work):
    both = jnp.concatenate([pair[1, 0], pair[1, 1]], axis=2).reshape(NF * sz.half, 2 * LANES)
    turned_two = dot3(both, w_ref)
    turned_rims = dot3(jnp.concatenate([pair_rims[1, 0], pair_rims[1, 1]], axis=1), w_ref)
    low = low_half((1, LANES))
    for f in range(NF):
        at = f * sz.half
        alpha = 2.0 / NF * ((f + NF // 2) % NF - NF // 2)
        spread = start[pl.ds(f, 1), :]
        starts = (jnp.where(low, spread, swap(spread)), jnp.where(low, swap(spread), spread))
        run = []
        for c in range(2):
            lanes = slice(c * LANES, (c + 1) * LANES)
            source = turned_two[at : at + sz.half, lanes] + alpha * pair[0, c, f]
            run.append(running_rows(sz, source, starts[c]))
            past = turned_rims[f : f + 1, lanes] + alpha * pair_rims[0, c, f : f + 1, :]
            work[c, f, 0:1, :] = jnp.where(low, starts[c], run[c][sz.half - 1 :] + past)
        rows = slice(8, 8 + sz.half)
        middle[0, f, rows, :] += row_scale * run[1]
        middle[1, f, rows, :] -= row_scale * run[0]
        near[0, f : f + 1, :] += row_scale * work[1, f, 0:1, :]
        near[1, f : f + 1, :] -= row_scale * work[0, f, 0:1, :]


def join_pieces(sz, whole, me, pieces, planes):
    for k, piece in enumerate(pieces):
        row = pl.multiple_of(partner(whole, me, k) * sz.rows, sz.rows)
        for g in range(sz.lane_groups):
            halves = []
            for c in range(2):
                at = (c * sz.blocks + 2 * g) * sz.half
                even = piece[at : at + sz.half, :]
                odd = piece[at + sz.half : at + 2 * sz.half, :]
                low = low_half(even.shape)
                top = jnp.where(low, even, swap(odd))
                bottom = jnp.where(low, swap(even), odd)
                halves.append(jnp.concatenate([top, bottom], axis=0))
            planes[g, pl.ds(row, sz.rows), :] = jnp.concatenate(halves, axis=1)


def post_kernel(sz, whole, running, row_scale, me_ref, *rest):
    pieces, rest = piece_refs(rest, whole, sz.group)
    if running != "add":
        w_ref, rest = rest[0], rest[1:]
    if running == "add":
        sums_ref, start_ref, rest = rest[0], rest[1], rest[2:]
    elif running == "make":
        alpha_ref, beta_ref, tri_ref, rest = rest[0], rest[1], rest[2], rest[3:]
        rest, source = rest[:-1], rest[-1]
    planes = rest[-1]
    outs = rest[:-1]
    if running != "make":
        outs = outs[1:]
    out = outs[0]
    join_pieces(sz, whole, me_ref[0], pieces, planes)
    every = planes[...].reshape(-1, 2 * LANES)
    if running != "add":
        every = dot3(every, w_ref)
    for g in range(sz.lane_groups):
        at = pl.ds(g * LANES, LANES)
        back = every[g * sz.block_rows : (g + 1) * sz.block_rows]
        halves = [back[:, :LANES], back[:, LANES:]]
        for c in range(2):
            out[c, 0, :, at] = halves[c]
        if running == "add":

            @pl.when(pl.program_id(0) == pl.num_programs(0) - 1)
            def _():
                sums = [sums_ref[c, :, at] + start_ref[pl.ds(c, 1), at] for c in range(2)]
                out[0, 0, :, at] += row_scale * sums[1]
                out[1, 0, :, at] -= row_scale * sums[0]

        if running == "make":

            @pl.when(pl.program_id(0) == 0)
            def _():
                for c in range(2):
                    source[g, :, c * LANES : (c + 1) * LANES] = halves[c] * alpha_ref[:, at]

            @pl.when(pl.program_id(0) == 1)
            def _():
                both = [
                    source[g, :, c * LANES : (c + 1) * LANES] + halves[c] * beta_ref[:, at]
                    for c in range(2)
                ]
                high, low = split(jnp.concatenate(both, axis=1))
                tri = tri_ref[...]
                total = jnp.dot(tri, low, preferred_element_type=F32)
                total = total + jnp.dot(tri, high, preferred_element_type=F32)
                for c in range(2):
                    outs[1][c, :, at] = total[:, c * LANES : (c + 1) * LANES]
                    outs[2][c : c + 1, at] = total[-1:, c * LANES : (c + 1) * LANES]


def post(sz, row_scale, me, pieces, fields, held, running=None, extra=()):
    count = len(fields)
    field = field_at(fields)
    w = halves_of(complex_lanes(span_matrix(-1) / NK))
    w_spec = pl.BlockSpec((2, 2 * LANES, 2 * LANES), lambda i, me: (0, 0, 0))
    in_specs = pieces.specs(sz.group) + [w_spec] * (running != "add")
    row_spec = pl.BlockSpec((1, sz.slots), lambda i, me: (0, 0))
    sums_spec = pl.BlockSpec((2, sz.block_rows, sz.slots), lambda i, me: (0, 0, 0))
    if running == "add":
        in_specs += [sums_spec, pl.BlockSpec((2, sz.slots), lambda i, me: (0, 0))]
    elif running == "make":
        square = pl.BlockSpec((sz.block_rows, sz.block_rows), lambda i, me: (0, 0))
        in_specs += [row_spec, row_spec, square]
    out_specs = [
        pl.BlockSpec((2, 1, sz.block_rows, sz.slots), lambda i, me: (0, field(i), 0, 0))
    ]
    out_shape = [jax.ShapeDtypeStruct((2, 5, sz.block_rows, sz.slots), F32)]
    aliases = {}
    operands = [me, *pieces.arrays, *([] if running == "add" else [w]), *extra]
    plane = pltpu.VMEM((sz.lane_groups, sz.block_rows, 2 * LANES), F32)
    if running == "make":
        out_specs.append(sums_spec)
        out_shape.append(jax.ShapeDtypeStruct((2, sz.block_rows, sz.slots), F32))
        out_specs.append(pl.BlockSpec((2, sz.slots), lambda i, me: (0, 0)))
        out_shape.append(jax.ShapeDtypeStruct((2, sz.slots), F32))
    else:
        in_specs.append(pl.BlockSpec(memory_space=pl.ANY))
        operands.append(held)
        aliases = {len(operands) - 1: 0}
    return pl.pallas_call(
        functools.partial(post_kernel, sz, pieces.whole, running, row_scale),
        grid_spec=pltpu.PrefetchScalarGridSpec(
            num_scalar_prefetch=1,
            grid=(count,),
            in_specs=in_specs,
            out_specs=out_specs,
            scratch_shapes=[plane] * (2 if running == "make" else 1),
        ),
        out_shape=out_shape,
        input_output_aliases=aliases,
        compiler_params=VMEM,
        cost_estimate=COST,
        name="post",
    )(*operands)


def after(value, *earlier):
    return lax.optimization_barrier((value, *earlier))[0]


def edge_kernel(first_ref, last_ref, before, middle, after, token, low, high, past):
    rows = first_ref.shape[1] * 2
    for c in range(2):
        for field in range(first_ref.shape[1]):
            at = c * rows + 2 * field
            low[at : at + 2, :] = last_ref[c, field, 6:8, :]
            high[at : at + 2, :] = first_ref[c, field, 0:2, :]
        at = 2 * rows + c
        low[at : at + 1, :] = after[0, c, 7:8, :]
        high[at : at + 1, :] = middle[0, c, 0:1, :]
        past[c : c + 1, :] = before[0, c, 0:1, :]


def edge_rows(sz, adjoint, forward, after):
    parts, fields = adjoint.shape[:2]
    rows = (parts, fields, 8, sz.slots)
    stored = (1, parts, 8, sz.slots)
    tiles = sz.block_rows // 8
    last = forward.shape[2] // 8 - 1
    count = parts * fields * 2 + parts
    return pl.pallas_call(
        edge_kernel,
        grid=(1,),
        in_specs=[
            pl.BlockSpec(rows, lambda i: (0, 0, 0, 0)),
            pl.BlockSpec(rows, lambda i: (0, 0, tiles - 1, 0)),
            pl.BlockSpec(stored, lambda i: (0, 0, 0, 0)),
            pl.BlockSpec(stored, lambda i: (0, 0, tiles, 0)),
            pl.BlockSpec(stored, lambda i: (0, 0, last, 0)),
            pl.BlockSpec(memory_space=pl.ANY),
        ],
        out_specs=[pl.BlockSpec((n, sz.slots), lambda i: (0, 0)) for n in (count, count, parts)],
        out_shape=[jax.ShapeDtypeStruct((n, sz.slots), F32) for n in (count, count, parts)],
        name="edge_rows",
    )(adjoint, adjoint, forward, forward, forward, after)


def shifted(value, axes, step, count):
    return lax.ppermute(value, axes, [(i, i + step) for i in range(count) if 0 <= i + step < count])


def nearer_sum_by_pairs(value, axis):
    count, mine = lax.axis_size(axis), lax.axis_index(axis)
    other = lax.ppermute(value, axis, [(i, i ^ 1) for i in range(count)])
    before = jnp.where(mine & 1 != 0, other, 0.0)
    both = total = value + other
    for k in range(2, count, 2):
        other = lax.ppermute(both, axis, [(i, i ^ k) for i in range(count)])
        before = before + jnp.where(mine ^ k < mine, other, 0.0)
        total = total + other
    return before, total


def nearer_sum(value):
    blocks = lax.axis_size(ROW_BLOCKS)
    return sum(shifted(value, ROW_BLOCKS, step, blocks) for step in range(1, blocks))


def on_device(adjoint, forward, mode_map):
    sz = Sizes(adjoint.shape[2], adjoint.shape[3])
    stations = lax.axis_size("ckpt")
    row_scale = 1.0 / math.sqrt(sz.block_rows * lax.axis_size("wall") * stations)
    me = lax.axis_index("mode").astype(jnp.int32)
    here = lax.axis_index("ckpt").astype(jnp.int32)
    block, blocks = lax.axis_index(ROW_BLOCKS), lax.axis_size(ROW_BLOCKS)
    is_first = (block == 0) & (me == 0)
    is_last = (block == blocks - 1) & (me == sz.group - 1)
    place = jnp.stack([me, here, is_first.astype(jnp.int32), is_last.astype(jnp.int32)])
    spread = halves_of(complex_lanes(span_matrix(1)))
    chunks = CHUNKS

    other = lax.dynamic_slice_in_dim(forward, (1 - here) * sz.block_rows, sz.block_rows, 2)
    moved = lax.ppermute(other, "ckpt", [(i, stations - 1 - i) for i in range(stations)])

    free = jnp.asarray(np.arange(4, dtype=np.int32)) if INWARD[0] else place
    pieces, (ends,) = adjoint_prep(sz, INWARD[0], free, adjoint, spread, chunks[0], spread)
    inward = [pieces.exchange()]

    low, high, past = edge_rows(sz, adjoint, forward, ends)
    low = shifted(low, ROW_BLOCKS, 1, blocks)
    high = shifted(high, ROW_BLOCKS, -1, blocks)
    past = shifted(past, ROW_BLOCKS, -stations, blocks)

    freq_index = lax.div(mode_map, jnp.int32(NK))
    span_index = lax.rem(mode_map, jnp.int32(NK))
    alpha = 2.0 / NF * ((freq_index + NF // 2) % NF - NF // 2).astype(F32)
    beta = 2.0 / NK * ((span_index + NK // 2) % NK - NK // 2).astype(F32)
    freq = freq_index.reshape(sz.blocks, NK)[:, :1].astype(F32)
    freq = jnp.pad(jnp.broadcast_to(freq, (sz.blocks, LANES)), ((0, 8 - sz.blocks), (0, 0)))

    stored, done = forward_prep(
        sz, STORED, place, forward, moved, (low, high, past), ends, freq, spread, chunks[0]
    )
    pieces, _ = adjoint_prep(
        sz, INWARD[1], place, adjoint, spread, chunks[1], done, (low, high)
    )
    stored = stored.exchange(inward[0].arrays if STORED else ())
    got = stored.in_order()
    inward.append(pieces.exchange(got if INWARD[1] else (got + got[-1:] * WINDOW)[WINDOW:]))

    phys, next_phys, rims, table = forward_physical(sz, place, stored, len(chunks[0]), spread)
    turn = halves_of(complex_lanes(beta_matrix()))
    out, (pair, pair_rims, total) = march(
        sz, OUTWARD[0], table, inward[0], phys, next_phys, len(chunks[0]), (rims, turn, spread)
    )
    start, whole = nearer_sum_by_pairs(total, "mode")
    got = inward[1].in_order()
    if OUTWARD[0]:
        back = [out.exchange([whole, *got])]
    else:
        back = [out.exchange([whole] * len(out.arrays))]
    start = start + nearer_sum(whole)
    back_span = halves_of(complex_lanes(span_matrix(-1) / NK))
    running = (pair, pair_rims, start, turn, back_span)
    out, _ = march(
        sz,
        OUTWARD[1],
        table,
        inward[1],
        phys,
        next_phys,
        len(chunks[1]),
        row_scale=row_scale,
        running=running,
    )
    got = back[0].in_order()
    back.append(out.exchange(got if OUTWARD[1] else (got + got[-1:] * WINDOW)[WINDOW:]))

    tri = jnp.asarray(np.tril(np.ones((sz.block_rows, sz.block_rows))), jnp.bfloat16)
    out, sums, total = post(
        sz, row_scale, place, back[0], chunks[0], None, "make", (alpha[None], beta[None], tri)
    )
    start = nearer_sum(total)
    (out,) = post(sz, row_scale, place, back[1], chunks[1], out, "add", (sums, start))
    return out


def solution(mesh):
    placed = (P(None, None, ROW_BLOCKS, "mode"), P("ckpt", None, "wall", "mode"), P("mode"))
    return jax.shard_map(
        on_device,
        mesh=mesh,
        in_specs=placed,
        out_specs=P(None, None, ROW_BLOCKS, "mode"),
        check_vma=False,
    )
```
